128 devices in a mesh: cube: 2 (over core), row: 4 (over x), col: 16 (over z, y).
Axes of the slice: x: 4, y: 4, z: 4, core: 2. Of those that a mesh axis runs over, the one named last changes fastest.
Arguments:
- front_init: float32 [2, 6144, 6144], P('cube', 'row', 'col'), may hold values from -4 to 30, as said below
- contribution: bfloat16 [2, 2048, 2048], P('cube', 'row', 'col'), may hold values from -1 to 2, as said below
- maps: int32 [2, 16], P('cube'), may hold values from 0 to 47, as said below
Outputs:
- factored: float32 [2, 6144, 6144], P('cube', 'row', 'col')
The draws below stay inside these ranges and needn't reach their ends.
Inputs may be any that keep to these rules, and one draw needn't show every extreme that they name: Each row of maps increases strictly, starts at 0, ends at 47, and its fourth entry lies between 33 and 35. front_init is symmetric; front_init plus any extend-added contribution block is positive definite. contribution is symmetric.
All inputs are finite; a program needn't handle non-finite values.
Results may differ from the reference program's by a relative error of at most 0.0014.
Values may be sent and summed in bfloat16 or wider, within the bound.
No kernel may reach another device: no remote copies, remote signals or barrier semaphores. Data moves between devices by JAX's collectives and lax.ppermute only.
A program may use at most 128 MiB of HBM per device.

```python
import math
import jax
import jax.numpy as jnp
from jax import lax

BLK = 128
M = 2048
PANEL = 384
PANELS = 4
F = 6144
MB = 16
N_CUBE = 2


def symmetric_from(entries, diagonal, offdiag_scale):
    order = entries.shape[1]
    paired = (entries + jnp.swapaxes(entries, 1, 2)) * (0.70710678 * offdiag_scale)
    unit_mask = jnp.arange(order)[:, None] == jnp.arange(order)[None, :]
    return jnp.where(unit_mask[None, :, :], diagonal[:, :, None], paired)


def involution_blocks(key, count, order, strength):
    perm_key, sign_key = jax.random.split(key)
    perm_keys = jax.random.split(perm_key, count)
    perms = jax.vmap(lambda one_key: jax.random.permutation(one_key, order))(perm_keys).astype(jnp.int32)
    signs = (2 * jax.random.randint(sign_key, (count, order), 0, 2) - 1).astype(jnp.float32)
    odd = 2 * perms + 1
    phase = odd[:, :, None] * odd[:, None, :] % (8 * order)
    angle = phase.astype(jnp.float32) * (math.pi / (4.0 * order))
    table = jnp.cos(angle) * (math.sqrt(2.0 / order) * strength)
    return table * signs[:, :, None] * signs[:, None, :]


def draw_front_init(key, part):
    key = jax.random.fold_in(key, 1)
    first = jax.random.fold_in(key, 0)
    second = jax.random.fold_in(key, 1)
    third = jax.random.fold_in(key, 2)
    fifth = jax.random.fold_in(key, 4)
    entries = jax.random.normal(first, (N_CUBE, F, F), jnp.float32)
    diagonal = jax.random.uniform(second, (N_CUBE, F), jnp.float32, 4.5, 6.5)
    profile = jax.random.uniform(third, (N_CUBE, F), jnp.float32, 0.5, 1.5)
    matrix = symmetric_from(entries, diagonal, 0.8 / math.sqrt(F))
    matrix = matrix + 2.0 / math.sqrt(F) * profile[:, :, None] * profile[:, None, :]
    block_count = F // PANEL
    blocks = involution_blocks(fifth, N_CUBE * block_count, PANEL, 2.0).reshape(N_CUBE, block_count, PANEL, PANEL)
    selector = jnp.eye(block_count, dtype=jnp.float32)
    placed = blocks[:, :, :, None, :] * selector[None, :, None, :, None]
    matrix = matrix + placed.reshape(N_CUBE, F, F)
    return matrix


def draw_contribution(key, part):
    key = jax.random.fold_in(key, 2)
    first, second, third = jax.random.split(key, 3)
    entries = jax.random.normal(first, (N_CUBE, M, M), jnp.float32)
    diagonal = jax.random.uniform(second, (N_CUBE, M), jnp.float32, 0.5, 1.5)
    profile = jax.random.uniform(third, (N_CUBE, M), jnp.float32, 0.5, 1.5)
    matrix = symmetric_from(entries, diagonal, 0.2 / math.sqrt(M))
    matrix = matrix + 2.0 / math.sqrt(M) * profile[:, :, None] * profile[:, None, :]
    return matrix.astype(jnp.bfloat16)


def draw_maps(key, part):
    key = jax.random.fold_in(key, 3)
    keys = jax.random.split(key, N_CUBE)

    def one_front(front_key):
        pivot_key, lower_key, upper_key = jax.random.split(front_key, 3)
        pivot = (2 * MB + 1 + jax.random.randint(pivot_key, (1,), 0, 3)).astype(jnp.int32)
        lower = jnp.sort(jax.random.permutation(lower_key, 2 * MB)[:2].astype(jnp.int32) + 1)
        room = 3 * MB - 2 - pivot
        slots = jnp.arange(MB - 3, dtype=jnp.int32)
        scores = jax.random.permutation(upper_key, MB - 3).astype(jnp.int32) + jnp.where(slots >= room, MB, 0).astype(jnp.int32)
        chosen = jnp.sort(jnp.argsort(scores)[:MB - 5].astype(jnp.int32))
        upper = (chosen + pivot + 1).astype(jnp.int32)
        first_block = jnp.zeros((1,), jnp.int32)
        last_block = jnp.full((1,), 3 * MB - 1, jnp.int32)
        return jnp.concatenate([first_block, lower, pivot, upper, last_block]).astype(jnp.int32)
    return jax.vmap(one_front)(keys).astype(jnp.int32)


def setup_inputs(seed: int = 0) -> dict:
    seeds = jax.random.split(jax.random.key(seed), 4)
    front_init = draw_front_init(jax.random.fold_in(seeds[3], 71), 0)
    contribution = draw_contribution(jax.random.fold_in(seeds[3], 71), 0)
    maps = draw_maps(jax.random.fold_in(seeds[3], 71), 0)
    return dict(front_init=front_init, contribution=contribution, maps=maps)


def assemble(frontal, child, index_map):
    blocks = (index_map[:, None] * BLK + jnp.arange(BLK, dtype=jnp.int32)[None, :]).reshape(-1).astype(jnp.int32)
    return frontal.at[blocks[:, None], blocks[None, :]].add(child.astype(jnp.float32))

def factor_front(frontal):
    for panel_index in range(PANELS):
        first_col = panel_index * PANEL
        end_col = first_col + PANEL
        factor = jnp.linalg.cholesky(frontal[first_col:end_col, first_col:end_col])
        lower_part = lax.linalg.triangular_solve(factor, frontal[end_col:, first_col:end_col], left_side=False, lower=True, transpose_a=True)
        rounded = lower_part.astype(jnp.bfloat16).astype(jnp.float32)
        update = jnp.dot(rounded, rounded.T, precision=lax.Precision.HIGHEST)
        frontal = frontal.at[end_col:, end_col:].add(-update)
        column = jnp.concatenate([jnp.zeros((first_col, PANEL), frontal.dtype), factor, lower_part], axis=0)
        frontal = frontal.at[:, first_col:end_col].set(column)
    return frontal

def reference(front_init, contribution, maps):
    outputs = []
    for cube_id in range(N_CUBE):
        partner = cube_id ^ 1
        frontal = assemble(front_init[cube_id], contribution[partner], maps[cube_id])
        outputs.append(factor_front(frontal))
    return jnp.stack(outputs)
```

```python
import functools

import jax
import jax.numpy as jnp
from jax import lax
from jax.experimental import pallas as pl
from jax.experimental.pallas import tpu as pltpu
from jax.sharding import PartitionSpec as P

BLK = 128
PANEL = 384
PANELS = 4
N_ROW = 4
N_COL = 16
PIECE = PANEL // N_ROW
LEAD = PANEL * PANELS
F32 = jnp.float32
BF16 = jnp.bfloat16

SOURCES = {11: [3, 4, 5], 12: [4, 5, 6, 7, 8], 13: [7, 8, 9, 10, 11], 14: [10, 11, 12, 13, 14], 15: [13, 14, 15]}
THICK = 5


def dot(a, b, ca, cb):
    return lax.dot_general(a, b, (((ca,), (cb,)), ((), ())), preferred_element_type=F32)


def split(x):
    high = x.astype(BF16)
    return high, (x - high.astype(F32)).astype(BF16)


def dot3(a, b, ca, cb):
    ah, al = split(a)
    bh, bl = split(b)
    return dot(jnp.concatenate([ah, ah, al], ca), jnp.concatenate([bh, bl, bh], cb), ca, cb)


def over_rows(x, i):
    return jnp.broadcast_to(x[i : i + 1, :], x.shape)


def over_lanes(x, j):
    return jnp.broadcast_to(x[:, j : j + 1], x.shape)


def factor_block(tiles, group=4):
    sub = lax.broadcasted_iota(jnp.int32, (8, BLK), 0)
    lane = lax.broadcasted_iota(jnp.int32, (8, BLK), 1)
    v = list(tiles)
    inv, upper, scale = [None] * 16, [None] * 16, [None] * 16
    for g in range(0, 16, group):
        for t in range(g, g + group):
            qs = range(t, g + group)
            c = {(q, j): over_lanes(v[q], 8 * t + j) for q in qs for j in range(8)}
            block = (lane >= 8 * t) & (lane < 8 * t + 8)
            sc = jnp.zeros((8, BLK), F32)
            w = {q: jnp.where(block, 0.0, v[q]) for q in qs}
            w[t] = jnp.where(lane - 8 * t == sub, 1.0, w[t])
            u = v[t]
            for i in range(8):
                pivot = over_rows(c[t, i], i)
                r = 1.0 / pivot
                sc = jnp.where(sub == i, lax.rsqrt(pivot), sc)
                m = {q: c[q, i] * r for q in qs}
                m[t] = jnp.where(sub > i, m[t], 0.0)
                for j in range(i + 1, 8):
                    row = over_rows(c[t, j], i)
                    for q in qs:
                        c[q, j] = c[q, j] - m[q] * row
                row = over_rows(w[t], i)
                for q in qs:
                    if q != t or i < 7:
                        w[q] = w[q] - m[q] * row
                if i < 7:
                    u = u - m[t] * over_rows(u, i)
            inv[t], scale[t], upper[t] = w[t], sc, u
            for q in range(t + 1, g + group):
                v[q] = w[q]
        if g + group < 16:
            sg = jnp.concatenate(scale[g : g + group], 0)
            ug = jnp.concatenate(upper[g : g + group], 0) * sg
            done = [
                jnp.where((lane >= 8 * t + 8) & (lane < 8 * g + 8 * group), 0.0, inv[t]) for t in range(g, g + group)
            ]
            wg = jnp.concatenate(done, 0) * sg
            update = dot3(ug, wg, 0, 0)
            block = (lane >= 8 * g) & (lane < 8 * g + 8 * group)
            for q in range(g + group, 16):
                v[q] = jnp.where(block, 0.0, v[q]) - update[8 * q : 8 * q + 8, :]
    return [a * s for a, s in zip(inv, scale)], [a * s for a, s in zip(upper, scale)]


def factor_panel(p, li, ud):
    sub = lax.broadcasted_iota(jnp.int32, (8, BLK), 0)
    lane = lax.broadcasted_iota(jnp.int32, (8, BLK), 1)

    def step(j, _):
        at = pl.multiple_of(j * BLK, BLK)
        inv, upper = factor_block([p[pl.ds(at + 8 * q, 8), pl.ds(at, BLK)] for q in range(16)])
        for q in range(16):
            li[8 * q : 8 * q + 8, :] = jnp.where(lane <= sub + 8 * q, inv[q], 0.0)
            ud[pl.ds(at + 8 * q, 8), :] = jnp.where(lane >= sub + 8 * q, upper[q], 0.0)
        row = dot3(li[...], p[pl.ds(at, BLK), :], 1, 0)
        p[pl.ds(at, BLK), :] = row
        p[pl.ds(at, BLK), pl.ds(at, BLK)] = li[...]
        for k in range(1, 3):

            @pl.when(k > j)
            def _():
                rows = slice(k * BLK, k * BLK + BLK)
                p[rows, pl.ds(at, BLK)] = jnp.zeros((BLK, BLK), F32)
                p[rows, :] = p[rows, :] - dot3(row[:, rows], p[pl.ds(at, BLK), :], 0, 0)

        return 0

    lax.fori_loop(0, 3, step, 0)


def panel_kernel(k, base, info, maps, *refs):
    r = list(refs)
    pieces, r = r[:4], r[4:]
    t_pieces, r = r[:4], r[4:]
    ups, r = r[:k], r[k:]
    invs, r = r[: 2 * k], r[2 * k :]
    inv_hi, inv_lo, up_out, low_out, mine_out = r[:5]
    a, t, p, li, ud = r[5:]
    me = info[0]
    col = info[1]
    for s in range(4):
        at = pl.multiple_of(lax.rem(me + 4 - s, 4) * PIECE, PIECE)
        buf = pieces[s]
        for j in range(k):
            a[pl.ds(j * PANEL + at, PIECE), :] = buf[base + (2 + j) * PIECE : base + (3 + j) * PIECE, :].astype(F32)
        a[pl.ds(k * PANEL + at, PIECE), :] = buf[base : base + PIECE, :].astype(F32) + buf[
            base + PIECE : base + 2 * PIECE, :
        ].astype(F32)
        for b in range(3):
            for u in range(3):
                t[pl.ds(at + 32 * u, 32), b * BLK : (b + 1) * BLK] = t_pieces[s][
                    2 * PIECE + 32 * b : 2 * PIECE + 32 * b + 32, u * BLK : (u + 1) * BLK
                ].astype(F32)
    for b in range(3):
        mb = maps[b] - 3 * k
        for i in range(3):
            ma = maps[i]

            @pl.when((mb >= 0) & (mb < 3) & (ma < 3 * (k + 1)))
            def _():
                rows = pl.ds(pl.multiple_of(ma * BLK, BLK), BLK)
                cols = pl.ds(pl.multiple_of(mb * BLK, BLK), BLK)
                a[rows, cols] = a[rows, cols] + t[i * BLK : (i + 1) * BLK, b * BLK : (b + 1) * BLK]

    mine_out[...] = jnp.zeros((PANEL, PANEL), F32)
    cur = []
    for j in range(k):
        z = a[j * PANEL : (j + 1) * PANEL, :]
        for i in range(j):
            z = z - dot(ups[j][i * PANEL : (i + 1) * PANEL, :], cur[i], 0, 0)
        zh, zl = split(z)
        ih, il = invs[2 * j][...], invs[2 * j + 1][...]
        uf = dot(ih, zh, 1, 0) + (dot(ih, zl, 1, 0) + dot(il, zh, 1, 0))

        @pl.when(col == j)
        def _():
            mine_out[...] = uf.T

        ub = uf.astype(BF16)
        up_out[j * PANEL : (j + 1) * PANEL, :] = ub
        cur.append(ub)
    if k == 0:
        up_out[...] = jnp.zeros(up_out.shape, BF16)
    z = a[k * PANEL : (k + 1) * PANEL, :]
    for j in range(k):
        z = z - dot(cur[j], cur[j], 0, 0)
    p[...] = z
    factor_panel(p, li, ud)
    for i in range(3):
        ri = slice(i * BLK, (i + 1) * BLK)
        for j in range(3):
            rj = slice(j * BLK, (j + 1) * BLK)
            if j <= i:
                hi, lo = split(p[ri, rj])
                inv_hi[ri, rj] = hi
                inv_lo[ri, rj] = lo
            else:
                inv_hi[ri, rj] = jnp.zeros((BLK, BLK), BF16)
                inv_lo[ri, rj] = jnp.zeros((BLK, BLK), BF16)
                low_out[ri, rj] = jnp.zeros((BLK, BLK), F32)
                low_out[rj, ri] = p[ri, rj].T
        low_out[ri, ri] = ud[ri, :].T


def panel_call(k, base, info, maps, pieces, t_pieces, ups, invs):
    vm = pl.BlockSpec(memory_space=pltpu.VMEM)
    sm = pl.BlockSpec(memory_space=pltpu.SMEM)
    args = list(pieces) + list(t_pieces) + list(ups) + list(invs)
    sq = (PANEL, PANEL)
    return pl.pallas_call(
        functools.partial(panel_kernel, k, base),
        out_shape=[
            jax.ShapeDtypeStruct(sq, BF16),
            jax.ShapeDtypeStruct(sq, BF16),
            jax.ShapeDtypeStruct((max(k, 1) * PANEL if k else 16, PANEL), BF16),
            jax.ShapeDtypeStruct(sq, F32),
            jax.ShapeDtypeStruct(sq, F32),
        ],
        in_specs=[sm, sm] + [vm] * len(args),
        out_specs=[vm] * 5,
        scratch_shapes=[
            pltpu.VMEM(((k + 1) * PANEL, PANEL), F32),
            pltpu.VMEM(sq, F32),
            pltpu.VMEM(sq, F32),
            pltpu.VMEM((BLK, BLK), F32),
            pltpu.VMEM((PANEL, BLK), F32),
        ],
        compiler_params=pltpu.CompilerParams(vmem_limit_bytes=40 * 2**20),
        cost_estimate=pl.CostEstimate(flops=10**10, bytes_accessed=10**6, transcendentals=0),
        name=f"panel{k}",
    )(info, maps, *args)


def tail_kernel(info, maps, front, a12, wide, *refs):
    r = list(refs)
    thick, r = r[:THICK], r[THICK:]
    t_pieces, r = r[:4], r[4:]
    ups, r = r[:3], r[3:]
    invs, r = r[:4], r[4:]
    lows, r = r[:4], r[4:]
    mines, r = r[:3], r[3:]
    out = r[0]
    x, t, y = r[1:]
    me = info[0]
    col = info[1]
    first = info[2]
    sq = (PANEL, PANEL)

    def blk(i):
        return slice(i * BLK, (i + 1) * BLK)

    def pan(i):
        return slice(i * PANEL, (i + 1) * PANEL)

    @pl.when((me == 0) & (col < PANELS))
    def _():
        for j in range(PANELS):

            @pl.when(col > j)
            def _():
                out[pan(j), :] = jnp.zeros(sq, F32)

            @pl.when(col == j)
            def _():
                out[pan(j), :] = lows[j][...]

            if j:

                @pl.when(col < j)
                def _():
                    out[pan(j), :] = mines[j - 1][...]

    def add(ref, row_block, col_slot, value):
        rows = pl.ds(pl.multiple_of(row_block * BLK, BLK), BLK)
        cols = pl.ds(pl.multiple_of(col_slot * BLK, BLK), BLK)
        ref[rows, cols] = ref[rows, cols] + value

    @pl.when(col >= PANELS)
    def _():
        @pl.when(me == 0)
        def _():
            x[...] = front[...]

        @pl.when(me != 0)
        def _():
            x[...] = a12[...].astype(F32)

        for s in range(4):
            at = pl.multiple_of(lax.rem(me + 4 - s, 4) * PIECE, PIECE)
            for b in range(3):
                for u in range(3):
                    t[pl.ds(at + 32 * u, 32), blk(b)] = t_pieces[s][
                        2 * PIECE + 32 * b : 2 * PIECE + 32 * b + 32, blk(u)
                    ].astype(F32)
        for i in range(3):
            ma = maps[i]
            for b in range(3):
                slot = maps[b] - 3 * col

                @pl.when((ma < 12) & (slot >= 0) & (slot < 3))
                def _():
                    add(x, ma, slot, t[blk(i), blk(b)])

            for j in range(THICK):
                slot = info[8 + j] - 3 * col

                @pl.when((ma < 12) & (slot >= 0) & (slot < 3))
                def _():
                    add(x, ma, slot, thick[j][blk(i), :].astype(F32))

        xs = []
        for j in range(PANELS):
            z = x[pan(j), :]
            for i in range(j):
                z = z - dot(ups[j - 1][pan(i), :], xs[i], 0, 0)
            xs.append(dot(invs[j][...], z.astype(BF16), 1, 0).astype(BF16))

            @pl.when(me == 0)
            def _():
                out[pan(j), :] = z

        for j in range(PANELS):
            x[pan(j), :] = xs[j].astype(F32)

    @pl.when(me > 0)
    def _():
        @pl.when(col >= PANELS)
        def _():
            out[...] = front[...]
            for q in range(12):
                ma = maps[first + q] - 12 * me

                @pl.when((ma >= 0) & (ma < 12))
                def _():
                    for b in range(3):
                        slot = maps[b] - 3 * col

                        @pl.when((slot >= 0) & (slot < 3))
                        def _():
                            piece = wide[(q // 3) * 4 + b, blk(q % 3), PANEL : PANEL + BLK]
                            add(out, ma, slot, piece.astype(F32))

                    for j in range(THICK):
                        slot = info[8 + j] - 3 * col

                        @pl.when((slot >= 0) & (slot < 3))
                        def _():
                            rows = pl.ds(pl.multiple_of((first + q) * BLK, BLK), BLK)
                            add(out, ma, slot, thick[j][rows, :].astype(F32))

        for z in range(4):
            for k in range(PANELS):
                y[k, pan(z), :] = wide[z * 4 + k, :, :PANEL].astype(F32)
        for q in range(12):
            ma = maps[first + q] - 12 * me

            @pl.when((ma >= 0) & (ma < 12))
            def _():
                for b in range(3):
                    mb = maps[b]

                    @pl.when(mb < 12)
                    def _():
                        panel = mb // 3
                        piece = wide[(q // 3) * 4 + b, blk(q % 3), PANEL : PANEL + BLK].astype(F32)
                        rows = pl.ds(pl.multiple_of(ma * BLK, BLK), BLK)
                        cols = pl.ds(pl.multiple_of((mb - panel * 3) * BLK, BLK), BLK)
                        y[panel, rows, cols] = y[panel, rows, cols] + piece

        def rows_step(q, _):
            rows = pl.ds(pl.multiple_of(q * PANEL, PANEL), PANEL)
            ys = []
            for k in range(PANELS):
                z = y[k, rows, :]
                for i in range(k):
                    z = z - dot(ys[i], ups[k - 1][pan(i), :], 1, 0)
                full = dot(z.astype(BF16), invs[k][...], 1, 1)
                ys.append(full.astype(BF16))

                @pl.when(col == k)
                def _():
                    out[rows, :] = full

            @pl.when(col >= PANELS)
            def _():
                acc = out[rows, :]
                for k in range(PANELS):
                    acc = acc - dot(ys[k], x[pan(k), :].astype(BF16), 1, 0)
                out[rows, :] = acc

            return 0

        lax.fori_loop(0, 4, rows_step, 0)


def tail_call(info, maps, front, a12, wide, thick, t_pieces, ups, invs, lows, mines):
    vm = pl.BlockSpec(memory_space=pltpu.VMEM)
    sm = pl.BlockSpec(memory_space=pltpu.SMEM)
    args = [front, a12, wide, *thick, *t_pieces, *ups, *invs, *lows, *mines]
    return pl.pallas_call(
        tail_kernel,
        out_shape=jax.ShapeDtypeStruct((LEAD, PANEL), F32),
        in_specs=[sm, sm] + [vm] * len(args),
        out_specs=vm,
        scratch_shapes=[
            pltpu.VMEM((LEAD, PANEL), F32),
            pltpu.VMEM((PANEL, PANEL), F32),
            pltpu.VMEM((PANELS, LEAD, PANEL), F32),
        ],
        compiler_params=pltpu.CompilerParams(vmem_limit_bytes=58 * 2**20),
        cost_estimate=pl.CostEstimate(flops=7 * 10**9, bytes_accessed=2 * 10**7, transcendentals=0),
        name="tail",
    )(info, maps, *args)


def per_device(front_init, contribution, maps):
    front = front_init[0]
    index_map = maps[0]
    me = lax.axis_index("row")
    col = lax.axis_index("col")
    y = lax.rem(col, 4)
    grid = ("row", "col")

    def flat(r, c):
        return r * N_COL + c

    def x_from0(value, s, cols):
        return lax.ppermute(value, grid, [(flat(0, c), flat(s, c)) for c in cols])

    def z_from0(value, s):
        return lax.ppermute(value, "col", [(b, 4 * s + b) for b in range(4)])

    def x_shift(value, s):
        return lax.ppermute(value, "row", [(i, (i + s) % 4) for i in range(4)])

    def y_shift(value, s):
        return lax.ppermute(value, "col", [(4 * z + b, 4 * z + (b + s) % 4) for z in range(4) for b in range(4)])

    received = lax.ppermute(contribution[0], "cube", [(0, 1), (1, 0)])

    high = front.astype(BF16)
    diag = lax.dynamic_slice_in_dim(front, y * PANEL, PANEL, 0)
    diag_high = diag.astype(BF16)
    diag_low = (diag - diag_high.astype(F32)).astype(BF16)

    def quarter(s):
        rows = slice(s * PIECE, (s + 1) * PIECE)
        child = received[rows, :]
        child = jnp.concatenate([child[:32], child[32:64], child[64:96]], axis=1)
        offs = [high[j * PANEL + s * PIECE : j * PANEL + (s + 1) * PIECE] for j in range(3)]
        return jnp.concatenate([diag_high[rows], diag_low[rows], *offs, child], axis=0)

    mine = jnp.where(me == 0, quarter(0), jnp.zeros((), BF16))
    for s in range(1, 4):
        mine = mine + x_from0(quarter(s), s, range(4))
    at_root = mine
    spread = jnp.where(col < 4, at_root, jnp.zeros((), BF16))
    for s in range(1, 4):
        spread = spread + z_from0(at_root, s)
    around = [spread] + [y_shift(spread, s) for s in range(1, 4)]
    stacked = jnp.stack(around)
    order = [lax.rem(y + 4 - k, 4) for k in range(4)]
    by_panel = [lax.dynamic_index_in_dim(stacked, order[k], 0, keepdims=False) for k in range(4)]
    r0 = jnp.concatenate([by_panel[0][: 2 * PIECE]] + [by_panel[b][5 * PIECE :] for b in range(3)], axis=0)
    r1 = by_panel[1][: 3 * PIECE]
    r23 = jnp.concatenate([by_panel[2][: 4 * PIECE], by_panel[3][: 5 * PIECE]], axis=0)
    g0 = [r0] + [x_shift(r0, s) for s in range(1, 4)]
    g1 = [r1] + [x_shift(r1, s) for s in range(1, 4)]
    g23 = [r23] + [x_shift(r23, s) for s in range(1, 4)]

    parts = [received] + [x_shift(received, s) for s in range(1, 4)]
    parts = jnp.stack(parts)
    column = jnp.concatenate(
        [lax.dynamic_index_in_dim(parts, lax.rem(me + 4 - i, 4), 0, keepdims=False) for i in range(4)], axis=0
    )
    first = jnp.where(me == 3, 4, 0)
    chosen = lax.dynamic_slice_in_dim(column, first * BLK, 12 * BLK, 0)
    thick = []
    for j in range(THICK):
        pairs = [(SOURCES[c][j], c) for c in SOURCES if j < len(SOURCES[c])]
        thick.append(lax.ppermute(column, "col", pairs))

    panel_wide = jnp.concatenate([high, chosen], axis=1)
    wide = jnp.where(col < 4, panel_wide[:PANEL], jnp.zeros((), BF16))
    for s in range(1, 4):
        wide = wide + z_from0(panel_wide[s * PANEL : (s + 1) * PANEL], s)
    wide = lax.all_gather(wide, "col")
    a12 = high
    got = jnp.zeros((), BF16)
    for s in range(1, 4):
        got = got + x_from0(high, s, range(4, N_COL))
    a12 = got

    ids = jnp.full((N_COL, THICK), -1, jnp.int32)
    for c in SOURCES:
        for j, b in enumerate(SOURCES[c]):
            ids = ids.at[c, j].set(b)
    held = jnp.take(ids, col, axis=0)
    targets = jnp.where(held >= 0, jnp.take(index_map, jnp.maximum(held, 0)), -1000)
    info = jnp.concatenate(
        [jnp.stack([me, col, first, 0, 0, 0, 0, 0]).astype(jnp.int32), targets.astype(jnp.int32), jnp.zeros((3,), jnp.int32)]
    )

    ups, invs, lows, mines = [], [], [], []
    flat_invs = []
    for k in range(PANELS):
        pieces = [g0, g1, g23, g23][k]
        base = 4 * PIECE if k == 3 else 0
        ih, il, up, low, mine_out = panel_call(k, base, info, index_map, pieces, g0, ups, flat_invs)
        flat_invs += [ih, il]
        ups.append(up)
        invs.append(ih)
        lows.append(low)
        mines.append(mine_out)
    out = tail_call(info, index_map, front, a12, wide, thick, g0, ups[1:], invs, lows, mines[1:])
    return out[None]


def solution(mesh):
    return jax.shard_map(
        per_device,
        mesh=mesh,
        in_specs=(P("cube", "row", "col"), P("cube", "row", "col"), P("cube", None)),
        out_specs=P("cube", "row", "col"),
        check_vma=False,
    )
```

```python
import functools

import jax
import jax.numpy as jnp
from jax import lax
from jax.experimental import pallas as pl
from jax.experimental.pallas import tpu as pltpu
from jax.sharding import PartitionSpec as P

BLK = 128
PANEL = 384
PANELS = 4
N_ROW = 4
N_COL = 16
PIECE = PANEL // N_ROW
PART = BLK // N_ROW
DIAG = 4 * PART
LEAD = PANEL * PANELS
F32 = jnp.float32
BF16 = jnp.bfloat16

SOURCES = {11: [3, 4, 5], 12: [4, 5, 6, 7, 8], 13: [7, 8, 9, 10, 11], 14: [10, 11, 12, 13, 14], 15: [13, 14, 15]}
THICK = 5


def dot(a, b, ca, cb):
    return lax.dot_general(a, b, (((ca,), (cb,)), ((), ())), preferred_element_type=F32)


def split(x):
    high = x.astype(BF16)
    return high, (x - high.astype(F32)).astype(BF16)


def dot3(a, b, ca, cb):
    ah, al = split(a)
    bh, bl = split(b)
    return dot(jnp.concatenate([ah, ah, al], ca), jnp.concatenate([bh, bl, bh], cb), ca, cb)


def over_rows(x, i):
    return jnp.broadcast_to(x[i : i + 1, :], x.shape)


def over_lanes(x, j):
    return jnp.broadcast_to(x[:, j : j + 1], x.shape)


def factor_block(tiles, group=4):
    sub = lax.broadcasted_iota(jnp.int32, (8, BLK), 0)
    lane = lax.broadcasted_iota(jnp.int32, (8, BLK), 1)
    v = list(tiles)
    inv, upper, scale = [None] * 16, [None] * 16, [None] * 16
    for g in range(0, 16, group):
        for t in range(g, g + group):
            qs = range(t, g + group)
            c = {(q, j): over_lanes(v[q], 8 * t + j) for q in qs for j in range(8)}
            block = (lane >= 8 * t) & (lane < 8 * t + 8)
            sc = jnp.zeros((8, BLK), F32)
            w = {q: jnp.where(block, 0.0, v[q]) for q in qs}
            w[t] = jnp.where(lane - 8 * t == sub, 1.0, w[t])
            u = v[t]
            for i in range(8):
                pivot = over_rows(c[t, i], i)
                r = 1.0 / pivot
                sc = jnp.where(sub == i, lax.rsqrt(pivot), sc)
                m = {q: c[q, i] * r for q in qs}
                m[t] = jnp.where(sub > i, m[t], 0.0)
                for j in range(i + 1, 8):
                    row = over_rows(c[t, j], i)
                    for q in qs:
                        c[q, j] = c[q, j] - m[q] * row
                row = over_rows(w[t], i)
                for q in qs:
                    if q != t or i < 7:
                        w[q] = w[q] - m[q] * row
                if i < 7:
                    u = u - m[t] * over_rows(u, i)
            inv[t], scale[t], upper[t] = w[t], sc, u
            for q in range(t + 1, g + group):
                v[q] = w[q]
        if g + group < 16:
            sg = jnp.concatenate(scale[g : g + group], 0)
            ug = jnp.concatenate(upper[g : g + group], 0) * sg
            done = [
                jnp.where((lane >= 8 * t + 8) & (lane < 8 * g + 8 * group), 0.0, inv[t]) for t in range(g, g + group)
            ]
            wg = jnp.concatenate(done, 0) * sg
            update = dot3(ug, wg, 0, 0)
            block = (lane >= 8 * g) & (lane < 8 * g + 8 * group)
            for q in range(g + group, 16):
                v[q] = jnp.where(block, 0.0, v[q]) - update[8 * q : 8 * q + 8, :]
    return [a * s for a, s in zip(inv, scale)], [a * s for a, s in zip(upper, scale)]


def factor_panel(p, li, ud):
    sub = lax.broadcasted_iota(jnp.int32, (8, BLK), 0)
    lane = lax.broadcasted_iota(jnp.int32, (8, BLK), 1)

    def step(j, _):
        at = pl.multiple_of(j * BLK, BLK)
        inv, upper = factor_block([p[pl.ds(at + 8 * q, 8), pl.ds(at, BLK)] for q in range(16)])
        for q in range(16):
            li[8 * q : 8 * q + 8, :] = jnp.where(lane <= sub + 8 * q, inv[q], 0.0)
            ud[pl.ds(at + 8 * q, 8), :] = jnp.where(lane >= sub + 8 * q, upper[q], 0.0)
        row = dot3(li[...], p[pl.ds(at, BLK), :], 1, 0)
        p[pl.ds(at, BLK), :] = row
        p[pl.ds(at, BLK), pl.ds(at, BLK)] = li[...]
        for k in range(1, 3):

            @pl.when(k > j)
            def _():
                rows = slice(k * BLK, k * BLK + BLK)
                p[rows, pl.ds(at, BLK)] = jnp.zeros((BLK, BLK), F32)
                p[rows, :] = p[rows, :] - dot3(row[:, rows], p[pl.ds(at, BLK), :], 0, 0)

        return 0

    lax.fori_loop(0, 3, step, 0)


def unpack_child(t, piece, x):
    at = pl.multiple_of(x * PIECE, 16)
    for b in range(3):
        for u in range(3):
            t[pl.ds(at + PART * u, PART), b * BLK : (b + 1) * BLK] = piece[
                DIAG + PART * b : DIAG + PART * (b + 1), u * BLK : (u + 1) * BLK
            ].astype(F32)


def panel_kernel(k, base, info, maps, *refs):
    r = list(refs)
    pieces, r = r[:4], r[4:]
    t_pieces, r = r[:4], r[4:]
    ups, r = r[:k], r[k:]
    invs, r = r[: 2 * k], r[2 * k :]
    inv_hi, inv_lo, up_out, low_out, mine_out = r[:5]
    a, t, p, li, ud = r[5:]
    me = info[0]
    col = info[1]
    for s in range(4):
        x = lax.rem(me + 4 - s, 4)
        buf = pieces[s]
        for j in range(k):
            at = pl.multiple_of(j * PANEL + x * PIECE, 16)
            a[pl.ds(at, PIECE), :] = buf[base + DIAG + j * PIECE : base + DIAG + (j + 1) * PIECE, :].astype(F32)
        at = pl.multiple_of(x * PART, PART)
        first = buf[base : base + PART, :].astype(F32) + buf[base + 2 * PART : base + 3 * PART, :].astype(F32)
        rest = buf[base + PART : base + 2 * PART, :].astype(F32) + buf[base + 3 * PART : base + 4 * PART, :].astype(F32)
        a[pl.ds(k * PANEL + at, PART), :] = first
        a[pl.ds(k * PANEL + BLK + at, PART), BLK:] = rest[:, : 2 * BLK]
        a[pl.ds(k * PANEL + 2 * BLK + at, PART), 2 * BLK :] = rest[:, 2 * BLK :]
        unpack_child(t, t_pieces[s], x)
    for b in range(3):
        mb = maps[b] - 3 * k
        for i in range(3):
            ma = maps[i]

            @pl.when((mb >= 0) & (mb < 3) & (ma < 3 * (k + 1)))
            def _():
                rows = pl.ds(pl.multiple_of(ma * BLK, BLK), BLK)
                cols = pl.ds(pl.multiple_of(mb * BLK, BLK), BLK)
                a[rows, cols] = a[rows, cols] + t[i * BLK : (i + 1) * BLK, b * BLK : (b + 1) * BLK]

    mine_out[...] = jnp.zeros((PANEL, PANEL), F32)
    cur = []
    for j in range(k):
        z = a[j * PANEL : (j + 1) * PANEL, :]
        for i in range(j):
            z = z - dot(ups[j][i * PANEL : (i + 1) * PANEL, :], cur[i], 0, 0)
        zh, zl = split(z)
        ih, il = invs[2 * j][...], invs[2 * j + 1][...]
        uf = dot(ih, zh, 1, 0) + (dot(ih, zl, 1, 0) + dot(il, zh, 1, 0))

        @pl.when(col == j)
        def _():
            mine_out[...] = uf.T

        ub = uf.astype(BF16)
        up_out[j * PANEL : (j + 1) * PANEL, :] = ub
        cur.append(ub)
    if k == 0:
        up_out[...] = jnp.zeros(up_out.shape, BF16)
    z = a[k * PANEL : (k + 1) * PANEL, :]
    for j in range(k):
        z = z - dot(cur[j], cur[j], 0, 0)
    p[...] = z
    factor_panel(p, li, ud)
    for i in range(3):
        ri = slice(i * BLK, (i + 1) * BLK)
        for j in range(3):
            rj = slice(j * BLK, (j + 1) * BLK)
            if j <= i:
                hi, lo = split(p[ri, rj])
                inv_hi[ri, rj] = hi
                inv_lo[ri, rj] = lo
            else:
                inv_hi[ri, rj] = jnp.zeros((BLK, BLK), BF16)
                inv_lo[ri, rj] = jnp.zeros((BLK, BLK), BF16)
                low_out[ri, rj] = jnp.zeros((BLK, BLK), F32)
                low_out[rj, ri] = p[ri, rj].T
        low_out[ri, ri] = ud[ri, :].T


def panel_call(k, base, info, maps, pieces, t_pieces, ups, invs):
    vm = pl.BlockSpec(memory_space=pltpu.VMEM)
    sm = pl.BlockSpec(memory_space=pltpu.SMEM)
    args = list(pieces) + list(t_pieces) + list(ups) + list(invs)
    sq = (PANEL, PANEL)
    return pl.pallas_call(
        functools.partial(panel_kernel, k, base),
        out_shape=[
            jax.ShapeDtypeStruct(sq, BF16),
            jax.ShapeDtypeStruct(sq, BF16),
            jax.ShapeDtypeStruct((max(k, 1) * PANEL if k else 16, PANEL), BF16),
            jax.ShapeDtypeStruct(sq, F32),
            jax.ShapeDtypeStruct(sq, F32),
        ],
        in_specs=[sm, sm] + [vm] * len(args),
        out_specs=[vm] * 5,
        scratch_shapes=[
            pltpu.VMEM(((k + 1) * PANEL, PANEL), F32),
            pltpu.VMEM(sq, F32),
            pltpu.VMEM(sq, F32),
            pltpu.VMEM((BLK, BLK), F32),
            pltpu.VMEM((PANEL, BLK), F32),
        ],
        compiler_params=pltpu.CompilerParams(vmem_limit_bytes=40 * 2**20),
        cost_estimate=pl.CostEstimate(flops=10**10, bytes_accessed=10**6, transcendentals=0),
        name=f"panel{k}",
    )(info, maps, *args)


def tail_kernel(info, maps, front, a12, wide, *refs):
    r = list(refs)
    thick, r = r[:THICK], r[THICK:]
    t_pieces, r = r[:4], r[4:]
    ups, r = r[:3], r[3:]
    invs, r = r[:4], r[4:]
    lows, r = r[:4], r[4:]
    mines, r = r[:3], r[3:]
    out = r[0]
    x, t, y = r[1:]
    me = info[0]
    col = info[1]
    first = info[2]
    sq = (PANEL, PANEL)

    def blk(i):
        return slice(i * BLK, (i + 1) * BLK)

    def pan(i):
        return slice(i * PANEL, (i + 1) * PANEL)

    @pl.when((me == 0) & (col < PANELS))
    def _():
        for j in range(PANELS):

            @pl.when(col > j)
            def _():
                out[pan(j), :] = jnp.zeros(sq, F32)

            @pl.when(col == j)
            def _():
                out[pan(j), :] = lows[j][...]

            if j:

                @pl.when(col < j)
                def _():
                    out[pan(j), :] = mines[j - 1][...]

    def add(ref, row_block, col_slot, value):
        rows = pl.ds(pl.multiple_of(row_block * BLK, BLK), BLK)
        cols = pl.ds(pl.multiple_of(col_slot * BLK, BLK), BLK)
        ref[rows, cols] = ref[rows, cols] + value

    @pl.when(col >= PANELS)
    def _():
        @pl.when(me == 0)
        def _():
            x[...] = front[...]

        @pl.when(me != 0)
        def _():
            x[...] = a12[...].astype(F32)

        for s in range(4):
            unpack_child(t, t_pieces[s], lax.rem(me + 4 - s, 4))
        for i in range(3):
            ma = maps[i]
            for b in range(3):
                slot = maps[b] - 3 * col

                @pl.when((ma < 12) & (slot >= 0) & (slot < 3))
                def _():
                    add(x, ma, slot, t[blk(i), blk(b)])

            for j in range(THICK):
                slot = info[8 + j] - 3 * col

                @pl.when((ma < 12) & (slot >= 0) & (slot < 3))
                def _():
                    add(x, ma, slot, thick[j][blk(i), :].astype(F32))

        xs = []
        for j in range(PANELS):
            z = x[pan(j), :]
            for i in range(j):
                z = z - dot(ups[j - 1][pan(i), :], xs[i], 0, 0)
            xs.append(dot(invs[j][...], z.astype(BF16), 1, 0).astype(BF16))

            @pl.when(me == 0)
            def _():
                out[pan(j), :] = z

        for j in range(PANELS):
            x[pan(j), :] = xs[j].astype(F32)

    @pl.when(me > 0)
    def _():
        @pl.when(col >= PANELS)
        def _():
            out[...] = front[...]
            for q in range(12):
                ma = maps[first + q] - 12 * me

                @pl.when((ma >= 0) & (ma < 12))
                def _():
                    for b in range(3):
                        slot = maps[b] - 3 * col

                        @pl.when((slot >= 0) & (slot < 3))
                        def _():
                            piece = wide[(q // 3) * 4 + b, blk(q % 3), PANEL : PANEL + BLK]
                            add(out, ma, slot, piece.astype(F32))

                    for j in range(THICK):
                        slot = info[8 + j] - 3 * col

                        @pl.when((slot >= 0) & (slot < 3))
                        def _():
                            rows = pl.ds(pl.multiple_of((first + q) * BLK, BLK), BLK)
                            add(out, ma, slot, thick[j][rows, :].astype(F32))

        for z in range(4):
            for k in range(PANELS):
                y[k, pan(z), :] = wide[z * 4 + k, :, :PANEL].astype(F32)
        for q in range(12):
            ma = maps[first + q] - 12 * me

            @pl.when((ma >= 0) & (ma < 12))
            def _():
                for b in range(3):
                    mb = maps[b]

                    @pl.when(mb < 12)
                    def _():
                        panel = mb // 3
                        piece = wide[(q // 3) * 4 + b, blk(q % 3), PANEL : PANEL + BLK].astype(F32)
                        rows = pl.ds(pl.multiple_of(ma * BLK, BLK), BLK)
                        cols = pl.ds(pl.multiple_of((mb - panel * 3) * BLK, BLK), BLK)
                        y[panel, rows, cols] = y[panel, rows, cols] + piece

        def rows_step(q, _):
            rows = pl.ds(pl.multiple_of(q * PANEL, PANEL), PANEL)
            ys = []
            for k in range(PANELS):
                z = y[k, rows, :]
                for i in range(k):
                    z = z - dot(ys[i], ups[k - 1][pan(i), :], 1, 0)
                full = dot(z.astype(BF16), invs[k][...], 1, 1)
                ys.append(full.astype(BF16))

                @pl.when(col == k)
                def _():
                    out[rows, :] = full

            @pl.when(col >= PANELS)
            def _():
                acc = out[rows, :]
                for k in range(PANELS):
                    acc = acc - dot(ys[k], x[pan(k), :].astype(BF16), 1, 0)
                out[rows, :] = acc

            return 0

        lax.fori_loop(0, 4, rows_step, 0)


def tail_call(info, maps, front, a12, wide, thick, t_pieces, ups, invs, lows, mines):
    vm = pl.BlockSpec(memory_space=pltpu.VMEM)
    sm = pl.BlockSpec(memory_space=pltpu.SMEM)
    args = [front, a12, wide, *thick, *t_pieces, *ups, *invs, *lows, *mines]
    return pl.pallas_call(
        tail_kernel,
        out_shape=jax.ShapeDtypeStruct((LEAD, PANEL), F32),
        in_specs=[sm, sm] + [vm] * len(args),
        out_specs=vm,
        scratch_shapes=[
            pltpu.VMEM((LEAD, PANEL), F32),
            pltpu.VMEM((PANEL, PANEL), F32),
            pltpu.VMEM((PANELS, LEAD, PANEL), F32),
        ],
        compiler_params=pltpu.CompilerParams(vmem_limit_bytes=58 * 2**20),
        cost_estimate=pl.CostEstimate(flops=7 * 10**9, bytes_accessed=2 * 10**7, transcendentals=0),
        name="tail",
    )(info, maps, *args)


def per_device(front_init, contribution, maps):
    front = front_init[0]
    index_map = maps[0]
    me = lax.axis_index("row")
    col = lax.axis_index("col")
    y = lax.rem(col, 4)
    grid = ("row", "col")

    def flat(r, c):
        return r * N_COL + c

    def x_from0(value, s, cols):
        return lax.ppermute(value, grid, [(flat(0, c), flat(s, c)) for c in cols])

    def z_from0(value, s):
        return lax.ppermute(value, "col", [(b, 4 * s + b) for b in range(4)])

    def x_shift(value, s):
        return lax.ppermute(value, "row", [(i, (i + s) % 4) for i in range(4)])

    def y_shift(value, s):
        return lax.ppermute(value, "col", [(4 * z + b, 4 * z + (b + s) % 4) for z in range(4) for b in range(4)])

    def after(value, *marks):
        return lax.optimization_barrier((value, *marks))[0]

    def own_or(root, value, *got):
        out = jnp.where(root, value, jnp.zeros((), BF16))
        for g in got:
            out = out + g
        return out

    def by_source(value, shift, index, order):
        around = jnp.stack([value] + [shift(value, s) for s in range(1, 4)])
        return [lax.dynamic_index_in_dim(around, lax.rem(index + 4 - k, 4), 0, keepdims=False) for k in order]

    received = lax.ppermute(contribution[0], "cube", [(0, 1), (1, 0)])
    high = front.astype(BF16)
    diag = lax.dynamic_slice_in_dim(front, y * PANEL, PANEL, 0)

    def diag_part(s):
        a = diag[s * PART : (s + 1) * PART]
        b = diag[BLK + s * PART : BLK + (s + 1) * PART, BLK:]
        c = diag[2 * BLK + s * PART : 2 * BLK + (s + 1) * PART, 2 * BLK :]
        rows = jnp.concatenate([a, jnp.concatenate([b, c], axis=1)], axis=0)
        upper = rows.astype(BF16)
        return [upper, (rows - upper.astype(F32)).astype(BF16)]

    def child_part(s):
        child = received[s * PIECE : (s + 1) * PIECE]
        return jnp.concatenate([child[:PART], child[PART : 2 * PART], child[2 * PART :]], axis=1)

    def rest_part(s):
        offs = [high[j * PANEL + s * PIECE : j * PANEL + (s + 1) * PIECE] for j in range(3)]
        return jnp.concatenate(diag_part(s) + offs, axis=0)

    def head_part(s):
        return jnp.concatenate(diag_part(s) + [child_part(s)], axis=0)

    rest = rest_part(0)
    rest_got = [x_from0(rest_part(s), s, range(1, 4)) for s in range(1, 4)]
    head = own_or(me == 0, head_part(0), *[x_from0(head_part(s), s, range(3)) for s in range(1, 4)])
    head_z = own_or(col < 4, head, *[z_from0(head, s) for s in range(1, 4)])
    head_y = by_source(head_z, y_shift, y, range(3))
    g0 = jnp.concatenate([head_y[0]] + [h[DIAG:] for h in head_y[1:]], axis=0)
    g0 = [g0] + [x_shift(g0, s) for s in range(1, 4)]
    rest = own_or(me == 0, rest, *after(rest_got, head_z))
    rest = own_or(col < 4, rest, *[z_from0(rest, s) for s in range(1, 4)])
    rest = after(rest, head_y[0])
    rest_y = by_source(rest, y_shift, y, range(1, 4))
    g1 = rest_y[0][: DIAG + PIECE]
    g1 = [g1] + [x_shift(g1, s) for s in range(1, 4)]
    g23 = jnp.concatenate([rest_y[1][: DIAG + 2 * PIECE], rest_y[2]], axis=0)
    g23 = [g23] + [x_shift(g23, s) for s in range(1, 4)]

    column = jnp.concatenate(by_source(after(received, head_z), x_shift, me, range(4)), axis=0)
    first = jnp.where(me == 3, 4, 0)
    chosen = lax.dynamic_slice_in_dim(column, first * BLK, 12 * BLK, 0)
    panel_wide = jnp.concatenate([high, chosen], axis=1)
    wide = own_or(
        col < 4, panel_wide[:PANEL], *[z_from0(panel_wide[s * PANEL : (s + 1) * PANEL], s) for s in range(1, 4)]
    )
    wide = lax.all_gather(wide, "col")
    a12 = after(high, g0[0], g0[1])
    got = [x_from0(a12, s, range(4, N_COL)) for s in range(1, 4)]
    a12 = got[0] + got[1] + got[2]

    ids = jnp.full((N_COL, THICK), -1, jnp.int32)
    for c in SOURCES:
        for j, b in enumerate(SOURCES[c]):
            ids = ids.at[c, j].set(b)
    held = jnp.take(ids, col, axis=0)
    targets = jnp.where(held >= 0, jnp.take(index_map, jnp.maximum(held, 0)), -1000)
    info = jnp.concatenate(
        [jnp.stack([me, col, first, 0, 0, 0, 0, 0]).astype(jnp.int32), targets.astype(jnp.int32), jnp.zeros((3,), jnp.int32)]
    )

    ups, invs, lows, mines = [], [], [], []
    flat_invs = []
    thick = None
    for k in range(PANELS):
        pieces = [g0, g1, g23, g23][k]
        base = DIAG + 2 * PIECE if k == 3 else 0
        ih, il, up, low, mine_out = panel_call(k, base, info, index_map, pieces, g0, ups, flat_invs)
        flat_invs += [ih, il]
        ups.append(up)
        invs.append(ih)
        lows.append(low)
        mines.append(mine_out)
        if k == 0:
            late = after(column, ih)
            thick = []
            for j in range(THICK):
                pairs = [(SOURCES[c][j], c) for c in SOURCES if j < len(SOURCES[c])]
                thick.append(lax.ppermute(late, "col", pairs))
    out = tail_call(info, index_map, front, a12, wide, thick, g0, ups[1:], invs, lows, mines[1:])
    return out[None]


def solution(mesh):
    return jax.shard_map(
        per_device,
        mesh=mesh,
        in_specs=(P("cube", "row", "col"), P("cube", "row", "col"), P("cube", None)),
        out_specs=P("cube", "row", "col"),
        check_vma=False,
    )
```

```python
import functools

import jax
import jax.numpy as jnp
from jax import lax
from jax.experimental import pallas as pl
from jax.experimental.pallas import tpu as pltpu
from jax.sharding import PartitionSpec as P

BLK = 128
PANEL = 384
PANELS = 4
N_ROW = 4
N_COL = 16
PIECE = PANEL // N_ROW
PART = BLK // N_ROW
DIAG = 4 * PART
LEAD = PANEL * PANELS
F32 = jnp.float32
BF16 = jnp.bfloat16

SOURCES = {11: [3, 4, 5], 12: [4, 5, 6, 7, 8], 13: [7, 8, 9, 10, 11], 14: [10, 11, 12, 13, 14], 15: [13, 14, 15]}
THICK = 5


def dot(a, b, ca, cb):
    return lax.dot_general(a, b, (((ca,), (cb,)), ((), ())), preferred_element_type=F32)


def split(x):
    high = x.astype(BF16)
    return high, (x - high.astype(F32)).astype(BF16)


def dot3(a, b, ca, cb):
    ah, al = split(a)
    bh, bl = split(b)
    return dot(jnp.concatenate([ah, ah, al], ca), jnp.concatenate([bh, bl, bh], cb), ca, cb)


def over_rows(x, i):
    return jnp.broadcast_to(x[i : i + 1, :], x.shape)


def over_lanes(x, j):
    return jnp.broadcast_to(x[:, j : j + 1], x.shape)


def factor_block(tiles, group=4):
    sub = lax.broadcasted_iota(jnp.int32, (8, BLK), 0)
    lane = lax.broadcasted_iota(jnp.int32, (8, BLK), 1)
    v = list(tiles)
    inv, upper, scale = [None] * 16, [None] * 16, [None] * 16
    for g in range(0, 16, group):
        for t in range(g, g + group):
            qs = range(t, g + group)
            c = {(q, j): over_lanes(v[q], 8 * t + j) for q in qs for j in range(8)}
            block = (lane >= 8 * t) & (lane < 8 * t + 8)
            sc = jnp.zeros((8, BLK), F32)
            w = {q: jnp.where(block, 0.0, v[q]) for q in qs}
            w[t] = jnp.where(lane - 8 * t == sub, 1.0, w[t])
            u = v[t]
            for i in range(8):
                pivot = over_rows(c[t, i], i)
                r = 1.0 / pivot
                sc = jnp.where(sub == i, lax.rsqrt(pivot), sc)
                m = {q: c[q, i] * r for q in qs}
                m[t] = jnp.where(sub > i, m[t], 0.0)
                for j in range(i + 1, 8):
                    row = over_rows(c[t, j], i)
                    for q in qs:
                        c[q, j] = c[q, j] - m[q] * row
                row = over_rows(w[t], i)
                for q in qs:
                    if q != t or i < 7:
                        w[q] = w[q] - m[q] * row
                if i < 7:
                    u = u - m[t] * over_rows(u, i)
            inv[t], scale[t], upper[t] = w[t], sc, u
            for q in range(t + 1, g + group):
                v[q] = w[q]
        if g + group < 16:
            sg = jnp.concatenate(scale[g : g + group], 0)
            ug = jnp.concatenate(upper[g : g + group], 0) * sg
            done = [
                jnp.where((lane >= 8 * t + 8) & (lane < 8 * g + 8 * group), 0.0, inv[t]) for t in range(g, g + group)
            ]
            wg = jnp.concatenate(done, 0) * sg
            update = dot3(ug, wg, 0, 0)
            block = (lane >= 8 * g) & (lane < 8 * g + 8 * group)
            for q in range(g + group, 16):
                v[q] = jnp.where(block, 0.0, v[q]) - update[8 * q : 8 * q + 8, :]
    return [a * s for a, s in zip(inv, scale)], [a * s for a, s in zip(upper, scale)]


def factor_panel(p, li, ud):
    sub = lax.broadcasted_iota(jnp.int32, (8, BLK), 0)
    lane = lax.broadcasted_iota(jnp.int32, (8, BLK), 1)

    def step(j, _):
        at = pl.multiple_of(j * BLK, BLK)
        inv, upper = factor_block([p[pl.ds(at + 8 * q, 8), pl.ds(at, BLK)] for q in range(16)])
        for q in range(16):
            li[8 * q : 8 * q + 8, :] = jnp.where(lane <= sub + 8 * q, inv[q], 0.0)
            ud[pl.ds(at + 8 * q, 8), :] = jnp.where(lane >= sub + 8 * q, upper[q], 0.0)
        row = dot3(li[...], p[pl.ds(at, BLK), :], 1, 0)
        p[pl.ds(at, BLK), :] = row
        p[pl.ds(at, BLK), pl.ds(at, BLK)] = li[...]
        for k in range(1, 3):

            @pl.when(k > j)
            def _():
                rows = slice(k * BLK, k * BLK + BLK)
                p[rows, pl.ds(at, BLK)] = jnp.zeros((BLK, BLK), F32)
                p[rows, :] = p[rows, :] - dot3(row[:, rows], p[pl.ds(at, BLK), :], 0, 0)

        return 0

    lax.fori_loop(0, 3, step, 0)


def unpack_child(t, piece, x):
    at = pl.multiple_of(x * PIECE, 16)
    for b in range(3):
        for u in range(3):
            t[pl.ds(at + PART * u, PART), b * BLK : (b + 1) * BLK] = piece[
                DIAG + PART * b : DIAG + PART * (b + 1), u * BLK : (u + 1) * BLK
            ].astype(F32)


def panel_kernel(k, base, info, maps, *refs):
    r = list(refs)
    pieces, r = r[:4], r[4:]
    t_pieces, r = r[:4], r[4:]
    ups, r = r[:k], r[k:]
    invs, r = r[: 2 * k], r[2 * k :]
    inv_hi, inv_lo, up_out, low_out, mine_out = r[:5]
    a, t, p, li, ud = r[5:]
    me = info[0]
    col = info[1]
    for s in range(4):
        x = lax.rem(me + 4 - s, 4)
        buf = pieces[s]
        for j in range(k):
            at = pl.multiple_of(j * PANEL + x * PIECE, 16)
            a[pl.ds(at, PIECE), :] = buf[base + DIAG + j * PIECE : base + DIAG + (j + 1) * PIECE, :].astype(F32)
        at = pl.multiple_of(x * PART, PART)
        first = buf[base : base + PART, :].astype(F32) + buf[base + 2 * PART : base + 3 * PART, :].astype(F32)
        rest = buf[base + PART : base + 2 * PART, :].astype(F32) + buf[base + 3 * PART : base + 4 * PART, :].astype(F32)
        a[pl.ds(k * PANEL + at, PART), :] = first
        a[pl.ds(k * PANEL + BLK + at, PART), BLK:] = rest[:, : 2 * BLK]
        a[pl.ds(k * PANEL + 2 * BLK + at, PART), 2 * BLK :] = rest[:, 2 * BLK :]
        unpack_child(t, t_pieces[s], x)
    for b in range(3):
        mb = maps[b] - 3 * k
        for i in range(3):
            ma = maps[i]

            @pl.when((mb >= 0) & (mb < 3) & (ma < 3 * (k + 1)))
            def _():
                rows = pl.ds(pl.multiple_of(ma * BLK, BLK), BLK)
                cols = pl.ds(pl.multiple_of(mb * BLK, BLK), BLK)
                a[rows, cols] = a[rows, cols] + t[i * BLK : (i + 1) * BLK, b * BLK : (b + 1) * BLK]

    mine_out[...] = jnp.zeros((PANEL, PANEL), F32)
    cur = []
    for j in range(k):
        z = a[j * PANEL : (j + 1) * PANEL, :]
        for i in range(j):
            z = z - dot(ups[j][i * PANEL : (i + 1) * PANEL, :], cur[i], 0, 0)
        zh, zl = split(z)
        ih, il = invs[2 * j][...], invs[2 * j + 1][...]
        uf = dot(ih, zh, 1, 0) + (dot(ih, zl, 1, 0) + dot(il, zh, 1, 0))

        @pl.when(col == j)
        def _():
            mine_out[...] = uf.T

        ub = uf.astype(BF16)
        up_out[j * PANEL : (j + 1) * PANEL, :] = ub
        cur.append(ub)
    if k == 0:
        up_out[...] = jnp.zeros(up_out.shape, BF16)
    z = a[k * PANEL : (k + 1) * PANEL, :]
    for j in range(k):
        z = z - dot(cur[j], cur[j], 0, 0)
    p[...] = z
    factor_panel(p, li, ud)
    for i in range(3):
        ri = slice(i * BLK, (i + 1) * BLK)
        for j in range(3):
            rj = slice(j * BLK, (j + 1) * BLK)
            if j <= i:
                hi, lo = split(p[ri, rj])
                inv_hi[ri, rj] = hi
                inv_lo[ri, rj] = lo
            else:
                inv_hi[ri, rj] = jnp.zeros((BLK, BLK), BF16)
                inv_lo[ri, rj] = jnp.zeros((BLK, BLK), BF16)
                low_out[ri, rj] = jnp.zeros((BLK, BLK), F32)
                low_out[rj, ri] = p[ri, rj].T
        low_out[ri, ri] = ud[ri, :].T


def panel_call(k, base, info, maps, pieces, t_pieces, ups, invs):
    vm = pl.BlockSpec(memory_space=pltpu.VMEM)
    sm = pl.BlockSpec(memory_space=pltpu.SMEM)
    args = list(pieces) + list(t_pieces) + list(ups) + list(invs)
    sq = (PANEL, PANEL)
    return pl.pallas_call(
        functools.partial(panel_kernel, k, base),
        out_shape=[
            jax.ShapeDtypeStruct(sq, BF16),
            jax.ShapeDtypeStruct(sq, BF16),
            jax.ShapeDtypeStruct((max(k, 1) * PANEL if k else 16, PANEL), BF16),
            jax.ShapeDtypeStruct(sq, F32),
            jax.ShapeDtypeStruct(sq, F32),
        ],
        in_specs=[sm, sm] + [vm] * len(args),
        out_specs=[vm] * 5,
        scratch_shapes=[
            pltpu.VMEM(((k + 1) * PANEL, PANEL), F32),
            pltpu.VMEM(sq, F32),
            pltpu.VMEM(sq, F32),
            pltpu.VMEM((BLK, BLK), F32),
            pltpu.VMEM((PANEL, BLK), F32),
        ],
        compiler_params=pltpu.CompilerParams(vmem_limit_bytes=40 * 2**20),
        cost_estimate=pl.CostEstimate(flops=10**10, bytes_accessed=10**6, transcendentals=0),
        name=f"panel{k}",
    )(info, maps, *args)


def tail_kernel(info, maps, front, a12, wide, *refs):
    r = list(refs)
    thick, r = r[:THICK], r[THICK:]
    t_pieces, r = r[:4], r[4:]
    ups, r = r[:3], r[3:]
    invs, r = r[:4], r[4:]
    lows, r = r[:4], r[4:]
    mines, r = r[:3], r[3:]
    out = r[0]
    x, t, y = r[1:]
    me = info[0]
    col = info[1]
    first = info[2]
    sq = (PANEL, PANEL)

    def blk(i):
        return slice(i * BLK, (i + 1) * BLK)

    def pan(i):
        return slice(i * PANEL, (i + 1) * PANEL)

    @pl.when((me == 0) & (col < PANELS))
    def _():
        for j in range(PANELS):

            @pl.when(col > j)
            def _():
                out[pan(j), :] = jnp.zeros(sq, F32)

            @pl.when(col == j)
            def _():
                out[pan(j), :] = lows[j][...]

            if j:

                @pl.when(col < j)
                def _():
                    out[pan(j), :] = mines[j - 1][...]

    def add(ref, row_block, col_slot, value):
        rows = pl.ds(pl.multiple_of(row_block * BLK, BLK), BLK)
        cols = pl.ds(pl.multiple_of(col_slot * BLK, BLK), BLK)
        ref[rows, cols] = ref[rows, cols] + value

    @pl.when(col >= PANELS)
    def _():
        @pl.when(me == 0)
        def _():
            x[...] = front[...]

        @pl.when(me != 0)
        def _():
            x[...] = a12[...].astype(F32)

        for s in range(4):
            unpack_child(t, t_pieces[s], lax.rem(me + 4 - s, 4))
        for i in range(3):
            ma = maps[i]
            for b in range(3):
                slot = maps[b] - 3 * col

                @pl.when((ma < 12) & (slot >= 0) & (slot < 3))
                def _():
                    add(x, ma, slot, t[blk(i), blk(b)])

            for j in range(THICK):
                slot = info[8 + j] - 3 * col

                @pl.when((ma < 12) & (slot >= 0) & (slot < 3))
                def _():
                    add(x, ma, slot, thick[j][blk(i), :].astype(F32))

        xs = []
        for j in range(PANELS):
            z = x[pan(j), :]
            for i in range(j):
                z = z - dot(ups[j - 1][pan(i), :], xs[i], 0, 0)
            xs.append(dot(invs[j][...], z.astype(BF16), 1, 0).astype(BF16))

            @pl.when(me == 0)
            def _():
                out[pan(j), :] = z

        for j in range(PANELS):
            x[pan(j), :] = xs[j].astype(F32)

    @pl.when(me > 0)
    def _():
        @pl.when(col >= PANELS)
        def _():
            out[...] = front[...]
            for q in range(12):
                ma = maps[first + q] - 12 * me

                @pl.when((ma >= 0) & (ma < 12))
                def _():
                    for b in range(3):
                        slot = maps[b] - 3 * col

                        @pl.when((slot >= 0) & (slot < 3))
                        def _():
                            piece = wide[(q // 3) * 4 + b, blk(q % 3), PANEL : PANEL + BLK]
                            add(out, ma, slot, piece.astype(F32))

                    for j in range(THICK):
                        slot = info[8 + j] - 3 * col

                        @pl.when((slot >= 0) & (slot < 3))
                        def _():
                            rows = pl.ds(pl.multiple_of((first + q) * BLK, BLK), BLK)
                            add(out, ma, slot, thick[j][rows, :].astype(F32))

        for z in range(4):
            for k in range(PANELS):
                y[k, pan(z), :] = wide[z * 4 + k, :, :PANEL].astype(F32)
        for q in range(12):
            ma = maps[first + q] - 12 * me

            @pl.when((ma >= 0) & (ma < 12))
            def _():
                for b in range(3):
                    mb = maps[b]

                    @pl.when(mb < 12)
                    def _():
                        panel = mb // 3
                        piece = wide[(q // 3) * 4 + b, blk(q % 3), PANEL : PANEL + BLK].astype(F32)
                        rows = pl.ds(pl.multiple_of(ma * BLK, BLK), BLK)
                        cols = pl.ds(pl.multiple_of((mb - panel * 3) * BLK, BLK), BLK)
                        y[panel, rows, cols] = y[panel, rows, cols] + piece

        def rows_step(q, _):
            rows = pl.ds(pl.multiple_of(q * PANEL, PANEL), PANEL)
            ys = []
            for k in range(PANELS):
                z = y[k, rows, :]
                for i in range(k):
                    z = z - dot(ys[i], ups[k - 1][pan(i), :], 1, 0)
                full = dot(z.astype(BF16), invs[k][...], 1, 1)
                ys.append(full.astype(BF16))

                @pl.when(col == k)
                def _():
                    out[rows, :] = full

            @pl.when(col >= PANELS)
            def _():
                acc = out[rows, :]
                for k in range(PANELS):
                    acc = acc - dot(ys[k], x[pan(k), :].astype(BF16), 1, 0)
                out[rows, :] = acc

            return 0

        lax.fori_loop(0, 4, rows_step, 0)


def tail_call(info, maps, front, a12, wide, thick, t_pieces, ups, invs, lows, mines):
    vm = pl.BlockSpec(memory_space=pltpu.VMEM)
    sm = pl.BlockSpec(memory_space=pltpu.SMEM)
    args = [front, a12, wide, *thick, *t_pieces, *ups, *invs, *lows, *mines]
    return pl.pallas_call(
        tail_kernel,
        out_shape=jax.ShapeDtypeStruct((LEAD, PANEL), F32),
        in_specs=[sm, sm] + [vm] * len(args),
        out_specs=vm,
        scratch_shapes=[
            pltpu.VMEM((LEAD, PANEL), F32),
            pltpu.VMEM((PANEL, PANEL), F32),
            pltpu.VMEM((PANELS, LEAD, PANEL), F32),
        ],
        compiler_params=pltpu.CompilerParams(vmem_limit_bytes=58 * 2**20),
        cost_estimate=pl.CostEstimate(flops=7 * 10**9, bytes_accessed=2 * 10**7, transcendentals=0),
        name="tail",
    )(info, maps, *args)


def per_device(front_init, contribution, maps):
    front = front_init[0]
    index_map = maps[0]
    me = lax.axis_index("row")
    col = lax.axis_index("col")
    y = lax.rem(col, 4)
    grid = ("row", "col")

    def flat(r, c):
        return r * N_COL + c

    def x_from0(value, s, cols):
        return lax.ppermute(value, grid, [(flat(0, c), flat(s, c)) for c in cols])

    def z_from0(value, s):
        return lax.ppermute(value, "col", [(b, 4 * s + b) for b in range(4)])

    def x_shift(value, s):
        return lax.ppermute(value, "row", [(i, (i + s) % 4) for i in range(4)])

    def y_shift(value, s):
        return lax.ppermute(value, "col", [(4 * z + b, 4 * z + (b + s) % 4) for z in range(4) for b in range(4)])

    def after(value, *marks):
        return lax.optimization_barrier((value, *marks))[0]

    def own_or(root, value, *got):
        out = jnp.where(root, value, jnp.zeros((), BF16))
        for g in got:
            out = out + g
        return out

    def by_source(value, shift, index, order):
        around = jnp.stack([value] + [shift(value, s) for s in range(1, 4)])
        return [lax.dynamic_index_in_dim(around, lax.rem(index + 4 - k, 4), 0, keepdims=False) for k in order]

    received = lax.ppermute(contribution[0], "cube", [(0, 1), (1, 0)])
    high = front.astype(BF16)
    diag = lax.dynamic_slice_in_dim(front, y * PANEL, PANEL, 0)

    def diag_part(s):
        a = diag[s * PART : (s + 1) * PART]
        b = diag[BLK + s * PART : BLK + (s + 1) * PART, BLK:]
        c = diag[2 * BLK + s * PART : 2 * BLK + (s + 1) * PART, 2 * BLK :]
        rows = jnp.concatenate([a, jnp.concatenate([b, c], axis=1)], axis=0)
        upper = rows.astype(BF16)
        return [upper, (rows - upper.astype(F32)).astype(BF16)]

    def child_part(s):
        child = received[s * PIECE : (s + 1) * PIECE]
        return jnp.concatenate([child[:PART], child[PART : 2 * PART], child[2 * PART :]], axis=1)

    def rest_part(s):
        offs = [high[j * PANEL + s * PIECE : j * PANEL + (s + 1) * PIECE] for j in range(3)]
        return jnp.concatenate(diag_part(s) + offs, axis=0)

    def head_part(s):
        off = high[s * PIECE : (s + 1) * PIECE]
        return jnp.concatenate(diag_part(s) + [child_part(s), off], axis=0)

    def x_swap(value, m):
        return lax.ppermute(value, "row", [(i, i ^ m) for i in range(4)])

    def x_pairs(value, pairs, cols):
        return lax.ppermute(value, grid, [(flat(p, c), flat(q, c)) for p, q in pairs for c in cols])

    def z_pairs(value, pairs):
        return lax.ppermute(value, "col", [(4 * p + b, 4 * q + b) for p, q in pairs for b in range(4)])

    def halves(value):
        n = value.shape[0] // 2
        return value[:n], value[n:]

    late_cols = (2, 3)
    rest_two = x_pairs(jnp.concatenate([rest_part(2), rest_part(3)], axis=0), [(0, 3)], late_cols)
    a12 = lax.psum(jnp.where(me == 0, high, jnp.zeros((), BF16)), "row")
    head = own_or(me == 0, head_part(0), *[x_from0(head_part(s), s, range(3)) for s in range(1, 4)])
    child_one = x_swap(received, 1)
    rest_two, rest_one, child_one = after((rest_two, rest_part(1), child_one), head)
    for_two, for_three = halves(rest_two)
    got = x_pairs(jnp.where(me == 0, rest_one, for_two), [(0, 1), (3, 2)], late_cols)
    rest = jnp.where(me == 0, rest_part(0), jnp.where(me == 3, for_three, got))
    pair = jnp.where(me % 2 == 0, jnp.stack([received, child_one]), jnp.stack([child_one, received]))
    pair = pair.reshape(-1, BLK)
    child_two = x_swap(pair, 3)

    head_z = own_or(col < 4, head, *[z_from0(head, s) for s in range(1, 4)])
    column = jnp.where(me < 2, jnp.concatenate([pair, child_two], axis=0), jnp.concatenate([child_two, pair], axis=0))
    rest, column = after((rest, column), head_z)
    first = jnp.where(me == 3, 4, 0)
    chosen = lax.dynamic_slice_in_dim(column, first * BLK, 12 * BLK, 0)
    panel_wide = jnp.concatenate([high, chosen], axis=1)
    rest_z1 = z_pairs(rest, [(0, 1)])
    wide_two = z_pairs(panel_wide[2 * PANEL :], [(0, 3)])

    head_y = by_source(head_z, y_shift, y, range(3))
    child = slice(DIAG, DIAG + PART)
    g0 = jnp.concatenate([head_y[0][: DIAG + PART], head_y[1][child], head_y[2][child]], axis=0)
    g1 = jnp.concatenate([head_y[1][:DIAG], head_y[1][DIAG + PART :]], axis=0)
    g01 = jnp.concatenate([g0, g1], axis=0)
    rest_z1, wide_two = after((rest_z1, wide_two), head_y[0])
    z = col // 4
    rest = jnp.where(z == 0, rest, rest_z1)
    rest_z2 = z_pairs(rest, [(0, 3), (1, 2)])
    for_two, for_three = halves(wide_two)
    wide_got = z_pairs(jnp.where(z == 0, panel_wide[PANEL : 2 * PANEL], for_two), [(0, 1), (3, 2)])
    wide = jnp.where(z == 0, panel_wide[:PANEL], jnp.where(z == 3, for_three, wide_got))

    g01 = [g01] + [x_shift(g01, s) for s in range(1, 4)]
    rest = jnp.where(z < 2, rest, rest_z2)
    rest = after(rest, *g01)
    rest_y = by_source(rest, y_shift, y, (2, 3))
    wide = lax.all_gather(wide, "col")

    ids = jnp.full((N_COL, THICK), -1, jnp.int32)
    for c in SOURCES:
        for j, b in enumerate(SOURCES[c]):
            ids = ids.at[c, j].set(b)
    held = jnp.take(ids, col, axis=0)
    targets = jnp.where(held >= 0, jnp.take(index_map, jnp.maximum(held, 0)), -1000)
    info = jnp.concatenate(
        [jnp.stack([me, col, first, 0, 0, 0, 0, 0]).astype(jnp.int32), targets.astype(jnp.int32), jnp.zeros((3,), jnp.int32)]
    )

    ups, invs, lows, mines = [], [], [], []
    flat_invs = []
    def contribution_column(value, j):
        pairs = [(SOURCES[c][j], c) for c in SOURCES if j < len(SOURCES[c])]
        return lax.ppermute(value, "col", pairs)

    head_rows = g01
    thick = []
    for k in range(PANELS):
        if k < 2:
            pieces = head_rows
        else:
            piece = after(rest_y[k - 2][: DIAG + k * PIECE], invs[k - 2])
            pieces = [piece] + [x_shift(piece, s) for s in range(1, 4)]
        if k >= 2:
            late = after(column, invs[k - 1])
            thick += [contribution_column(late, j) for j in ((0, 1) if k == 2 else (2, 3, 4))]
        base = DIAG + 3 * PART if k == 1 else 0
        ih, il, up, low, mine_out = panel_call(k, base, info, index_map, pieces, head_rows, ups, flat_invs)
        flat_invs += [ih, il]
        ups.append(up)
        invs.append(ih)
        lows.append(low)
        mines.append(mine_out)
    out = tail_call(info, index_map, front, a12, wide, thick, head_rows, ups[1:], invs, lows, mines[1:])
    return out[None]


def solution(mesh):
    return jax.shard_map(
        per_device,
        mesh=mesh,
        in_specs=(P("cube", "row", "col"), P("cube", "row", "col"), P("cube", None)),
        out_specs=P("cube", "row", "col"),
        check_vma=False,
    )
```

```python
import functools

import jax
import jax.numpy as jnp
from jax import lax
from jax.experimental import pallas as pl
from jax.experimental.pallas import tpu as pltpu
from jax.sharding import Mesh
from jax.sharding import PartitionSpec as P

BLK = 128
PANEL = 384
PANELS = 4
N_ROW = 4
N_COL = 16
PIECE = PANEL // N_ROW
PART = BLK // N_ROW
DIAG = 4 * PART
LEAD = PANEL * PANELS
COL = ("z", "y")
F32 = jnp.float32
BF16 = jnp.bfloat16

SOURCES = {11: [3, 4, 5], 12: [4, 5, 6, 7, 8], 13: [7, 8, 9, 10, 11], 14: [10, 11, 12, 13, 14], 15: [13, 14, 15]}
THICK = 5


def dot(a, b, ca, cb):
    return lax.dot_general(a, b, (((ca,), (cb,)), ((), ())), preferred_element_type=F32)


def split(x):
    high = x.astype(BF16)
    return high, (x - high.astype(F32)).astype(BF16)


def dot3(a, b, ca, cb):
    ah, al = split(a)
    bh, bl = split(b)
    return dot(jnp.concatenate([ah, ah, al], ca), jnp.concatenate([bh, bl, bh], cb), ca, cb)


def over_rows(x, i):
    return jnp.broadcast_to(x[i : i + 1, :], x.shape)


def over_lanes(x, j):
    return jnp.broadcast_to(x[:, j : j + 1], x.shape)


def factor_block(tiles, group=4):
    sub = lax.broadcasted_iota(jnp.int32, (8, BLK), 0)
    lane = lax.broadcasted_iota(jnp.int32, (8, BLK), 1)
    v = list(tiles)
    inv, upper, scale = [None] * 16, [None] * 16, [None] * 16
    for g in range(0, 16, group):
        for t in range(g, g + group):
            qs = range(t, g + group)
            c = {(q, j): over_lanes(v[q], 8 * t + j) for q in qs for j in range(8)}
            block = (lane >= 8 * t) & (lane < 8 * t + 8)
            sc = jnp.zeros((8, BLK), F32)
            w = {q: jnp.where(block, 0.0, v[q]) for q in qs}
            w[t] = jnp.where(lane - 8 * t == sub, 1.0, w[t])
            u = v[t]
            for i in range(8):
                pivot = over_rows(c[t, i], i)
                r = 1.0 / pivot
                sc = jnp.where(sub == i, lax.rsqrt(pivot), sc)
                m = {q: c[q, i] * r for q in qs}
                m[t] = jnp.where(sub > i, m[t], 0.0)
                for j in range(i + 1, 8):
                    row = over_rows(c[t, j], i)
                    for q in qs:
                        c[q, j] = c[q, j] - m[q] * row
                row = over_rows(w[t], i)
                for q in qs:
                    if q != t or i < 7:
                        w[q] = w[q] - m[q] * row
                if i < 7:
                    u = u - m[t] * over_rows(u, i)
            inv[t], scale[t], upper[t] = w[t], sc, u
            for q in range(t + 1, g + group):
                v[q] = w[q]
        if g + group < 16:
            sg = jnp.concatenate(scale[g : g + group], 0)
            ug = jnp.concatenate(upper[g : g + group], 0) * sg
            done = [
                jnp.where((lane >= 8 * t + 8) & (lane < 8 * g + 8 * group), 0.0, inv[t]) for t in range(g, g + group)
            ]
            wg = jnp.concatenate(done, 0) * sg
            update = dot3(ug, wg, 0, 0)
            block = (lane >= 8 * g) & (lane < 8 * g + 8 * group)
            for q in range(g + group, 16):
                v[q] = jnp.where(block, 0.0, v[q]) - update[8 * q : 8 * q + 8, :]
    return [a * s for a, s in zip(inv, scale)], [a * s for a, s in zip(upper, scale)]


def factor_panel(p, li, ud):
    sub = lax.broadcasted_iota(jnp.int32, (8, BLK), 0)
    lane = lax.broadcasted_iota(jnp.int32, (8, BLK), 1)

    def step(j, _):
        at = pl.multiple_of(j * BLK, BLK)
        inv, upper = factor_block([p[pl.ds(at + 8 * q, 8), pl.ds(at, BLK)] for q in range(16)])
        for q in range(16):
            li[8 * q : 8 * q + 8, :] = jnp.where(lane <= sub + 8 * q, inv[q], 0.0)
            ud[pl.ds(at + 8 * q, 8), :] = jnp.where(lane >= sub + 8 * q, upper[q], 0.0)
        row = dot3(li[...], p[pl.ds(at, BLK), :], 1, 0)
        p[pl.ds(at, BLK), :] = row
        p[pl.ds(at, BLK), pl.ds(at, BLK)] = li[...]
        for k in range(1, 3):

            @pl.when(k > j)
            def _():
                rows = slice(k * BLK, k * BLK + BLK)
                p[rows, pl.ds(at, BLK)] = jnp.zeros((BLK, BLK), F32)
                p[rows, :] = p[rows, :] - dot3(row[:, rows], p[pl.ds(at, BLK), :], 0, 0)

        return 0

    lax.fori_loop(0, 3, step, 0)


def unpack_child(t, piece, x):
    at = pl.multiple_of(x * PIECE, 16)
    for b in range(3):
        for u in range(3):
            t[pl.ds(at + PART * u, PART), b * BLK : (b + 1) * BLK] = piece[
                DIAG + PART * b : DIAG + PART * (b + 1), u * BLK : (u + 1) * BLK
            ].astype(F32)


def panel_kernel(k, base, info, maps, *refs):
    r = list(refs)
    pieces, r = r[:4], r[4:]
    t_pieces, r = r[:4], r[4:]
    ups, r = r[:k], r[k:]
    invs, r = r[: 2 * k], r[2 * k :]
    inv_hi, inv_lo, up_out, low_out, mine_out = r[:5]
    a, t, p, li, ud = r[5:]
    me = info[0]
    col = info[1]
    for s in range(4):
        x = lax.rem(me + 4 - s, 4)
        buf = pieces[s]
        for j in range(k):
            at = pl.multiple_of(j * PANEL + x * PIECE, 16)
            a[pl.ds(at, PIECE), :] = buf[base + DIAG + j * PIECE : base + DIAG + (j + 1) * PIECE, :].astype(F32)
        at = pl.multiple_of(x * PART, PART)
        first = buf[base : base + PART, :].astype(F32) + buf[base + 2 * PART : base + 3 * PART, :].astype(F32)
        rest = buf[base + PART : base + 2 * PART, :].astype(F32) + buf[base + 3 * PART : base + 4 * PART, :].astype(F32)
        a[pl.ds(k * PANEL + at, PART), :] = first
        a[pl.ds(k * PANEL + BLK + at, PART), BLK:] = rest[:, : 2 * BLK]
        a[pl.ds(k * PANEL + 2 * BLK + at, PART), 2 * BLK :] = rest[:, 2 * BLK :]
        unpack_child(t, t_pieces[s], x)
    for b in range(3):
        mb = maps[b] - 3 * k
        for i in range(3):
            ma = maps[i]

            @pl.when((mb >= 0) & (mb < 3) & (ma < 3 * (k + 1)))
            def _():
                rows = pl.ds(pl.multiple_of(ma * BLK, BLK), BLK)
                cols = pl.ds(pl.multiple_of(mb * BLK, BLK), BLK)
                a[rows, cols] = a[rows, cols] + t[i * BLK : (i + 1) * BLK, b * BLK : (b + 1) * BLK]

    mine_out[...] = jnp.zeros((PANEL, PANEL), F32)
    cur = []
    for j in range(k):
        z = a[j * PANEL : (j + 1) * PANEL, :]
        for i in range(j):
            z = z - dot(ups[j][i * PANEL : (i + 1) * PANEL, :], cur[i], 0, 0)
        zh, zl = split(z)
        ih, il = invs[2 * j][...], invs[2 * j + 1][...]
        uf = dot(ih, zh, 1, 0) + (dot(ih, zl, 1, 0) + dot(il, zh, 1, 0))

        @pl.when(col == j)
        def _():
            mine_out[...] = uf.T

        ub = uf.astype(BF16)
        up_out[j * PANEL : (j + 1) * PANEL, :] = ub
        cur.append(ub)
    if k == 0:
        up_out[...] = jnp.zeros(up_out.shape, BF16)
    z = a[k * PANEL : (k + 1) * PANEL, :]
    for j in range(k):
        z = z - dot(cur[j], cur[j], 0, 0)
    p[...] = z
    factor_panel(p, li, ud)
    for i in range(3):
        ri = slice(i * BLK, (i + 1) * BLK)
        for j in range(3):
            rj = slice(j * BLK, (j + 1) * BLK)
            if j <= i:
                hi, lo = split(p[ri, rj])
                inv_hi[ri, rj] = hi
                inv_lo[ri, rj] = lo
            else:
                inv_hi[ri, rj] = jnp.zeros((BLK, BLK), BF16)
                inv_lo[ri, rj] = jnp.zeros((BLK, BLK), BF16)
                low_out[ri, rj] = jnp.zeros((BLK, BLK), F32)
                low_out[rj, ri] = p[ri, rj].T
        low_out[ri, ri] = ud[ri, :].T


def panel_call(k, base, info, maps, pieces, t_pieces, ups, invs):
    vm = pl.BlockSpec(memory_space=pltpu.VMEM)
    sm = pl.BlockSpec(memory_space=pltpu.SMEM)
    args = list(pieces) + list(t_pieces) + list(ups) + list(invs)
    sq = (PANEL, PANEL)
    return pl.pallas_call(
        functools.partial(panel_kernel, k, base),
        out_shape=[
            jax.ShapeDtypeStruct(sq, BF16),
            jax.ShapeDtypeStruct(sq, BF16),
            jax.ShapeDtypeStruct((max(k, 1) * PANEL if k else 16, PANEL), BF16),
            jax.ShapeDtypeStruct(sq, F32),
            jax.ShapeDtypeStruct(sq, F32),
        ],
        in_specs=[sm, sm] + [vm] * len(args),
        out_specs=[vm] * 5,
        scratch_shapes=[
            pltpu.VMEM(((k + 1) * PANEL, PANEL), F32),
            pltpu.VMEM(sq, F32),
            pltpu.VMEM(sq, F32),
            pltpu.VMEM((BLK, BLK), F32),
            pltpu.VMEM((PANEL, BLK), F32),
        ],
        compiler_params=pltpu.CompilerParams(vmem_limit_bytes=40 * 2**20),
        cost_estimate=pl.CostEstimate(flops=10**10, bytes_accessed=10**6, transcendentals=0),
        name=f"panel{k}",
    )(info, maps, *args)


def pack_kernel(info, front, high, lead, *outs):
    heads, rests = outs[:4], outs[4:]
    at = pl.multiple_of(info[3] * PANEL, PANEL)
    full = front[...].astype(BF16)
    high[...] = full
    lead[...] = jnp.where(info[0] == 0, full, jnp.zeros((), BF16))
    for s in range(4):
        a = front[pl.ds(at + s * PART, PART), :]
        b = front[pl.ds(at + BLK + s * PART, PART), BLK:]
        c = front[pl.ds(at + 2 * BLK + s * PART, PART), 2 * BLK :]
        ah, al = split(a)
        bh, bl = split(b)
        ch, cl = split(c)
        for out in (heads[s], rests[s]):
            out[0:PART, :] = ah
            out[PART : 2 * PART, : 2 * BLK] = bh
            out[PART : 2 * PART, 2 * BLK :] = ch
            out[2 * PART : 3 * PART, :] = al
            out[3 * PART : 4 * PART, : 2 * BLK] = bl
            out[3 * PART : 4 * PART, 2 * BLK :] = cl
        for j in range(3):
            rests[s][DIAG + j * PIECE : DIAG + (j + 1) * PIECE, :] = full[j * PANEL + s * PIECE : j * PANEL + (s + 1) * PIECE]
        heads[s][DIAG : DIAG + PART, :] = jnp.zeros((PART, PANEL), BF16)
        heads[s][DIAG + PART :, :] = full[s * PIECE : (s + 1) * PIECE]


def child_kernel(child, *refs):
    for s in range(4):
        refs[4 + s][...] = refs[s][...]
        for u in range(3):
            rows = s * PIECE + u * PART
            refs[4 + s][DIAG : DIAG + PART, u * BLK : (u + 1) * BLK] = child[rows : rows + PART, :]


def pack_call(info, front):
    vm = pl.BlockSpec(memory_space=pltpu.VMEM)
    sm = pl.BlockSpec(memory_space=pltpu.SMEM)
    full = jax.ShapeDtypeStruct((LEAD, PANEL), BF16)
    head = jax.ShapeDtypeStruct((DIAG + PART + PIECE, PANEL), BF16)
    rest = jax.ShapeDtypeStruct((DIAG + 3 * PIECE, PANEL), BF16)
    out = pl.pallas_call(
        pack_kernel,
        out_shape=[full, full] + [head] * 4 + [rest] * 4,
        in_specs=[sm, vm],
        out_specs=[vm] * 10,
        compiler_params=pltpu.CompilerParams(vmem_limit_bytes=24 * 2**20),
        name="pack",
    )(info, front)
    return out[0], out[1], out[2:6], out[6:]


def child_call(child, heads):
    vm = pl.BlockSpec(memory_space=pltpu.VMEM)
    return pl.pallas_call(
        child_kernel,
        out_shape=[jax.ShapeDtypeStruct(h.shape, h.dtype) for h in heads],
        in_specs=[vm] * 5,
        out_specs=[vm] * 4,
        name="child",
    )(child, *heads)


def tail_kernel(info, maps, front, a12, wide, *refs):
    r = list(refs)
    thick, r = r[:THICK], r[THICK:]
    t_pieces, r = r[:4], r[4:]
    ups, r = r[:3], r[3:]
    invs, r = r[:4], r[4:]
    lows, r = r[:4], r[4:]
    mines, r = r[:3], r[3:]
    out = r[0]
    x, t, y = r[1:]
    me = info[0]
    col = info[1]
    first = info[2]
    sq = (PANEL, PANEL)

    def blk(i):
        return slice(i * BLK, (i + 1) * BLK)

    def pan(i):
        return slice(i * PANEL, (i + 1) * PANEL)

    @pl.when((me == 0) & (col < PANELS))
    def _():
        for j in range(PANELS):

            @pl.when(col > j)
            def _():
                out[pan(j), :] = jnp.zeros(sq, F32)

            @pl.when(col == j)
            def _():
                out[pan(j), :] = lows[j][...]

            if j:

                @pl.when(col < j)
                def _():
                    out[pan(j), :] = mines[j - 1][...]

    def add(ref, row_block, col_slot, value):
        rows = pl.ds(pl.multiple_of(row_block * BLK, BLK), BLK)
        cols = pl.ds(pl.multiple_of(col_slot * BLK, BLK), BLK)
        ref[rows, cols] = ref[rows, cols] + value

    @pl.when(col >= PANELS)
    def _():
        @pl.when(me == 0)
        def _():
            x[...] = front[...]

        @pl.when(me != 0)
        def _():
            x[...] = a12[...].astype(F32)

        for s in range(4):
            unpack_child(t, t_pieces[s], lax.rem(me + 4 - s, 4))
        for i in range(3):
            ma = maps[i]
            for b in range(3):
                slot = maps[b] - 3 * col

                @pl.when((ma < 12) & (slot >= 0) & (slot < 3))
                def _():
                    add(x, ma, slot, t[blk(i), blk(b)])

            for j in range(THICK):
                slot = info[8 + j] - 3 * col

                @pl.when((ma < 12) & (slot >= 0) & (slot < 3))
                def _():
                    add(x, ma, slot, thick[j][blk(i), :].astype(F32))

        xs = []
        for j in range(PANELS):
            z = x[pan(j), :]
            for i in range(j):
                z = z - dot(ups[j - 1][pan(i), :], xs[i], 0, 0)
            xs.append(dot(invs[j][...], z.astype(BF16), 1, 0).astype(BF16))

            @pl.when(me == 0)
            def _():
                out[pan(j), :] = z

        for j in range(PANELS):
            x[pan(j), :] = xs[j].astype(F32)

    @pl.when(me > 0)
    def _():
        @pl.when(col >= PANELS)
        def _():
            out[...] = front[...]
            for q in range(12):
                ma = maps[first + q] - 12 * me

                @pl.when((ma >= 0) & (ma < 12))
                def _():
                    for b in range(3):
                        slot = maps[b] - 3 * col

                        @pl.when((slot >= 0) & (slot < 3))
                        def _():
                            piece = wide[(q // 3) * 4 + b, blk(q % 3), PANEL : PANEL + BLK]
                            add(out, ma, slot, piece.astype(F32))

                    for j in range(THICK):
                        slot = info[8 + j] - 3 * col

                        @pl.when((slot >= 0) & (slot < 3))
                        def _():
                            rows = pl.ds(pl.multiple_of((first + q) * BLK, BLK), BLK)
                            add(out, ma, slot, thick[j][rows, :].astype(F32))

        for z in range(4):
            for k in range(PANELS):
                y[k, pan(z), :] = wide[z * 4 + k, :, :PANEL].astype(F32)
        for q in range(12):
            ma = maps[first + q] - 12 * me

            @pl.when((ma >= 0) & (ma < 12))
            def _():
                for b in range(3):
                    mb = maps[b]

                    @pl.when(mb < 12)
                    def _():
                        panel = mb // 3
                        piece = wide[(q // 3) * 4 + b, blk(q % 3), PANEL : PANEL + BLK].astype(F32)
                        rows = pl.ds(pl.multiple_of(ma * BLK, BLK), BLK)
                        cols = pl.ds(pl.multiple_of((mb - panel * 3) * BLK, BLK), BLK)
                        y[panel, rows, cols] = y[panel, rows, cols] + piece

        def rows_step(q, _):
            rows = pl.ds(pl.multiple_of(q * PANEL, PANEL), PANEL)
            ys = []
            for k in range(PANELS):
                z = y[k, rows, :]
                for i in range(k):
                    z = z - dot(ys[i], ups[k - 1][pan(i), :], 1, 0)
                full = dot(z.astype(BF16), invs[k][...], 1, 1)
                ys.append(full.astype(BF16))

                @pl.when(col == k)
                def _():
                    out[rows, :] = full

            @pl.when(col >= PANELS)
            def _():
                acc = out[rows, :]
                for k in range(PANELS):
                    acc = acc - dot(ys[k], x[pan(k), :].astype(BF16), 1, 0)
                out[rows, :] = acc

            return 0

        lax.fori_loop(0, 4, rows_step, 0)


def tail_call(info, maps, front, a12, wide, thick, t_pieces, ups, invs, lows, mines):
    vm = pl.BlockSpec(memory_space=pltpu.VMEM)
    sm = pl.BlockSpec(memory_space=pltpu.SMEM)
    args = [front, a12, wide, *thick, *t_pieces, *ups, *invs, *lows, *mines]
    return pl.pallas_call(
        tail_kernel,
        out_shape=jax.ShapeDtypeStruct((LEAD, PANEL), F32),
        in_specs=[sm, sm] + [vm] * len(args),
        out_specs=vm,
        scratch_shapes=[
            pltpu.VMEM((LEAD, PANEL), F32),
            pltpu.VMEM((PANEL, PANEL), F32),
            pltpu.VMEM((PANELS, LEAD, PANEL), F32),
        ],
        compiler_params=pltpu.CompilerParams(vmem_limit_bytes=58 * 2**20),
        cost_estimate=pl.CostEstimate(flops=7 * 10**9, bytes_accessed=2 * 10**7, transcendentals=0),
        name="tail",
    )(info, maps, *args)


def per_device(front_init, contribution, maps):
    front = front_init[0]
    index_map = maps[0]
    me = lax.axis_index("row")
    col = lax.axis_index(COL)
    y = lax.axis_index("y")
    grid = ("row", "z", "y")

    def flat(r, c):
        return r * N_COL + c

    def x_from0(value, s, cols):
        return lax.ppermute(value, grid, [(flat(0, c), flat(s, c)) for c in cols])

    def z_from0(value, s):
        return lax.ppermute(value, COL, [(b, 4 * s + b) for b in range(4)])

    def x_shift(value, s):
        return lax.ppermute(value, "row", [(i, (i + s) % 4) for i in range(4)])

    def y_shift(value, s):
        return lax.ppermute(value, COL, [(4 * z + b, 4 * z + (b + s) % 4) for z in range(4) for b in range(4)])

    def never(mark):
        return mark[0, 0] > 3e38

    def own_or(root, value, *got):
        out = jnp.where(root, value, jnp.zeros((), BF16))
        for g in got:
            out = out + g
        return out

    def by_source(value, shift, index, order):
        around = jnp.stack([value] + [shift(value, s) for s in range(1, 4)])
        return [lax.dynamic_index_in_dim(around, lax.rem(index + 4 - k, 4), 0, keepdims=False) for k in order]

    received = lax.ppermute(contribution[0], "cube", [(0, 1), (1, 0)])
    first = jnp.where(me == 3, 4, 0)
    high, lead, heads, rests = pack_call(jnp.stack([me, col, first, y]).astype(jnp.int32), front)
    heads = child_call(received, heads)

    def x_swap(value, m):
        return lax.ppermute(value, "row", [(i, i ^ m) for i in range(4)])

    def x_pairs(value, pairs, cols):
        return lax.ppermute(value, grid, [(flat(p, c), flat(q, c)) for p, q in pairs for c in cols])

    def z_pairs(value, pairs):
        return lax.ppermute(value, COL, [(4 * p + b, 4 * q + b) for p, q in pairs for b in range(4)])

    def halves(value):
        n = value.shape[0] // 2
        return value[:n], value[n:]

    late_cols = (2, 3)
    a12 = lax.psum(lead, "row")
    rest_two = x_pairs(jnp.concatenate([rests[2], rests[3]], axis=0), [(0, 3)], late_cols)
    head = own_or(me == 0, heads[0], *[x_from0(heads[s], s, range(3)) for s in range(1, 4)])
    child_one = x_swap(received, 1)
    for_two, for_three = halves(rest_two)
    got = x_pairs(jnp.where((me == 0) | never(head), rests[1], for_two), [(0, 1), (3, 2)], late_cols)
    even = (me % 2 == 0) | never(head)
    pair = jnp.where(even, jnp.stack([received, child_one]), jnp.stack([child_one, received]))
    pair = pair.reshape(-1, BLK)
    child_two = x_swap(pair, 3)

    head_z = own_or(col < 4, head, *[z_from0(head, s) for s in range(1, 4)])
    rest = jnp.where((me == 0) | never(head_z), rests[0], jnp.where(me == 3, for_three, got))
    low_rows = (me < 2) | never(head_z)
    column = jnp.where(low_rows, jnp.concatenate([pair, child_two], axis=0), jnp.concatenate([child_two, pair], axis=0))
    chosen = lax.dynamic_slice_in_dim(column, first * BLK, 12 * BLK, 0)
    panel_wide = jnp.concatenate([high, chosen], axis=1)
    rest_z1 = z_pairs(rest, [(0, 1)])

    head_y = by_source(head_z, y_shift, y, range(3))
    child = slice(DIAG, DIAG + PART)
    g01 = jnp.concatenate(
        [head_y[0][: DIAG + PART], head_y[1][child], head_y[2][child], head_y[1][:DIAG], head_y[1][DIAG + PART :]], axis=0
    )
    z = lax.axis_index("z")
    at_zero = (z == 0) | never(g01)
    rest_z2 = z_pairs(jnp.where(at_zero, rest, rest_z1), [(0, 3), (1, 2)])

    g01 = [g01] + [x_shift(g01, s) for s in range(1, 4)]
    arrived = never(g01[1]) | never(g01[2]) | never(g01[3])
    rest = jnp.where((z == 0) | arrived, rest, jnp.where(z == 1, rest_z1, rest_z2))
    rest_y = by_source(rest, y_shift, y, (2, 3))
    wide = lax.psum_scatter(jnp.where((z == 0) | never(a12), panel_wide, jnp.zeros((), BF16)), "z", tiled=True)
    wide = lax.all_gather(wide, COL)

    ids = jnp.full((N_COL, THICK), -1, jnp.int32)
    for c in SOURCES:
        for j, b in enumerate(SOURCES[c]):
            ids = ids.at[c, j].set(b)
    held = jnp.take(ids, col, axis=0)
    targets = jnp.where(held >= 0, jnp.take(index_map, jnp.maximum(held, 0)), -1000)
    info = jnp.concatenate(
        [jnp.stack([me, col, first, 0, 0, 0, 0, 0]).astype(jnp.int32), targets.astype(jnp.int32), jnp.zeros((3,), jnp.int32)]
    )

    ups, invs, lows, mines = [], [], [], []
    flat_invs = []
    def contribution_column(value, j):
        pairs = [(SOURCES[c][j], c) for c in SOURCES if j < len(SOURCES[c])]
        return lax.ppermute(value, COL, pairs)

    head_rows = g01
    thick = []
    for k in range(PANELS):
        if k < 2:
            pieces = head_rows
        else:
            piece = rest_y[k - 2][: DIAG + k * PIECE]
            piece = jnp.where(never(invs[k - 2]), jnp.zeros((), BF16), piece)
            pieces = [piece] + [x_shift(piece, s) for s in range(1, 4)]
        if k >= 2:
            late = jnp.where(never(invs[k - 1]), jnp.zeros((), BF16), column)
            thick += [contribution_column(late, j) for j in ((0, 1) if k == 2 else (2, 3, 4))]
        base = DIAG + 3 * PART if k == 1 else 0
        ih, il, up, low, mine_out = panel_call(k, base, info, index_map, pieces, head_rows, ups, flat_invs)
        flat_invs += [ih, il]
        ups.append(up)
        invs.append(ih)
        lows.append(low)
        mines.append(mine_out)
    out = tail_call(info, index_map, front, a12, wide, thick, head_rows, ups[1:], invs, lows, mines[1:])
    return out[None]


def solution(mesh):
    split_mesh = Mesh(mesh.devices.reshape(2, N_ROW, 4, 4), ("cube", "row", "z", "y"))
    return jax.shard_map(
        per_device,
        mesh=split_mesh,
        in_specs=(P("cube", "row", COL), P("cube", "row", COL), P("cube", None)),
        out_specs=P("cube", "row", COL),
        check_vma=False,
    )
```

```python
import functools

import jax
import jax.numpy as jnp
from jax import lax
from jax.experimental import pallas as pl
from jax.experimental.pallas import tpu as pltpu
from jax.sharding import Mesh
from jax.sharding import PartitionSpec as P

BLK = 128
PANEL = 384
PANELS = 4
N_ROW = 4
N_COL = 16
PIECE = PANEL // N_ROW
PART = BLK // N_ROW
DIAG = 4 * PART
LEAD = PANEL * PANELS
COL = ("z", "y")
F32 = jnp.float32
BF16 = jnp.bfloat16

SOURCES = {11: [3, 4, 5], 12: [4, 5, 6, 7, 8], 13: [7, 8, 9, 10, 11], 14: [10, 11, 12, 13, 14], 15: [13, 14, 15]}
THICK = 5


def dot(a, b, ca, cb):
    return lax.dot_general(a, b, (((ca,), (cb,)), ((), ())), preferred_element_type=F32)


def split(x):
    high = x.astype(BF16)
    return high, (x - high.astype(F32)).astype(BF16)


def dot3(a, b, ca, cb):
    ah, al = split(a)
    bh, bl = split(b)
    return dot(jnp.concatenate([ah, ah, al], ca), jnp.concatenate([bh, bl, bh], cb), ca, cb)


def over_rows(x, i):
    return jnp.broadcast_to(x[i : i + 1, :], x.shape)


def over_lanes(x, j):
    return jnp.broadcast_to(x[:, j : j + 1], x.shape)


def factor_block(tiles, group=4):
    sub = lax.broadcasted_iota(jnp.int32, (8, BLK), 0)
    lane = lax.broadcasted_iota(jnp.int32, (8, BLK), 1)
    v = list(tiles)
    inv, upper, scale = [None] * 16, [None] * 16, [None] * 16
    for g in range(0, 16, group):
        for t in range(g, g + group):
            qs = range(t, g + group)
            c = {(q, j): over_lanes(v[q], 8 * t + j) for q in qs for j in range(8)}
            block = (lane >= 8 * t) & (lane < 8 * t + 8)
            sc = jnp.zeros((8, BLK), F32)
            w = {q: jnp.where(block, 0.0, v[q]) for q in qs}
            w[t] = jnp.where(lane - 8 * t == sub, 1.0, w[t])
            u = v[t]
            for i in range(8):
                pivot = over_rows(c[t, i], i)
                r = 1.0 / pivot
                sc = jnp.where(sub == i, lax.rsqrt(pivot), sc)
                m = {q: c[q, i] * r for q in qs}
                m[t] = jnp.where(sub > i, m[t], 0.0)
                for j in range(i + 1, 8):
                    row = over_rows(c[t, j], i)
                    for q in qs:
                        c[q, j] = c[q, j] - m[q] * row
                row = over_rows(w[t], i)
                for q in qs:
                    if q != t or i < 7:
                        w[q] = w[q] - m[q] * row
                if i < 7:
                    u = u - m[t] * over_rows(u, i)
            inv[t], scale[t], upper[t] = w[t], sc, u
            for q in range(t + 1, g + group):
                v[q] = w[q]
        if g + group < 16:
            sg = jnp.concatenate(scale[g : g + group], 0)
            ug = jnp.concatenate(upper[g : g + group], 0) * sg
            done = [
                jnp.where((lane >= 8 * t + 8) & (lane < 8 * g + 8 * group), 0.0, inv[t]) for t in range(g, g + group)
            ]
            wg = jnp.concatenate(done, 0) * sg
            update = dot3(ug, wg, 0, 0)
            block = (lane >= 8 * g) & (lane < 8 * g + 8 * group)
            for q in range(g + group, 16):
                v[q] = jnp.where(block, 0.0, v[q]) - update[8 * q : 8 * q + 8, :]
    return [a * s for a, s in zip(inv, scale)], [a * s for a, s in zip(upper, scale)]


def factor_panel(p, li, ud):
    sub = lax.broadcasted_iota(jnp.int32, (8, BLK), 0)
    lane = lax.broadcasted_iota(jnp.int32, (8, BLK), 1)

    def step(j, _):
        at = pl.multiple_of(j * BLK, BLK)
        inv, upper = factor_block([p[pl.ds(at + 8 * q, 8), pl.ds(at, BLK)] for q in range(16)])
        for q in range(16):
            li[8 * q : 8 * q + 8, :] = jnp.where(lane <= sub + 8 * q, inv[q], 0.0)
            ud[pl.ds(at + 8 * q, 8), :] = jnp.where(lane >= sub + 8 * q, upper[q], 0.0)
        row = dot3(li[...], p[pl.ds(at, BLK), :], 1, 0)
        p[pl.ds(at, BLK), :] = row
        p[pl.ds(at, BLK), pl.ds(at, BLK)] = li[...]
        for k in range(1, 3):

            @pl.when(k > j)
            def _():
                rows = slice(k * BLK, k * BLK + BLK)
                p[rows, pl.ds(at, BLK)] = jnp.zeros((BLK, BLK), F32)
                p[rows, :] = p[rows, :] - dot3(row[:, rows], p[pl.ds(at, BLK), :], 0, 0)

        return 0

    lax.fori_loop(0, 3, step, 0)


def unpack_child(t, piece, x):
    at = pl.multiple_of(x * PIECE, 16)
    for b in range(3):
        for u in range(3):
            t[pl.ds(at + PART * u, PART), b * BLK : (b + 1) * BLK] = piece[
                DIAG + PART * b : DIAG + PART * (b + 1), u * BLK : (u + 1) * BLK
            ].astype(F32)


def panel_kernel(k, base, marks, info, maps, *refs):
    r = list(refs)
    pieces, r = r[:4], r[4:]
    t_pieces, r = (r[:4], r[4:]) if k else (pieces, r)
    packs, r = r[:k], r[k:]
    r = r[marks:]
    _, pack, result, a, t, p, li, ud, low, sem = r
    me = info[0]
    col = info[1]
    for s in range(4):
        x = lax.rem(me + 4 - s, 4)
        buf = pieces[s]
        for j in range(k):
            at = pl.multiple_of(j * PANEL + x * PIECE, 16)
            a[pl.ds(at, PIECE), :] = buf[base + DIAG + j * PIECE : base + DIAG + (j + 1) * PIECE, :].astype(F32)
        at = pl.multiple_of(x * PART, PART)
        first = buf[base : base + PART, :].astype(F32) + buf[base + 2 * PART : base + 3 * PART, :].astype(F32)
        rest = buf[base + PART : base + 2 * PART, :].astype(F32) + buf[base + 3 * PART : base + 4 * PART, :].astype(F32)
        a[pl.ds(k * PANEL + at, PART), :] = first
        a[pl.ds(k * PANEL + BLK + at, PART), BLK:] = rest[:, : 2 * BLK]
        a[pl.ds(k * PANEL + 2 * BLK + at, PART), 2 * BLK :] = rest[:, 2 * BLK :]
        unpack_child(t, t_pieces[s], x)
    for b in range(3):
        mb = maps[b] - 3 * k
        for i in range(b + 1):
            ma = maps[i]

            @pl.when((mb >= 0) & (mb < 3) & (ma < 3 * (k + 1)))
            def _():
                rows = pl.ds(pl.multiple_of(ma * BLK, BLK), BLK)
                cols = pl.ds(pl.multiple_of(mb * BLK, BLK), BLK)
                a[rows, cols] = a[rows, cols] + t[i * BLK : (i + 1) * BLK, b * BLK : (b + 1) * BLK]

    up = 2 * PANEL
    for j in range(k):
        z = a[j * PANEL : (j + 1) * PANEL, :]
        if j:
            z = z - dot(packs[j][up : up + j * PANEL, :], pack[up : up + j * PANEL, :], 0, 0)
        zh, zl = split(z)
        ih, il = packs[j][:PANEL, :], packs[j][PANEL:up, :]
        uf = dot(ih, zh, 1, 0) + (dot(ih, zl, 1, 0) + dot(il, zh, 1, 0))

        @pl.when((me == 0) & (col == j))
        def _():
            low[...] = uf.T

        pack[up + j * PANEL : up + (j + 1) * PANEL, :] = uf.astype(BF16)
    z = a[k * PANEL : (k + 1) * PANEL, :]
    if k:
        u = pack[up : up + k * PANEL, :]
        z = z - dot(u, u, 0, 0)
    p[...] = z
    factor_panel(p, li, ud)
    for i in range(3):
        ri = slice(i * BLK, (i + 1) * BLK)
        for j in range(3):
            rj = slice(j * BLK, (j + 1) * BLK)
            lo = slice(PANEL + i * BLK, PANEL + (i + 1) * BLK)
            if j <= i:
                pack[ri, rj], pack[lo, rj] = split(p[ri, rj])
            else:
                pack[ri, rj] = jnp.zeros((BLK, BLK), BF16)
                pack[lo, rj] = jnp.zeros((BLK, BLK), BF16)

    @pl.when((me == 0) & (col == k))
    def _():
        for i in range(3):
            ri = slice(i * BLK, (i + 1) * BLK)
            low[ri, ri] = ud[ri, :].T
            for j in range(i + 1, 3):
                rj = slice(j * BLK, (j + 1) * BLK)
                low[ri, rj] = jnp.zeros((BLK, BLK), F32)
                low[rj, ri] = p[ri, rj].T

    @pl.when((me == 0) & (col > k) & (col < PANELS))
    def _():
        low[...] = jnp.zeros((PANEL, PANEL), F32)

    @pl.when((me == 0) & (col < PANELS))
    def _():
        copy = pltpu.make_async_copy(low, result.at[pl.ds(k * PANEL, PANEL), :], sem)
        copy.start()
        copy.wait()


def panel_call(k, base, info, maps, pieces, t_pieces, packs, marks, result):
    vm = pl.BlockSpec(memory_space=pltpu.VMEM)
    sm = pl.BlockSpec(memory_space=pltpu.SMEM)
    anywhere = pl.BlockSpec(memory_space=pl.ANY)
    args = list(pieces) + (list(t_pieces) if k else []) + list(packs)
    sq = (PANEL, PANEL)
    return pl.pallas_call(
        functools.partial(panel_kernel, k, base, len(marks)),
        out_shape=[
            jax.ShapeDtypeStruct(((2 + k) * PANEL, PANEL), BF16),
            jax.ShapeDtypeStruct((LEAD, PANEL), F32),
        ],
        in_specs=[sm, sm] + [vm] * len(args) + [anywhere] * (len(marks) + 1),
        out_specs=[vm, anywhere],
        scratch_shapes=[
            pltpu.VMEM(((k + 1) * PANEL, PANEL), F32),
            pltpu.VMEM(sq, F32),
            pltpu.VMEM(sq, F32),
            pltpu.VMEM((BLK, BLK), F32),
            pltpu.VMEM((PANEL, BLK), F32),
            pltpu.VMEM(sq, F32),
            pltpu.SemaphoreType.DMA,
        ],
        input_output_aliases={2 + len(args) + len(marks): 1},
        compiler_params=pltpu.CompilerParams(vmem_limit_bytes=32 * 2**20),
        cost_estimate=pl.CostEstimate(flops=10**10, bytes_accessed=10**6, transcendentals=0),
        name=f"panel{k}",
    )(info, maps, *args, *marks, result)


def pack_kernel(info, front, high, lead, *outs):
    heads, rests = outs[:4], outs[4:]
    at = pl.multiple_of(info[3] * PANEL, PANEL)
    full = front[...].astype(BF16)
    high[...] = full
    lead[...] = jnp.where(info[0] == 0, full, jnp.zeros((), BF16))
    for s in range(4):
        a = front[pl.ds(at + s * PART, PART), :]
        b = front[pl.ds(at + BLK + s * PART, PART), BLK:]
        c = front[pl.ds(at + 2 * BLK + s * PART, PART), 2 * BLK :]
        ah, al = split(a)
        bh, bl = split(b)
        ch, cl = split(c)
        for out in (heads[s], rests[s]):
            out[0:PART, :] = ah
            out[PART : 2 * PART, : 2 * BLK] = bh
            out[PART : 2 * PART, 2 * BLK :] = ch
            out[2 * PART : 3 * PART, :] = al
            out[3 * PART : 4 * PART, : 2 * BLK] = bl
            out[3 * PART : 4 * PART, 2 * BLK :] = cl
        for j in range(3):
            rests[s][DIAG + j * PIECE : DIAG + (j + 1) * PIECE, :] = full[j * PANEL + s * PIECE : j * PANEL + (s + 1) * PIECE]
        heads[s][DIAG : DIAG + PART, :] = jnp.zeros((PART, PANEL), BF16)
        heads[s][DIAG + PART :, :] = full[s * PIECE : (s + 1) * PIECE]


def child_kernel(child, *refs):
    for s in range(4):
        refs[4 + s][...] = refs[s][...]
        for u in range(3):
            rows = s * PIECE + u * PART
            refs[4 + s][DIAG : DIAG + PART, u * BLK : (u + 1) * BLK] = child[rows : rows + PART, :]


def pack_call(info, front):
    vm = pl.BlockSpec(memory_space=pltpu.VMEM)
    sm = pl.BlockSpec(memory_space=pltpu.SMEM)
    full = jax.ShapeDtypeStruct((LEAD, PANEL), BF16)
    head = jax.ShapeDtypeStruct((DIAG + PART + PIECE, PANEL), BF16)
    rest = jax.ShapeDtypeStruct((DIAG + 3 * PIECE, PANEL), BF16)
    out = pl.pallas_call(
        pack_kernel,
        out_shape=[full, full] + [head] * 4 + [rest] * 4,
        in_specs=[sm, vm],
        out_specs=[vm] * 10,
        compiler_params=pltpu.CompilerParams(vmem_limit_bytes=24 * 2**20),
        name="pack",
    )(info, front)
    return out[0], out[1], out[2:6], out[6:]


def child_call(child, heads):
    vm = pl.BlockSpec(memory_space=pltpu.VMEM)
    return pl.pallas_call(
        child_kernel,
        out_shape=[jax.ShapeDtypeStruct(h.shape, h.dtype) for h in heads],
        in_specs=[vm] * 5,
        out_specs=[vm] * 4,
        name="child",
    )(child, *heads)


def tail_kernel(info, maps, front, a12, wide, *refs):
    r = list(refs)
    thick, r = r[:THICK], r[THICK:]
    packs, r = r[:PANELS], r[PANELS:]
    t_pieces, r = r[:4], r[4:]
    _, out, r = r[0], r[1], r[2:]
    inv, ups, a12v, x, xb, t, wv, fv, tv, yb = r[:10]
    sem_p, sem_a, sem_w, sem_f, sem_t, sem_o = r[10:]
    me = info[0]
    col = info[1]
    first = info[2]

    def blk(i):
        return slice(i * BLK, (i + 1) * BLK)

    def pan(i):
        return slice(i * PANEL, (i + 1) * PANEL)

    def tile(q):
        return pl.ds(pl.multiple_of(q * PANEL, PANEL), PANEL)

    def up_rows(j):
        return slice(j * (j - 1) // 2 * PANEL, j * (j + 1) // 2 * PANEL)

    copy = pltpu.make_async_copy
    pack_copies = []
    for j in range(PANELS):
        pack_copies.append(copy(packs[j].at[:PANEL, :], inv.at[j], sem_p.at[2 * j]))
        if j:
            pack_copies.append(copy(packs[j].at[2 * PANEL :, :], ups.at[up_rows(j), :], sem_p.at[2 * j + 1]))

    def wide_copy(q):
        return copy(wide.at[pl.ds(4 * q, 4)], wv.at[pl.ds(4 * q, 4)], sem_w.at[q])

    def front_copy(q):
        return copy(front.at[tile(q), :], fv.at[tile(q), :], sem_f.at[q])

    def out_copy(q):
        return copy(fv.at[tile(q), :], out.at[tile(q), :], sem_o.at[q])

    def slot_of(value):
        slot = value - 3 * col
        return slot, (slot >= 0) & (slot < 3)

    def add(ref, row_block, col_slot, value):
        rows = pl.ds(pl.multiple_of(row_block * BLK, BLK), BLK)
        cols = pl.ds(pl.multiple_of(col_slot * BLK, BLK), BLK)
        ref[rows, cols] = ref[rows, cols] + value

    right = col >= PANELS
    lower = me > 0

    @pl.when(right | lower)
    def _():
        for c in pack_copies:
            c.start()

    @pl.when(right & lower)
    def _():
        copy(a12, a12v, sem_a).start()

    @pl.when(right & (me == 0))
    def _():
        for q in range(4):
            front_copy(q).start()

    for j in range(THICK):

        @pl.when(slot_of(info[8 + j])[1])
        def _():
            copy(thick[j], tv.at[j], sem_t.at[j]).start()

    @pl.when(lower)
    def _():
        for q in range(4):
            wide_copy(q).start()

        @pl.when(right)
        def _():
            for q in range(4):
                front_copy(q).start()

    for s in range(4):
        unpack_child(t, t_pieces[s], lax.rem(me + 4 - s, 4))

    @pl.when(right | lower)
    def _():
        for c in pack_copies:
            c.wait()

    for j in range(THICK):

        @pl.when(slot_of(info[8 + j])[1])
        def _():
            copy(thick[j], tv.at[j], sem_t.at[j]).wait()

    @pl.when(right)
    def _():
        @pl.when(me == 0)
        def _():
            for q in range(4):
                front_copy(q).wait()
            x[...] = fv[...]

        @pl.when(lower)
        def _():
            copy(a12, a12v, sem_a).wait()
            x[...] = a12v[...].astype(F32)

        for i in range(3):
            ma = maps[i]

            @pl.when(ma < 12)
            def _():
                for b in range(3):
                    slot, here = slot_of(maps[b])

                    @pl.when(here)
                    def _():
                        add(x, ma, slot, t[blk(i), blk(b)])

                for j in range(THICK):
                    slot, here = slot_of(info[8 + j])

                    @pl.when(here)
                    def _():
                        add(x, ma, slot, tv[j, blk(i), :].astype(F32))

        for j in range(PANELS):
            z = x[pan(j), :]
            if j:
                z = z - dot(ups[up_rows(j), :], xb[: j * PANEL, :], 0, 0)

            @pl.when(me == 0)
            def _():
                fv[pan(j), :] = z
                out_copy(j).start()

            xb[pan(j), :] = dot(inv[j], z.astype(BF16), 1, 0).astype(BF16)

        @pl.when(me == 0)
        def _():
            for q in range(4):
                out_copy(q).wait()

    @pl.when(lower)
    def _():
        for q in range(4):
            wide_copy(q).wait()

        def rows_step(q, _):
            @pl.when(right)
            def _():
                front_copy(q).wait()

            for i in range(12):
                ma = maps[first + i] - 12 * me

                @pl.when((ma >= 3 * q) & (ma < 3 * q + 3))
                def _():
                    rows = pl.ds(pl.multiple_of((ma - 3 * q) * BLK, BLK), BLK)
                    for b in range(3):
                        mb = maps[b]
                        piece = wv[(i // 3) * 4 + b, blk(i % 3), PANEL : PANEL + BLK]

                        @pl.when(mb < 12)
                        def _():
                            panel = mb // 3
                            cols = pl.ds(pl.multiple_of((mb - panel * 3) * BLK, BLK), BLK)
                            at = 4 * q + panel
                            wv[at, rows, cols] = (wv[at, rows, cols].astype(F32) + piece.astype(F32)).astype(BF16)

                        slot, here = slot_of(mb)

                        @pl.when(right & here)
                        def _():
                            add(fv, ma, slot, piece.astype(F32))

                    for j in range(THICK):
                        slot, here = slot_of(info[8 + j])

                        @pl.when(here)
                        def _():
                            held = pl.ds(pl.multiple_of((first + i) * BLK, BLK), BLK)
                            add(fv, ma, slot, tv[j, held, :].astype(F32))

            for k in range(PANELS):
                z = wv[4 * q + k, :, :PANEL]
                if k:
                    z = (z.astype(F32) - dot(yb[:, : k * PANEL], ups[up_rows(k), :], 1, 0)).astype(BF16)
                full = dot(z, inv[k], 1, 1)
                yb[:, pan(k)] = full.astype(BF16)

                @pl.when(col == k)
                def _():
                    fv[tile(q), :] = full

            @pl.when(right)
            def _():
                fv[tile(q), :] = fv[tile(q), :] - dot(yb[...], xb[...], 1, 0)

            out_copy(q).start()
            return 0

        lax.fori_loop(0, 4, rows_step, 0)
        for q in range(4):
            out_copy(q).wait()


def tail_call(info, maps, front, a12, wide, thick, t_pieces, packs, result):
    vm = pl.BlockSpec(memory_space=pltpu.VMEM)
    sm = pl.BlockSpec(memory_space=pltpu.SMEM)
    anywhere = pl.BlockSpec(memory_space=pl.ANY)
    sem = pltpu.SemaphoreType.DMA
    args = [front, a12, wide, *thick, *packs]
    return pl.pallas_call(
        tail_kernel,
        out_shape=jax.ShapeDtypeStruct((LEAD, PANEL), F32),
        in_specs=[sm, sm] + [anywhere] * len(args) + [vm] * 4 + [anywhere],
        out_specs=anywhere,
        scratch_shapes=[
            pltpu.VMEM((PANELS, PANEL, PANEL), BF16),
            pltpu.VMEM((6 * PANEL, PANEL), BF16),
            pltpu.VMEM((LEAD, PANEL), BF16),
            pltpu.VMEM((LEAD, PANEL), F32),
            pltpu.VMEM((LEAD, PANEL), BF16),
            pltpu.VMEM((PANEL, PANEL), F32),
            pltpu.VMEM((N_COL, PANEL, PANEL + BLK), BF16),
            pltpu.VMEM((LEAD, PANEL), F32),
            pltpu.VMEM((THICK, 16 * BLK, BLK), BF16),
            pltpu.VMEM((PANEL, LEAD), BF16),
            sem((2 * PANELS,)),
            sem,
            sem((4,)),
            sem((4,)),
            sem((THICK,)),
            sem((4,)),
        ],
        input_output_aliases={2 + len(args) + 4: 0},
        compiler_params=pltpu.CompilerParams(vmem_limit_bytes=36 * 2**20),
        cost_estimate=pl.CostEstimate(flops=7 * 10**9, bytes_accessed=2 * 10**7, transcendentals=0),
        name="tail",
    )(info, maps, *args, *t_pieces, result)


def per_device(front_init, contribution, maps):
    front = front_init[0]
    index_map = maps[0]
    me = lax.axis_index("row")
    col = lax.axis_index(COL)
    y = lax.axis_index("y")
    grid = ("row", "z", "y")

    def flat(r, c):
        return r * N_COL + c

    def x_from0(value, s, cols):
        return lax.ppermute(value, grid, [(flat(0, c), flat(s, c)) for c in cols])

    def z_from0(value, s):
        return lax.ppermute(value, COL, [(b, 4 * s + b) for b in range(4)])

    def x_shift(value, s):
        return lax.ppermute(value, "row", [(i, (i + s) % 4) for i in range(4)])

    def y_shift(value, s):
        return lax.ppermute(value, COL, [(4 * z + b, 4 * z + (b + s) % 4) for z in range(4) for b in range(4)])

    def never(mark):
        return mark[0, 0] > 3e38

    def own_or(root, value, *got):
        out = jnp.where(root, value, jnp.zeros((), BF16))
        for g in got:
            out = out + g
        return out

    def by_source(value, shift, index, order):
        around = jnp.stack([value] + [shift(value, s) for s in range(1, 4)])
        return [lax.dynamic_index_in_dim(around, lax.rem(index + 4 - k, 4), 0, keepdims=False) for k in order]

    received = lax.ppermute(contribution[0], "cube", [(0, 1), (1, 0)])
    first = jnp.where(me == 3, 4, 0)
    high, lead, heads, rests = pack_call(jnp.stack([me, col, first, y]).astype(jnp.int32), front)
    heads = child_call(received, heads)

    def x_swap(value, m):
        return lax.ppermute(value, "row", [(i, i ^ m) for i in range(4)])

    def x_pairs(value, pairs, cols):
        return lax.ppermute(value, grid, [(flat(p, c), flat(q, c)) for p, q in pairs for c in cols])

    def z_pairs(value, pairs):
        return lax.ppermute(value, COL, [(4 * p + b, 4 * q + b) for p, q in pairs for b in range(4)])

    def halves(value):
        n = value.shape[0] // 2
        return value[:n], value[n:]

    late_cols = (2, 3)
    a12 = lax.psum(lead, "row")
    rest_two = x_pairs(jnp.concatenate([rests[2], rests[3]], axis=0), [(0, 3)], late_cols)
    head = own_or(me == 0, heads[0], *[x_from0(heads[s], s, range(3)) for s in range(1, 4)])
    child_one = x_swap(received, 1)
    for_two, for_three = halves(rest_two)
    got = x_pairs(jnp.where((me == 0) | never(head), rests[1], for_two), [(0, 1), (3, 2)], late_cols)
    even = (me % 2 == 0) | never(head)
    pair = jnp.where(even, jnp.stack([received, child_one]), jnp.stack([child_one, received]))
    pair = pair.reshape(-1, BLK)
    child_two = x_swap(pair, 3)

    head_z = own_or(col < 4, head, *[z_from0(head, s) for s in range(1, 4)])
    rest = jnp.where((me == 0) | never(head_z), rests[0], jnp.where(me == 3, for_three, got))
    low_rows = me < 2
    column = jnp.where(low_rows, jnp.concatenate([pair, child_two], axis=0), jnp.concatenate([child_two, pair], axis=0))
    chosen = lax.dynamic_slice_in_dim(column, first * BLK, 12 * BLK, 0)
    panel_wide = jnp.concatenate([high, chosen], axis=1)
    rest_z1 = z_pairs(rest, [(0, 1)])

    head_y = by_source(head_z, y_shift, y, range(3))
    child = slice(DIAG, DIAG + PART)
    g01 = jnp.concatenate(
        [head_y[0][: DIAG + PART], head_y[1][child], head_y[2][child], head_y[1][:DIAG], head_y[1][DIAG + PART :]], axis=0
    )
    z = lax.axis_index("z")
    at_zero = (z == 0) | never(g01)
    rest_z2 = z_pairs(jnp.where(at_zero, rest, rest_z1), [(0, 3), (1, 2)])

    g01 = [g01] + [x_shift(g01, s) for s in range(1, 4)]
    arrived = never(g01[1]) | never(g01[2]) | never(g01[3])
    rest = jnp.where((z == 0) | arrived, rest, jnp.where(z == 1, rest_z1, rest_z2))
    rest_y = by_source(rest, y_shift, y, (2, 3))
    wide_in = jnp.where(at_zero, panel_wide, jnp.zeros((), BF16))
    wide_part = lax.psum_scatter(wide_in, "z", tiled=True)
    wide = lax.all_gather(wide_part, COL)

    ids = jnp.full((N_COL, THICK), -1, jnp.int32)
    for c in SOURCES:
        for j, b in enumerate(SOURCES[c]):
            ids = ids.at[c, j].set(b)
    held = jnp.take(ids, col, axis=0)
    targets = jnp.where(held >= 0, jnp.take(index_map, jnp.maximum(held, 0)), -1000)
    info = jnp.concatenate(
        [jnp.stack([me, col, first, 0, 0, 0, 0, 0]).astype(jnp.int32), targets.astype(jnp.int32), jnp.zeros((3,), jnp.int32)]
    )

    def contribution_column(value, j):
        pairs = [(SOURCES[c][j], c) for c in SOURCES if j < len(SOURCES[c])]
        return lax.ppermute(value, COL, pairs)

    head_rows = g01
    thick, packs = [], []
    result = jnp.zeros((LEAD, PANEL), F32)
    for k in range(PANELS):
        if k < 2:
            pieces = head_rows
        else:
            piece = rest_y[k - 2][: DIAG + k * PIECE]
            if k == 3:
                piece = jnp.where(never(packs[1]), jnp.zeros((), BF16), piece)
            pieces = [piece] + [x_shift(piece, s) for s in range(1, 4)]
        if k:
            late = jnp.where(never(packs[k - 1]), jnp.zeros((), BF16), column)
            thick += [contribution_column(late, j) for j in ((0, 1), (2, 3), (4,))[k - 1]]
        base = DIAG + 3 * PART if k == 1 else 0
        marks = [[wide_in], [wide_part], [], []][k]
        pack, result = panel_call(k, base, info, index_map, pieces, head_rows, packs, marks, result)
        packs.append(pack)
    out = tail_call(info, index_map, front, a12, wide, thick, head_rows, packs, result)
    return out[None]


def solution(mesh):
    split_mesh = Mesh(mesh.devices.reshape(2, N_ROW, 4, 4), ("cube", "row", "z", "y"))
    return jax.shard_map(
        per_device,
        mesh=split_mesh,
        in_specs=(P("cube", "row", COL), P("cube", "row", COL), P("cube", None)),
        out_specs=P("cube", "row", COL),
        check_vma=False,
    )
```

```python
import functools

import jax
import jax.numpy as jnp
from jax import lax
from jax.experimental import pallas as pl
from jax.experimental.pallas import tpu as pltpu
from jax.sharding import Mesh
from jax.sharding import PartitionSpec as P

BLK = 128
PANEL = 384
PANELS = 4
N_ROW = 4
N_COL = 16
PIECE = PANEL // N_ROW
PART = BLK // N_ROW
DIAG = 4 * PART
LEAD = PANEL * PANELS
COL = ("z", "y")
F32 = jnp.float32
BF16 = jnp.bfloat16

SOURCES = {11: [3, 4, 5], 12: [4, 5, 6, 7, 8], 13: [7, 8, 9, 10, 11], 14: [10, 11, 12, 13, 14], 15: [13, 14, 15]}
THICK = 5


def dot(a, b, ca, cb):
    return lax.dot_general(a, b, (((ca,), (cb,)), ((), ())), preferred_element_type=F32)


def split(x):
    high = x.astype(BF16)
    return high, (x - high.astype(F32)).astype(BF16)


def dot3(a, b, ca, cb):
    ah, al = split(a)
    bh, bl = split(b)
    return dot(jnp.concatenate([ah, ah, al], ca), jnp.concatenate([bh, bl, bh], cb), ca, cb)


def over_rows(x, i):
    return jnp.broadcast_to(x[i : i + 1, :], x.shape)


def over_lanes(x, j):
    return jnp.broadcast_to(x[:, j : j + 1], x.shape)


def factor_block(tiles, group=4):
    sub = lax.broadcasted_iota(jnp.int32, (8, BLK), 0)
    lane = lax.broadcasted_iota(jnp.int32, (8, BLK), 1)
    v = list(tiles)
    inv, upper, scale = [None] * 16, [None] * 16, [None] * 16
    for g in range(0, 16, group):
        for t in range(g, g + group):
            qs = range(t, g + group)
            c = {(q, j): over_lanes(v[q], 8 * t + j) for q in qs for j in range(8)}
            block = (lane >= 8 * t) & (lane < 8 * t + 8)
            sc = jnp.zeros((8, BLK), F32)
            w = {q: jnp.where(block, 0.0, v[q]) for q in qs}
            w[t] = jnp.where(lane - 8 * t == sub, 1.0, w[t])
            u = v[t]
            for i in range(8):
                pivot = over_rows(c[t, i], i)
                r = 1.0 / pivot
                sc = jnp.where(sub == i, lax.rsqrt(pivot), sc)
                m = {q: c[q, i] * r for q in qs}
                m[t] = jnp.where(sub > i, m[t], 0.0)
                for j in range(i + 1, 8):
                    row = over_rows(c[t, j], i)
                    for q in qs:
                        c[q, j] = c[q, j] - m[q] * row
                row = over_rows(w[t], i)
                for q in qs:
                    if q != t or i < 7:
                        w[q] = w[q] - m[q] * row
                if i < 7:
                    u = u - m[t] * over_rows(u, i)
            inv[t], scale[t], upper[t] = w[t], sc, u
            for q in range(t + 1, g + group):
                v[q] = w[q]
        if g + group < 16:
            sg = jnp.concatenate(scale[g : g + group], 0)
            ug = jnp.concatenate(upper[g : g + group], 0) * sg
            done = [
                jnp.where((lane >= 8 * t + 8) & (lane < 8 * g + 8 * group), 0.0, inv[t]) for t in range(g, g + group)
            ]
            wg = jnp.concatenate(done, 0) * sg
            update = dot3(ug, wg, 0, 0)
            block = (lane >= 8 * g) & (lane < 8 * g + 8 * group)
            for q in range(g + group, 16):
                v[q] = jnp.where(block, 0.0, v[q]) - update[8 * q : 8 * q + 8, :]
    return [a * s for a, s in zip(inv, scale)], [a * s for a, s in zip(upper, scale)]


def factor_panel(p, li, ud):
    sub = lax.broadcasted_iota(jnp.int32, (8, BLK), 0)
    lane = lax.broadcasted_iota(jnp.int32, (8, BLK), 1)

    def step(j, _):
        at = pl.multiple_of(j * BLK, BLK)
        inv, upper = factor_block([p[pl.ds(at + 8 * q, 8), pl.ds(at, BLK)] for q in range(16)])
        for q in range(16):
            li[8 * q : 8 * q + 8, :] = jnp.where(lane <= sub + 8 * q, inv[q], 0.0)
            ud[pl.ds(at + 8 * q, 8), :] = jnp.where(lane >= sub + 8 * q, upper[q], 0.0)
        row = dot3(li[...], p[pl.ds(at, BLK), :], 1, 0)
        p[pl.ds(at, BLK), :] = row
        p[pl.ds(at, BLK), pl.ds(at, BLK)] = li[...]
        for k in range(1, 3):

            @pl.when(k > j)
            def _():
                rows = slice(k * BLK, k * BLK + BLK)
                p[rows, pl.ds(at, BLK)] = jnp.zeros((BLK, BLK), F32)
                p[rows, :] = p[rows, :] - dot3(row[:, rows], p[pl.ds(at, BLK), :], 0, 0)

        return 0

    lax.fori_loop(0, 3, step, 0)


def unpack_child(t, piece, x):
    at = pl.multiple_of(x * PIECE, 16)
    for b in range(3):
        for u in range(3):
            t[pl.ds(at + PART * u, PART), b * BLK : (b + 1) * BLK] = piece[
                DIAG + PART * b : DIAG + PART * (b + 1), u * BLK : (u + 1) * BLK
            ].astype(F32)


def panel_kernel(k, marks, info, maps, *refs):
    r = list(refs)
    pieces, r = r[:4], r[4:]
    t_pieces, r = (r[:4], r[4:]) if k else (pieces, r)
    packs, r = r[:k], r[k:]
    r = r[marks:]
    _, pack, result, a, t, p, li, ud, low, sem = r
    me = info[0]
    col = info[1]
    for s in range(4):
        x = lax.rem(me + 4 - s, 4)
        buf = pieces[s]
        for j in range(k):
            at = pl.multiple_of(j * PANEL + x * PIECE, 16)
            a[pl.ds(at, PIECE), :] = buf[DIAG + j * PIECE : DIAG + (j + 1) * PIECE, :].astype(F32)
        at = pl.multiple_of(x * PART, PART)
        first = buf[:PART, :].astype(F32) + buf[2 * PART : 3 * PART, :].astype(F32)
        rest = buf[PART : 2 * PART, :].astype(F32) + buf[3 * PART : 4 * PART, :].astype(F32)
        a[pl.ds(k * PANEL + at, PART), :] = first
        a[pl.ds(k * PANEL + BLK + at, PART), BLK:] = rest[:, : 2 * BLK]
        a[pl.ds(k * PANEL + 2 * BLK + at, PART), 2 * BLK :] = rest[:, 2 * BLK :]
        unpack_child(t, t_pieces[s], x)
    for b in range(3):
        mb = maps[b] - 3 * k
        for i in range(b + 1):
            ma = maps[i]

            @pl.when((mb >= 0) & (mb < 3) & (ma < 3 * (k + 1)))
            def _():
                rows = pl.ds(pl.multiple_of(ma * BLK, BLK), BLK)
                cols = pl.ds(pl.multiple_of(mb * BLK, BLK), BLK)
                a[rows, cols] = a[rows, cols] + t[i * BLK : (i + 1) * BLK, b * BLK : (b + 1) * BLK]

    up = 2 * PANEL
    for j in range(k):
        z = a[j * PANEL : (j + 1) * PANEL, :]
        if j:
            z = z - dot(packs[j][up : up + j * PANEL, :], pack[up : up + j * PANEL, :], 0, 0)
        zh, zl = split(z)
        ih, il = packs[j][:PANEL, :], packs[j][PANEL:up, :]
        uf = dot(ih, zh, 1, 0) + (dot(ih, zl, 1, 0) + dot(il, zh, 1, 0))

        @pl.when((me == 0) & (col == j))
        def _():
            low[...] = uf.T

        pack[up + j * PANEL : up + (j + 1) * PANEL, :] = uf.astype(BF16)
    z = a[k * PANEL : (k + 1) * PANEL, :]
    if k:
        u = pack[up : up + k * PANEL, :]
        z = z - dot(u, u, 0, 0)
    p[...] = z
    factor_panel(p, li, ud)
    for i in range(3):
        ri = slice(i * BLK, (i + 1) * BLK)
        for j in range(3):
            rj = slice(j * BLK, (j + 1) * BLK)
            lo = slice(PANEL + i * BLK, PANEL + (i + 1) * BLK)
            if j <= i:
                pack[ri, rj], pack[lo, rj] = split(p[ri, rj])
            else:
                pack[ri, rj] = jnp.zeros((BLK, BLK), BF16)
                pack[lo, rj] = jnp.zeros((BLK, BLK), BF16)

    @pl.when((me == 0) & (col == k))
    def _():
        for i in range(3):
            ri = slice(i * BLK, (i + 1) * BLK)
            low[ri, ri] = ud[ri, :].T
            for j in range(i + 1, 3):
                rj = slice(j * BLK, (j + 1) * BLK)
                low[ri, rj] = jnp.zeros((BLK, BLK), F32)
                low[rj, ri] = p[ri, rj].T

    @pl.when((me == 0) & (col > k) & (col < PANELS))
    def _():
        low[...] = jnp.zeros((PANEL, PANEL), F32)

    @pl.when((me == 0) & (col < PANELS))
    def _():
        copy = pltpu.make_async_copy(low, result.at[pl.ds(k * PANEL, PANEL), :], sem)
        copy.start()
        copy.wait()


def panel_call(k, info, maps, pieces, t_pieces, packs, marks, result):
    vm = pl.BlockSpec(memory_space=pltpu.VMEM)
    sm = pl.BlockSpec(memory_space=pltpu.SMEM)
    anywhere = pl.BlockSpec(memory_space=pl.ANY)
    args = list(pieces) + (list(t_pieces) if k else []) + list(packs)
    sq = (PANEL, PANEL)
    return pl.pallas_call(
        functools.partial(panel_kernel, k, len(marks)),
        out_shape=[
            jax.ShapeDtypeStruct(((2 + k) * PANEL, PANEL), BF16),
            jax.ShapeDtypeStruct((LEAD, PANEL), F32),
        ],
        in_specs=[sm, sm] + [vm] * len(args) + [anywhere] * (len(marks) + 1),
        out_specs=[vm, anywhere],
        scratch_shapes=[
            pltpu.VMEM(((k + 1) * PANEL, PANEL), F32),
            pltpu.VMEM(sq, F32),
            pltpu.VMEM(sq, F32),
            pltpu.VMEM((BLK, BLK), F32),
            pltpu.VMEM((PANEL, BLK), F32),
            pltpu.VMEM(sq, F32),
            pltpu.SemaphoreType.DMA,
        ],
        input_output_aliases={2 + len(args) + len(marks): 1},
        compiler_params=pltpu.CompilerParams(vmem_limit_bytes=32 * 2**20),
        cost_estimate=pl.CostEstimate(flops=10**10, bytes_accessed=10**6, transcendentals=0),
        name=f"panel{k}",
    )(info, maps, *args, *marks, result)


def vmem_call(kernel, outs, scalars, args, marks=(), name=None):
    vm = pl.BlockSpec(memory_space=pltpu.VMEM)
    sm = pl.BlockSpec(memory_space=pltpu.SMEM)
    anywhere = pl.BlockSpec(memory_space=pl.ANY)

    def body(info, *refs):
        kernel(info, refs[: len(args)], refs[len(args) + len(marks) :])

    return pl.pallas_call(
        body,
        out_shape=[jax.ShapeDtypeStruct(shape, BF16) for shape in outs],
        in_specs=[sm] + [vm] * len(args) + [anywhere] * len(marks),
        out_specs=[vm] * len(outs),
        compiler_params=pltpu.CompilerParams(vmem_limit_bytes=32 * 2**20),
        name=name,
    )(scalars, *args, *marks)


REST = DIAG + 3 * PIECE
CHILD = DIAG + 2 * PIECE


def pick(outs, index, refs):
    for i, ref in enumerate(refs):

        @pl.when(index == i)
        def _():
            outs[...] = ref[...]


def pack_kernel(info, ins, outs):
    front, child = ins
    y = info[3]
    at = pl.multiple_of(y * PANEL, PANEL)
    for s, out in enumerate(outs):
        a = front[pl.ds(at + s * PART, PART), :]
        b = front[pl.ds(at + BLK + s * PART, PART), BLK:]
        c = front[pl.ds(at + 2 * BLK + s * PART, PART), 2 * BLK :]
        ah, al = split(a)
        bh, bl = split(b)
        ch, cl = split(c)
        out[:PART, :] = ah
        out[PART : 2 * PART, : 2 * BLK] = bh
        out[PART : 2 * PART, 2 * BLK :] = ch
        out[2 * PART : 3 * PART, :] = al
        out[3 * PART : DIAG, : 2 * BLK] = bl
        out[3 * PART : DIAG, 2 * BLK :] = cl
        for j in range(3):
            o = DIAG + j * PIECE
            out[o : o + PIECE, :] = front[j * PANEL + s * PIECE : j * PANEL + (s + 1) * PIECE, :].astype(BF16)

        @pl.when(y < 3)
        def _():
            for u in range(3):
                rows = s * PIECE + u * PART
                out[CHILD : CHILD + PART, u * BLK : (u + 1) * BLK] = child[rows : rows + PART, :]


def stage1_kernel(info, ins, outs):
    child, child_one, front = ins[4:]
    piece, pair, high, lead = outs
    me = info[0]
    pick(piece, me, ins[:4])
    n = child.shape[0]
    odd = lax.rem(me, 2)

    @pl.when(odd == 0)
    def _():
        pair[:n, :] = child[...]
        pair[n:, :] = child_one[...]

    @pl.when(odd == 1)
    def _():
        pair[:n, :] = child_one[...]
        pair[n:, :] = child[...]

    full = front[...].astype(BF16)
    high[...] = full
    lead[...] = jnp.where(me == 0, full, jnp.zeros((), BF16))


def stage2_kernel(info, ins, outs):
    pair, pair_got, high = ins[4:]
    piece, wide = outs
    me, z, first = info[0], info[4], info[2]
    pick(piece, z, ins[:4])

    @pl.when(z == 0)
    def _():
        wide[:, :PANEL] = high[...]
        n = 4 * BLK

        @pl.when(me < 2)
        def _():
            wide[: 2 * n, PANEL:] = pair[...]
            wide[2 * n :, PANEL:] = pair_got[:n, :]

        @pl.when(me == 2)
        def _():
            wide[: 2 * n, PANEL:] = pair_got[...]
            wide[2 * n :, PANEL:] = pair[:n, :]

        @pl.when(me == 3)
        def _():
            wide[:n, PANEL:] = pair_got[n:, :]
            wide[n:, PANEL:] = pair[...]

    @pl.when(z != 0)
    def _():
        wide[...] = jnp.zeros(wide.shape, BF16)


def stage3_kernel(info, ins, outs):
    g0, r1, r2, r3 = outs
    for s in range(4):
        source = lax.rem(info[3] + 4 - s, 4)
        for b, out in enumerate(outs):

            @pl.when(source == b)
            def _():
                if b == 0:
                    g0[:DIAG, :] = ins[s][:DIAG, :]
                else:
                    out[...] = ins[s][: out.shape[0], :]
                if b < 3:
                    g0[DIAG + b * PART : DIAG + (b + 1) * PART, :] = ins[s][CHILD : CHILD + PART, :]


def copy_kernel(info, ins, outs):
    for a, b in zip(ins, outs):
        b[...] = a[...]


def spread_kernel(info, ins, outs):
    out = outs[0]
    out[...] = jnp.zeros(out.shape, BF16)
    for j, ref in enumerate(ins):
        slot = info[8 + j] - 3 * info[1]

        @pl.when((slot >= 0) & (slot < 3))
        def _():
            out[:, pl.ds(pl.multiple_of(slot * BLK, BLK), BLK)] = ref[...]


def tail_kernel(info, maps, front, a12, wide, *refs):
    r = list(refs)
    thick, r = r[:4], r[4:]
    packs, r = r[:PANELS], r[PANELS:]
    t_pieces, r = r[:4], r[4:]
    _, out, r = r[0], r[1], r[2:]
    inv, ups, a12v, x, xb, t, wv, fv, tv, yb = r[:10]
    sem_p, sem_a, sem_w, sem_f, sem_t, sem_o = r[10:]
    me = info[0]
    col = info[1]
    first = info[2]

    def blk(i):
        return slice(i * BLK, (i + 1) * BLK)

    def pan(i):
        return slice(i * PANEL, (i + 1) * PANEL)

    def tile(q):
        return pl.ds(pl.multiple_of(q * PANEL, PANEL), PANEL)

    def up_rows(j):
        return slice(j * (j - 1) // 2 * PANEL, j * (j + 1) // 2 * PANEL)

    copy = pltpu.make_async_copy
    pack_copies = []
    for j in range(PANELS):
        pack_copies.append(copy(packs[j].at[:PANEL, :], inv.at[j], sem_p.at[2 * j]))
        if j:
            pack_copies.append(copy(packs[j].at[2 * PANEL :, :], ups.at[up_rows(j), :], sem_p.at[2 * j + 1]))

    def wide_copy(q):
        return copy(wide.at[pl.ds(4 * q, 4)], wv.at[pl.ds(4 * q, 4)], sem_w.at[q])

    def front_copy(q):
        return copy(front.at[tile(q), :], fv.at[tile(q), :], sem_f.at[q])

    def out_copy(q):
        return copy(fv.at[tile(q), :], out.at[tile(q), :], sem_o.at[q])

    def slot_of(value):
        slot = value - 3 * col
        return slot, (slot >= 0) & (slot < 3)

    def add(ref, row_block, col_slot, value):
        rows = pl.ds(pl.multiple_of(row_block * BLK, BLK), BLK)
        cols = pl.ds(pl.multiple_of(col_slot * BLK, BLK), BLK)
        ref[rows, cols] = ref[rows, cols] + value

    right = col >= PANELS
    lower = me > 0

    @pl.when(right | lower)
    def _():
        for c in pack_copies:
            c.start()

    @pl.when(right & lower)
    def _():
        copy(a12, a12v, sem_a).start()

    @pl.when(right & (me == 0))
    def _():
        for q in range(4):
            front_copy(q).start()

    far = col >= min(SOURCES)

    def thick_copy(i):
        return copy(thick[i], tv.at[lax.rem(me + 4 - i, 4)], sem_t.at[i])

    @pl.when(far)
    def _():
        for i in range(4):
            thick_copy(i).start()

    @pl.when(lower)
    def _():
        for q in range(4):
            wide_copy(q).start()

        @pl.when(right)
        def _():
            for q in range(4):
                front_copy(q).start()

    for s in range(4):
        unpack_child(t, t_pieces[s], lax.rem(me + 4 - s, 4))

    @pl.when(right | lower)
    def _():
        for c in pack_copies:
            c.wait()

    @pl.when(far)
    def _():
        for i in range(4):
            thick_copy(i).wait()

    @pl.when(right)
    def _():
        @pl.when(me == 0)
        def _():
            for q in range(4):
                front_copy(q).wait()
            x[...] = fv[...]

        @pl.when(lower)
        def _():
            copy(a12, a12v, sem_a).wait()
            x[...] = a12v[...].astype(F32)

        for i in range(3):
            ma = maps[i]

            @pl.when(ma < 12)
            def _():
                for b in range(3):
                    slot, here = slot_of(maps[b])

                    @pl.when(here)
                    def _():
                        add(x, ma, slot, t[blk(i), blk(b)])

                @pl.when(far)
                def _():
                    rows = pl.ds(pl.multiple_of(ma * BLK, BLK), BLK)
                    x[rows, :] = x[rows, :] + tv[0, blk(i), :].astype(F32)

        for j in range(PANELS):
            z = x[pan(j), :]
            if j:
                z = z - dot(ups[up_rows(j), :], xb[: j * PANEL, :], 0, 0)

            @pl.when(me == 0)
            def _():
                fv[pan(j), :] = z
                out_copy(j).start()

            if j < PANELS - 1:
                xb[pan(j), :] = dot(inv[j], z.astype(BF16), 1, 0).astype(BF16)

        @pl.when(lower)
        def _():
            last = dot(inv[PANELS - 1], z.astype(BF16), 1, 0)
            xb[pan(PANELS - 1), :] = last.astype(BF16)
            for j in reversed(range(PANELS)):
                v = xb[pan(j), :]
                for i in range(j + 1, PANELS):
                    at = up_rows(i).start + j * PANEL
                    part = dot(ups[at : at + PANEL, :], xb[pan(i), :], 1, 0)
                    v = v.astype(F32) - part
                xb[pan(j), :] = dot(inv[j], v.astype(BF16), 0, 0).astype(BF16)

        @pl.when(me == 0)
        def _():
            for q in range(4):
                out_copy(q).wait()

    @pl.when(lower)
    def _():
        for q in range(4):
            wide_copy(q).wait()

        def rows_step(q, _):
            @pl.when(right)
            def _():
                front_copy(q).wait()

            for i in range(12):
                ma = maps[first + i] - 12 * me

                @pl.when((ma >= 3 * q) & (ma < 3 * q + 3))
                def _():
                    rows = pl.ds(pl.multiple_of((ma - 3 * q) * BLK, BLK), BLK)
                    for b in range(3):
                        mb = maps[b]
                        piece = wv[(i // 3) * 4 + b, blk(i % 3), PANEL : PANEL + BLK]

                        @pl.when(mb < 12)
                        def _():
                            panel = mb // 3
                            cols = pl.ds(pl.multiple_of((mb - panel * 3) * BLK, BLK), BLK)
                            at = 4 * q + panel
                            wv[at, rows, cols] = (wv[at, rows, cols].astype(F32) + piece.astype(F32)).astype(BF16)

                        slot, here = slot_of(mb)

                        @pl.when(right & here)
                        def _():
                            add(fv, ma, slot, piece.astype(F32))

                    @pl.when(far)
                    def _():
                        held = pl.ds(pl.multiple_of(lax.rem(first + i, 4) * BLK, BLK), BLK)
                        to = pl.ds(pl.multiple_of(ma * BLK, BLK), BLK)
                        fv[to, :] = fv[to, :] + tv[(first + i) // 4, held, :].astype(F32)

            @pl.when(right)
            def _():
                rows = [wv[4 * q + k, :, :PANEL] for k in range(PANELS)]
                fv[tile(q), :] = fv[tile(q), :] - dot(jnp.concatenate(rows, axis=1), xb[...], 1, 0)

            for k in range(PANELS):

                @pl.when(col >= k)
                def _():
                    @pl.when(col < PANELS)
                    def _():
                        z = wv[4 * q + k, :, :PANEL]
                        if k:
                            z = (z.astype(F32) - dot(yb[:, : k * PANEL], ups[up_rows(k), :], 1, 0)).astype(BF16)
                        full = dot(z, inv[k], 1, 1)
                        yb[:, pan(k)] = full.astype(BF16)
                        fv[tile(q), :] = full

            out_copy(q).start()
            return 0

        lax.fori_loop(0, 4, rows_step, 0)
        for q in range(4):
            out_copy(q).wait()


def tail_call(info, maps, front, a12, wide, thick, t_pieces, packs, result):
    vm = pl.BlockSpec(memory_space=pltpu.VMEM)
    sm = pl.BlockSpec(memory_space=pltpu.SMEM)
    anywhere = pl.BlockSpec(memory_space=pl.ANY)
    sem = pltpu.SemaphoreType.DMA
    args = [front, a12, wide, *thick, *packs]
    return pl.pallas_call(
        tail_kernel,
        out_shape=jax.ShapeDtypeStruct((LEAD, PANEL), F32),
        in_specs=[sm, sm] + [anywhere] * len(args) + [vm] * 4 + [anywhere],
        out_specs=anywhere,
        scratch_shapes=[
            pltpu.VMEM((PANELS, PANEL, PANEL), BF16),
            pltpu.VMEM((6 * PANEL, PANEL), BF16),
            pltpu.VMEM((LEAD, PANEL), BF16),
            pltpu.VMEM((LEAD, PANEL), F32),
            pltpu.VMEM((LEAD, PANEL), BF16),
            pltpu.VMEM((PANEL, PANEL), F32),
            pltpu.VMEM((N_COL, PANEL, PANEL + BLK), BF16),
            pltpu.VMEM((LEAD, PANEL), F32),
            pltpu.VMEM((4, 4 * BLK, PANEL), BF16),
            pltpu.VMEM((PANEL, LEAD), BF16),
            sem((2 * PANELS,)),
            sem,
            sem((4,)),
            sem((4,)),
            sem((4,)),
            sem((4,)),
        ],
        input_output_aliases={2 + len(args) + 4: 0},
        compiler_params=pltpu.CompilerParams(vmem_limit_bytes=58 * 2**20),
        cost_estimate=pl.CostEstimate(flops=7 * 10**9, bytes_accessed=2 * 10**7, transcendentals=0),
        name="tail",
    )(info, maps, *args, *t_pieces, result)


def per_device(front_init, contribution, maps):
    front = front_init[0]
    index_map = maps[0]
    me = lax.axis_index("row")
    col = lax.axis_index(COL)
    y = lax.axis_index("y")
    grid = ("row", "z", "y")

    def flat(r, c):
        return r * N_COL + c

    def x_from0(value, s, cols):
        return lax.ppermute(value, grid, [(flat(0, c), flat(s, c)) for c in cols])

    def z_from0(value, s):
        return lax.ppermute(value, COL, [(b, 4 * s + b) for b in range(4)])

    def x_shift(value, s):
        return lax.ppermute(value, "row", [(i, (i + s) % 4) for i in range(4)])

    def y_shift(value, s):
        return lax.ppermute(value, COL, [(4 * z + b, 4 * z + (b + s) % 4) for z in range(4) for b in range(4)])

    def x_swap(value, m):
        return lax.ppermute(value, "row", [(i, i ^ m) for i in range(4)])

    def x_pairs(value, pairs, cols):
        return lax.ppermute(value, grid, [(flat(p, c), flat(q, c)) for p, q in pairs for c in cols])

    def shifts(shift, value):
        return [shift(value, s) for s in range(1, 4)]

    z = lax.axis_index("z")
    first = jnp.where(me == 3, 4, 0)
    ids = jnp.full((N_COL, THICK), -1, jnp.int32)
    for c in SOURCES:
        for j, b in enumerate(SOURCES[c]):
            ids = ids.at[c, j].set(b)
    held = jnp.take(ids, col, axis=0)
    targets = jnp.where(held >= 0, jnp.take(index_map, jnp.maximum(held, 0)), -1000)
    info = jnp.concatenate(
        [jnp.stack([me, col, first, y, z, 0, 0, 0]).astype(jnp.int32), targets.astype(jnp.int32), jnp.zeros((3,), jnp.int32)]
    )

    def contribution_column(value, j):
        pairs = [(SOURCES[c][j], c) for c in SOURCES if j < len(SOURCES[c])]
        return lax.ppermute(value, COL, pairs)

    def staged(kernel, outs, args, marks=(), name=None):
        return vmem_call(kernel, outs, info, args, marks, name)

    received = lax.ppermute(contribution[0], "cube", [(0, 1), (1, 0)])
    piece, full = (REST, PANEL), (LEAD, PANEL)
    pieces = staged(pack_kernel, [piece] * 4, [front, received], name="pack")
    got = [x_from0(pieces[s], s, range(4)) for s in range(1, 4)]
    child_one = x_swap(received, 1)
    own, pair, high, lead = staged(
        stage1_kernel,
        [piece, (8 * BLK, BLK), full, full],
        [pieces[0], *got, received, child_one, front],
        name="stage1",
    )
    got = [z_from0(own, s) for s in range(1, 4)]
    pair_got = x_swap(pair, 3)
    a12 = lax.psum(lead, "row")
    own, wide_in = staged(
        stage2_kernel, [piece, (LEAD, PANEL + BLK)], [own, *got, pair, pair_got, high], name="stage2"
    )
    got = shifts(y_shift, own)
    wide_part = lax.psum_scatter(wide_in, "z", tiled=True)
    rows = [DIAG + 3 * PART] + [DIAG + b * PIECE for b in range(1, 4)]
    g0, r1, r2, r3 = staged(stage3_kernel, [(n, PANEL) for n in rows], [own, *got], name="stage3")
    g0 = [g0] + shifts(x_shift, g0)
    r1, received, wide_part = staged(
        copy_kernel, [r1.shape, received.shape, wide_part.shape], [r1, received, wide_part], g0[1:], name="stage4"
    )
    result = jnp.zeros((LEAD, PANEL), F32)
    packs = []
    g1 = [r1] + shifts(x_shift, r1)
    wide = lax.all_gather(wide_part, COL)
    thick = [contribution_column(received, j) for j in range(THICK)]
    pack, result = panel_call(0, info, index_map, g0, [], [], [r1], result)
    packs.append(pack)
    (r2,) = staged(copy_kernel, [r2.shape], [r2], [pack, *g1[1:]], name="stage5")
    g2 = [r2] + shifts(x_shift, r2)
    pack, result = panel_call(1, info, index_map, g1, g0, packs, [r2, a12], result)
    packs.append(pack)
    (r3,) = staged(copy_kernel, [r3.shape], [r3], [pack, *g2[1:]], name="stage6")
    g3 = [r3] + shifts(x_shift, r3)
    pack, result = panel_call(2, info, index_map, g2, g0, packs, [r3], result)
    packs.append(pack)
    (spread,) = staged(spread_kernel, [(4 * BLK, PANEL)], thick, [pack, *g3[1:]], name="spread")
    far = range(min(SOURCES), N_COL)
    spread = [spread] + [x_pairs(spread, [(i, (i + s) % 4) for i in range(4)], far) for s in range(1, 4)]
    pack, result = panel_call(3, info, index_map, g3, g0, packs, [spread[0], wide], result)
    packs.append(pack)
    out = tail_call(info, index_map, front, a12, wide, spread, g0, packs, result)
    return out[None]


def solution(mesh):
    split_mesh = Mesh(mesh.devices.reshape(2, N_ROW, 4, 4), ("cube", "row", "z", "y"))
    return jax.shard_map(
        per_device,
        mesh=split_mesh,
        in_specs=(P("cube", "row", COL), P("cube", "row", COL), P("cube", None)),
        out_specs=P("cube", "row", COL),
        check_vma=False,
    )
```

```python
import functools

import jax
import jax.numpy as jnp
from jax import lax
from jax.experimental import pallas as pl
from jax.experimental.pallas import tpu as pltpu
from jax.sharding import Mesh
from jax.sharding import PartitionSpec as P

BLK = 128
PANEL = 384
PANELS = 4
N_ROW = 4
N_COL = 16
PIECE = PANEL // N_ROW
PART = BLK // N_ROW
DIAG = 4 * PART
LEAD = PANEL * PANELS
COL = ("z", "y")
F32 = jnp.float32
BF16 = jnp.bfloat16

SOURCES = {11: [3, 4, 5], 12: [4, 5, 6, 7, 8], 13: [7, 8, 9, 10, 11], 14: [10, 11, 12, 13, 14], 15: [13, 14, 15]}
THICK = 5


def dot(a, b, ca, cb):
    return lax.dot_general(a, b, (((ca,), (cb,)), ((), ())), preferred_element_type=F32)


def split(x):
    high = x.astype(BF16)
    return high, (x - high.astype(F32)).astype(BF16)


def dot3(a, b, ca, cb):
    ah, al = split(a)
    bh, bl = split(b)
    return dot(jnp.concatenate([ah, ah, al], ca), jnp.concatenate([bh, bl, bh], cb), ca, cb)


def over_rows(x, i):
    return jnp.broadcast_to(x[i : i + 1, :], x.shape)


def over_lanes(x, j):
    return jnp.broadcast_to(x[:, j : j + 1], x.shape)


def factor_block(tiles, group=4):
    sub = lax.broadcasted_iota(jnp.int32, (8, BLK), 0)
    lane = lax.broadcasted_iota(jnp.int32, (8, BLK), 1)
    v = list(tiles)
    inv, upper, scale = [None] * 16, [None] * 16, [None] * 16
    for g in range(0, 16, group):
        for t in range(g, g + group):
            qs = range(t, g + group)
            c = {(q, j): over_lanes(v[q], 8 * t + j) for q in qs for j in range(8)}
            block = (lane >= 8 * t) & (lane < 8 * t + 8)
            sc = jnp.zeros((8, BLK), F32)
            w = {q: jnp.where(block, 0.0, v[q]) for q in qs}
            w[t] = jnp.where(lane - 8 * t == sub, 1.0, w[t])
            u = v[t]
            for i in range(8):
                pivot = over_rows(c[t, i], i)
                r = 1.0 / pivot
                sc = jnp.where(sub == i, lax.rsqrt(pivot), sc)
                m = {q: c[q, i] * r for q in qs}
                m[t] = jnp.where(sub > i, m[t], 0.0)
                for j in range(i + 1, 8):
                    row = over_rows(c[t, j], i)
                    for q in qs:
                        c[q, j] = c[q, j] - m[q] * row
                row = over_rows(w[t], i)
                for q in qs:
                    if q != t or i < 7:
                        w[q] = w[q] - m[q] * row
                if i < 7:
                    u = u - m[t] * over_rows(u, i)
            inv[t], scale[t], upper[t] = w[t], sc, u
            for q in range(t + 1, g + group):
                v[q] = w[q]
        if g + group < 16:
            sg = jnp.concatenate(scale[g : g + group], 0)
            ug = jnp.concatenate(upper[g : g + group], 0) * sg
            done = [
                jnp.where((lane >= 8 * t + 8) & (lane < 8 * g + 8 * group), 0.0, inv[t]) for t in range(g, g + group)
            ]
            wg = jnp.concatenate(done, 0) * sg
            update = dot3(ug, wg, 0, 0)
            block = (lane >= 8 * g) & (lane < 8 * g + 8 * group)
            for q in range(g + group, 16):
                v[q] = jnp.where(block, 0.0, v[q]) - update[8 * q : 8 * q + 8, :]
    return [a * s for a, s in zip(inv, scale)], [a * s for a, s in zip(upper, scale)]


def factor_panel(p, li, ud):
    sub = lax.broadcasted_iota(jnp.int32, (8, BLK), 0)
    lane = lax.broadcasted_iota(jnp.int32, (8, BLK), 1)

    def step(j, _):
        at = pl.multiple_of(j * BLK, BLK)
        inv, upper = factor_block([p[pl.ds(at + 8 * q, 8), pl.ds(at, BLK)] for q in range(16)])
        for q in range(16):
            li[8 * q : 8 * q + 8, :] = jnp.where(lane <= sub + 8 * q, inv[q], 0.0)
            ud[pl.ds(at + 8 * q, 8), :] = jnp.where(lane >= sub + 8 * q, upper[q], 0.0)
        row = dot3(li[...], p[pl.ds(at, BLK), :], 1, 0)
        p[pl.ds(at, BLK), :] = row
        p[pl.ds(at, BLK), pl.ds(at, BLK)] = li[...]
        for k in range(1, 3):

            @pl.when(k > j)
            def _():
                rows = slice(k * BLK, k * BLK + BLK)
                p[rows, pl.ds(at, BLK)] = jnp.zeros((BLK, BLK), F32)
                p[rows, :] = p[rows, :] - dot3(row[:, rows], p[pl.ds(at, BLK), :], 0, 0)

        return 0

    lax.fori_loop(0, 3, step, 0)


def unpack_child(t, piece, x):
    at = x * PIECE
    for b in range(3):
        for u in range(3):
            t[pl.ds(at + PART * u, PART), b * BLK : (b + 1) * BLK] = piece[
                DIAG + PART * b : DIAG + PART * (b + 1), u * BLK : (u + 1) * BLK
            ]


def panel_kernel(k, marks, info, maps, *refs):
    r = list(refs)
    pieces, r = r[0], r[1:]
    if k:
        t, r = r[0], r[1:]
    packs, r = r[:k], r[k:]
    r = r[marks + 1 :]
    pack, result, r = r[0], r[1], r[2:]
    if not k:
        t, r = r[0], r[1:]
    a, p, li, ud, low, sem = r
    me = info[0]
    col = info[1]
    part = pieces.shape[0] // N_ROW
    for x in range(4):
        buf = pieces.at[x * part : (x + 1) * part, :]
        for j in range(k):
            at = j * PANEL + x * PIECE
            a[pl.ds(at, PIECE), :] = buf[DIAG + j * PIECE : DIAG + (j + 1) * PIECE, :].astype(F32)
        at = x * PART
        first = buf[:PART, :].astype(F32) + buf[2 * PART : 3 * PART, :].astype(F32)
        rest = buf[PART : 2 * PART, :].astype(F32) + buf[3 * PART : 4 * PART, :].astype(F32)
        a[pl.ds(k * PANEL + at, PART), :] = first
        a[pl.ds(k * PANEL + BLK + at, PART), BLK:] = rest[:, : 2 * BLK]
        a[pl.ds(k * PANEL + 2 * BLK + at, PART), 2 * BLK :] = rest[:, 2 * BLK :]
        if not k:
            unpack_child(t, buf, x)
    for b in range(3):
        mb = maps[b] - 3 * k
        for i in range(b + 1):
            ma = maps[i]

            @pl.when((mb >= 0) & (mb < 3) & (ma < 3 * (k + 1)))
            def _():
                rows = pl.ds(pl.multiple_of(ma * BLK, BLK), BLK)
                cols = pl.ds(pl.multiple_of(mb * BLK, BLK), BLK)
                a[rows, cols] = a[rows, cols] + t[i * BLK : (i + 1) * BLK, b * BLK : (b + 1) * BLK].astype(F32)

    up = 2 * PANEL
    for j in range(k):
        z = a[j * PANEL : (j + 1) * PANEL, :]
        if j:
            z = z - dot(packs[j][up : up + j * PANEL, :], pack[up : up + j * PANEL, :], 0, 0)
        zh, zl = split(z)
        ih, il = packs[j][:PANEL, :], packs[j][PANEL:up, :]
        uf = dot(ih, zh, 1, 0) + (dot(ih, zl, 1, 0) + dot(il, zh, 1, 0))

        @pl.when((me == 0) & (col == j))
        def _():
            low[...] = uf.T

        pack[up + j * PANEL : up + (j + 1) * PANEL, :] = uf.astype(BF16)
    z = a[k * PANEL : (k + 1) * PANEL, :]
    if k:
        u = pack[up : up + k * PANEL, :]
        z = z - dot(u, u, 0, 0)
    p[...] = z
    factor_panel(p, li, ud)
    for i in range(3):
        ri = slice(i * BLK, (i + 1) * BLK)
        for j in range(3):
            rj = slice(j * BLK, (j + 1) * BLK)
            lo = slice(PANEL + i * BLK, PANEL + (i + 1) * BLK)
            if j <= i:
                pack[ri, rj], pack[lo, rj] = split(p[ri, rj])
            else:
                pack[ri, rj] = jnp.zeros((BLK, BLK), BF16)
                pack[lo, rj] = jnp.zeros((BLK, BLK), BF16)

    @pl.when((me == 0) & (col == k))
    def _():
        for i in range(3):
            ri = slice(i * BLK, (i + 1) * BLK)
            low[ri, ri] = ud[ri, :].T
            for j in range(i + 1, 3):
                rj = slice(j * BLK, (j + 1) * BLK)
                low[ri, rj] = jnp.zeros((BLK, BLK), F32)
                low[rj, ri] = p[ri, rj].T

    @pl.when((me == 0) & (col > k) & (col < PANELS))
    def _():
        low[...] = jnp.zeros((PANEL, PANEL), F32)

    @pl.when((me == 0) & (col < PANELS))
    def _():
        copy = pltpu.make_async_copy(low, result.at[pl.ds(k * PANEL, PANEL), :], sem)
        copy.start()
        copy.wait()


def panel_call(k, info, maps, pieces, t, packs, marks, result):
    vm = pl.BlockSpec(memory_space=pltpu.VMEM)
    sm = pl.BlockSpec(memory_space=pltpu.SMEM)
    anywhere = pl.BlockSpec(memory_space=pl.ANY)
    args = [pieces] + ([t] if k else []) + list(packs)
    sq = (PANEL, PANEL)
    pinned = pl.BlockSpec(memory_space=pltpu.HBM)
    mark_specs = [pinned if m.size > 2**19 else anywhere for m in marks]
    return pl.pallas_call(
        functools.partial(panel_kernel, k, len(marks)),
        out_shape=[
            jax.ShapeDtypeStruct(((2 + k) * PANEL, PANEL), BF16),
            jax.ShapeDtypeStruct((LEAD, PANEL), F32),
        ]
        + ([] if k else [jax.ShapeDtypeStruct(sq, BF16)]),
        in_specs=[sm, sm] + [vm] * len(args) + mark_specs + [pinned],
        out_specs=[vm, pinned] + ([] if k else [vm]),
        scratch_shapes=[
            pltpu.VMEM(((k + 1) * PANEL, PANEL), F32),
            pltpu.VMEM(sq, F32),
            pltpu.VMEM((BLK, BLK), F32),
            pltpu.VMEM((PANEL, BLK), F32),
            pltpu.VMEM(sq, F32),
            pltpu.SemaphoreType.DMA,
        ],
        input_output_aliases={2 + len(args) + len(marks): 1},
        compiler_params=pltpu.CompilerParams(vmem_limit_bytes=24 * 2**20),
        cost_estimate=pl.CostEstimate(flops=10**10, bytes_accessed=10**6, transcendentals=0),
        name=f"panel{k}",
    )(info, maps, *args, *marks, result)


def vmem_call(kernel, outs, scalars, args, marks=(), name=None):
    vm = pl.BlockSpec(memory_space=pltpu.VMEM)
    sm = pl.BlockSpec(memory_space=pltpu.SMEM)
    anywhere = pl.BlockSpec(memory_space=pl.ANY)

    def body(info, *refs):
        kernel(info, refs[: len(args)], refs[len(args) + len(marks) :])

    return pl.pallas_call(
        body,
        out_shape=[jax.ShapeDtypeStruct(shape, BF16) for shape in outs],
        in_specs=[sm] + [vm] * len(args) + [anywhere] * len(marks),
        out_specs=[vm] * len(outs),
        compiler_params=pltpu.CompilerParams(vmem_limit_bytes=24 * 2**20),
        name=name,
    )(scalars, *args, *marks)


REST = DIAG + 3 * PIECE
CHILD = DIAG + 2 * PIECE


def pick(outs, index, refs):
    for i, ref in enumerate(refs):

        @pl.when(index == i)
        def _():
            outs[...] = ref[...]


def pack_kernel(info, ins, outs):
    front, child = ins
    y = info[3]
    at = pl.multiple_of(y * PANEL, PANEL)
    for s, out in enumerate(outs):
        a = front[pl.ds(at + s * PART, PART), :]
        b = front[pl.ds(at + BLK + s * PART, PART), BLK:]
        c = front[pl.ds(at + 2 * BLK + s * PART, PART), 2 * BLK :]
        ah, al = split(a)
        bh, bl = split(b)
        ch, cl = split(c)
        out[:PART, :] = ah
        out[PART : 2 * PART, : 2 * BLK] = bh
        out[PART : 2 * PART, 2 * BLK :] = ch
        out[2 * PART : 3 * PART, :] = al
        out[3 * PART : DIAG, : 2 * BLK] = bl
        out[3 * PART : DIAG, 2 * BLK :] = cl
        for j in range(3):
            o = DIAG + j * PIECE
            out[o : o + PIECE, :] = front[j * PANEL + s * PIECE : j * PANEL + (s + 1) * PIECE, :].astype(BF16)

        @pl.when(y < 3)
        def _():
            for u in range(3):
                rows = s * PIECE + u * PART
                out[CHILD : CHILD + PART, u * BLK : (u + 1) * BLK] = child[rows : rows + PART, :]


def stage1_kernel(info, ins, outs):
    child, child_one, front = ins[4:]
    piece, pair, high, lead = outs
    me = info[0]
    pick(piece, me, ins[:4])
    n = child.shape[0]
    odd = lax.rem(me, 2)

    @pl.when(odd == 0)
    def _():
        pair[:n, :] = child[...]
        pair[n:, :] = child_one[...]

    @pl.when(odd == 1)
    def _():
        pair[:n, :] = child_one[...]
        pair[n:, :] = child[...]

    full = front[...].astype(BF16)
    high[...] = full
    lead[...] = jnp.where(me == 0, full, jnp.zeros((), BF16))


def stage2_kernel(info, ins, outs):
    pair, pair_got, high = ins[4:]
    piece, wide = outs
    me, z, first = info[0], info[4], info[2]
    pick(piece, z, ins[:4])

    @pl.when(z == 0)
    def _():
        wide[:, :PANEL] = high[...]
        n = 4 * BLK

        @pl.when(me < 2)
        def _():
            wide[: 2 * n, PANEL:] = pair[...]
            wide[2 * n :, PANEL:] = pair_got[:n, :]

        @pl.when(me == 2)
        def _():
            wide[: 2 * n, PANEL:] = pair_got[...]
            wide[2 * n :, PANEL:] = pair[:n, :]

        @pl.when(me == 3)
        def _():
            wide[:n, PANEL:] = pair_got[n:, :]
            wide[n:, PANEL:] = pair[...]

    @pl.when(z != 0)
    def _():
        wide[...] = jnp.zeros(wide.shape, BF16)


def stage3_kernel(info, ins, outs):
    g0, r1, r2, r3 = outs
    for s in range(4):
        source = lax.rem(info[3] + 4 - s, 4)
        for b, out in enumerate(outs):

            @pl.when(source == b)
            def _():
                if b == 0:
                    g0[:DIAG, :] = ins[s][:DIAG, :]
                else:
                    out[...] = ins[s][: out.shape[0], :]
                if b < 3:
                    g0[DIAG + b * PART : DIAG + (b + 1) * PART, :] = ins[s][CHILD : CHILD + PART, :]


def copy_kernel(info, ins, outs):
    for a, b in zip(ins, outs):
        b[...] = a[...]


def join_kernel(info, ins, outs):
    joined = outs[0]
    n = ins[0].shape[0]
    for s in range(4):
        x = lax.rem(info[0] + 4 - s, 4)
        joined[pl.ds(pl.multiple_of(x * n, 16), n), :] = ins[s][...]
    copy_kernel(info, ins[4:], outs[1:])


def spread_kernel(info, ins, outs):
    join_kernel(info, ins[:5], outs[:2])
    out = outs[2]
    out[...] = jnp.zeros(out.shape, BF16)
    for j, ref in enumerate(ins[5:]):
        slot = info[8 + j] - 3 * info[1]

        @pl.when((slot >= 0) & (slot < 3))
        def _():
            out[:, pl.ds(pl.multiple_of(slot * BLK, BLK), BLK)] = ref[...]


def tail_kernel(info, maps, front, a12, wide, *refs):
    r = list(refs)
    thick, r = r[:4], r[4:]
    packs, r = r[:PANELS], r[PANELS:]
    t = r[0]
    out, r = r[2], r[3:]
    inv, ups, a12v, x, xb, wv, fv, tv, yb = r[:9]
    sem_p, sem_a, sem_w, sem_f, sem_t, sem_o = r[9:]
    me = info[0]
    col = info[1]
    first = info[2]

    def blk(i):
        return slice(i * BLK, (i + 1) * BLK)

    def pan(i):
        return slice(i * PANEL, (i + 1) * PANEL)

    def tile(q):
        return pl.ds(pl.multiple_of(q * PANEL, PANEL), PANEL)

    def up_rows(j):
        return slice(j * (j - 1) // 2 * PANEL, j * (j + 1) // 2 * PANEL)

    copy = pltpu.make_async_copy
    pack_copies = []
    for j in range(PANELS):
        pack_copies.append(copy(packs[j].at[:PANEL, :], inv.at[j], sem_p.at[2 * j]))
        if j:
            pack_copies.append(copy(packs[j].at[2 * PANEL :, :], ups.at[up_rows(j), :], sem_p.at[2 * j + 1]))

    def wide_copy(q):
        return copy(wide.at[pl.ds(4 * q, 4)], wv.at[pl.ds(4 * q, 4)], sem_w.at[q])

    def front_copy(q):
        return copy(front.at[tile(q), :], fv.at[tile(q), :], sem_f.at[q])

    def out_copy(q):
        return copy(fv.at[tile(q), :], out.at[tile(q), :], sem_o.at[q])

    def slot_of(value):
        slot = value - 3 * col
        return slot, (slot >= 0) & (slot < 3)

    def add(ref, row_block, col_slot, value):
        rows = pl.ds(pl.multiple_of(row_block * BLK, BLK), BLK)
        cols = pl.ds(pl.multiple_of(col_slot * BLK, BLK), BLK)
        ref[rows, cols] = ref[rows, cols] + value

    right = col >= PANELS
    lower = me > 0

    @pl.when(right | lower)
    def _():
        for c in pack_copies:
            c.start()

    @pl.when(right & lower)
    def _():
        copy(a12, a12v, sem_a).start()

    @pl.when(right & (me == 0))
    def _():
        for q in range(4):
            front_copy(q).start()

    far = col >= min(SOURCES)

    def thick_copy(i):
        return copy(thick[i], tv.at[lax.rem(me + 4 - i, 4)], sem_t.at[i])

    @pl.when(far)
    def _():
        for i in range(4):
            thick_copy(i).start()

    @pl.when(lower)
    def _():
        for q in range(4):
            wide_copy(q).start()

        @pl.when(right)
        def _():
            for q in range(4):
                front_copy(q).start()

    @pl.when(right | lower)
    def _():
        for c in pack_copies:
            c.wait()

    @pl.when(far)
    def _():
        for i in range(4):
            thick_copy(i).wait()

    @pl.when(right)
    def _():
        @pl.when(me == 0)
        def _():
            for q in range(4):
                front_copy(q).wait()
            x[...] = fv[...]

        @pl.when(lower)
        def _():
            copy(a12, a12v, sem_a).wait()
            x[...] = a12v[...].astype(F32)

        for i in range(3):
            ma = maps[i]

            @pl.when(ma < 12)
            def _():
                for b in range(3):
                    slot, here = slot_of(maps[b])

                    @pl.when(here)
                    def _():
                        add(x, ma, slot, t[blk(i), blk(b)].astype(F32))

                @pl.when(far)
                def _():
                    rows = pl.ds(pl.multiple_of(ma * BLK, BLK), BLK)
                    x[rows, :] = x[rows, :] + tv[0, blk(i), :].astype(F32)

        for j in range(PANELS):
            z = x[pan(j), :]
            if j:
                z = z - dot(ups[up_rows(j), :], xb[: j * PANEL, :], 0, 0)

            @pl.when(me == 0)
            def _():
                fv[pan(j), :] = z
                out_copy(j).start()

            if j < PANELS - 1:
                xb[pan(j), :] = dot(inv[j], z.astype(BF16), 1, 0).astype(BF16)

        @pl.when(lower)
        def _():
            last = dot(inv[PANELS - 1], z.astype(BF16), 1, 0)
            xb[pan(PANELS - 1), :] = last.astype(BF16)
            for j in reversed(range(PANELS)):
                v = xb[pan(j), :]
                for i in range(j + 1, PANELS):
                    at = up_rows(i).start + j * PANEL
                    part = dot(ups[at : at + PANEL, :], xb[pan(i), :], 1, 0)
                    v = v.astype(F32) - part
                xb[pan(j), :] = dot(inv[j], v.astype(BF16), 0, 0).astype(BF16)

        @pl.when(me == 0)
        def _():
            for q in range(4):
                out_copy(q).wait()

    @pl.when(lower)
    def _():
        for q in range(4):
            wide_copy(q).wait()

        def rows_step(q, _):
            @pl.when(right)
            def _():
                front_copy(q).wait()

            for i in range(12):
                ma = maps[first + i] - 12 * me

                @pl.when((ma >= 3 * q) & (ma < 3 * q + 3))
                def _():
                    rows = pl.ds(pl.multiple_of((ma - 3 * q) * BLK, BLK), BLK)
                    for b in range(3):
                        mb = maps[b]
                        piece = wv[(i // 3) * 4 + b, blk(i % 3), PANEL : PANEL + BLK]

                        @pl.when(mb < 12)
                        def _():
                            panel = mb // 3
                            cols = pl.ds(pl.multiple_of((mb - panel * 3) * BLK, BLK), BLK)
                            at = 4 * q + panel
                            wv[at, rows, cols] = (wv[at, rows, cols].astype(F32) + piece.astype(F32)).astype(BF16)

                        slot, here = slot_of(mb)

                        @pl.when(right & here)
                        def _():
                            add(fv, ma, slot, piece.astype(F32))

                    @pl.when(far)
                    def _():
                        held = pl.ds(pl.multiple_of(lax.rem(first + i, 4) * BLK, BLK), BLK)
                        to = pl.ds(pl.multiple_of(ma * BLK, BLK), BLK)
                        fv[to, :] = fv[to, :] + tv[(first + i) // 4, held, :].astype(F32)

            @pl.when(right)
            def _():
                rows = [wv[4 * q + k, :, :PANEL] for k in range(PANELS)]
                fv[tile(q), :] = fv[tile(q), :] - dot(jnp.concatenate(rows, axis=1), xb[...], 1, 0)

            for k in range(PANELS):

                @pl.when(col >= k)
                def _():
                    @pl.when(col < PANELS)
                    def _():
                        z = wv[4 * q + k, :, :PANEL]
                        if k:
                            z = (z.astype(F32) - dot(yb[:, : k * PANEL], ups[up_rows(k), :], 1, 0)).astype(BF16)
                        full = dot(z, inv[k], 1, 1)
                        yb[:, pan(k)] = full.astype(BF16)
                        fv[tile(q), :] = full

            out_copy(q).start()
            return 0

        lax.fori_loop(0, 4, rows_step, 0)
        for q in range(4):
            out_copy(q).wait()


def tail_call(info, maps, front, a12, wide, thick, t, packs, result):
    vm = pl.BlockSpec(memory_space=pltpu.VMEM)
    sm = pl.BlockSpec(memory_space=pltpu.SMEM)
    anywhere = pl.BlockSpec(memory_space=pl.ANY)
    sem = pltpu.SemaphoreType.DMA
    pinned = pl.BlockSpec(memory_space=pltpu.HBM)
    args = [front, a12, wide, *thick, *packs]
    return pl.pallas_call(
        tail_kernel,
        out_shape=jax.ShapeDtypeStruct((LEAD, PANEL), F32),
        in_specs=[sm, sm] + [pinned] * (len(args) - PANELS) + [anywhere] * PANELS + [vm, pinned],
        out_specs=pinned,
        scratch_shapes=[
            pltpu.VMEM((PANELS, PANEL, PANEL), BF16),
            pltpu.VMEM((6 * PANEL, PANEL), BF16),
            pltpu.VMEM((LEAD, PANEL), BF16),
            pltpu.VMEM((LEAD, PANEL), F32),
            pltpu.VMEM((LEAD, PANEL), BF16),
            pltpu.VMEM((N_COL, PANEL, PANEL + BLK), BF16),
            pltpu.VMEM((LEAD, PANEL), F32),
            pltpu.VMEM((4, 4 * BLK, PANEL), BF16),
            pltpu.VMEM((PANEL, LEAD), BF16),
            sem((2 * PANELS,)),
            sem,
            sem((4,)),
            sem((4,)),
            sem((4,)),
            sem((4,)),
        ],
        input_output_aliases={2 + len(args) + 1: 0},
        compiler_params=pltpu.CompilerParams(vmem_limit_bytes=28 * 2**20),
        cost_estimate=pl.CostEstimate(flops=7 * 10**9, bytes_accessed=2 * 10**7, transcendentals=0),
        name="tail",
    )(info, maps, *args, t, result)


def per_device(front_init, contribution, maps):
    front = front_init[0]
    index_map = maps[0]
    me = lax.axis_index("row")
    col = lax.axis_index(COL)
    y = lax.axis_index("y")
    grid = ("row", "z", "y")

    def flat(r, c):
        return r * N_COL + c

    def x_from0(value, s, cols):
        return lax.ppermute(value, grid, [(flat(0, c), flat(s, c)) for c in cols])

    def z_from0(value, s):
        return lax.ppermute(value, COL, [(b, 4 * s + b) for b in range(4)])

    def x_shift(value, s):
        return lax.ppermute(value, "row", [(i, (i + s) % 4) for i in range(4)])

    def y_shift(value, s):
        return lax.ppermute(value, COL, [(4 * z + b, 4 * z + (b + s) % 4) for z in range(4) for b in range(4)])

    def x_swap(value, m):
        return lax.ppermute(value, "row", [(i, i ^ m) for i in range(4)])

    def x_pairs(value, pairs, cols):
        return lax.ppermute(value, grid, [(flat(p, c), flat(q, c)) for p, q in pairs for c in cols])

    def shifts(shift, value):
        return [shift(value, s) for s in range(1, 4)]

    z = lax.axis_index("z")
    first = jnp.where(me == 3, 4, 0)
    ids = jnp.full((N_COL, THICK), -1, jnp.int32)
    for c in SOURCES:
        for j, b in enumerate(SOURCES[c]):
            ids = ids.at[c, j].set(b)
    held = jnp.take(ids, col, axis=0)
    targets = jnp.where(held >= 0, jnp.take(index_map, jnp.maximum(held, 0)), -1000)
    info = jnp.concatenate(
        [jnp.stack([me, col, first, y, z, 0, 0, 0]).astype(jnp.int32), targets.astype(jnp.int32), jnp.zeros((3,), jnp.int32)]
    )

    def contribution_column(value, j):
        pairs = [(SOURCES[c][j], c) for c in SOURCES if j < len(SOURCES[c])]
        return lax.ppermute(value, COL, pairs)

    def staged(kernel, outs, args, marks=(), name=None):
        return vmem_call(kernel, outs, info, args, marks, name)

    received = lax.ppermute(contribution[0], "cube", [(0, 1), (1, 0)])
    piece, full = (REST, PANEL), (LEAD, PANEL)
    pieces = staged(pack_kernel, [piece] * 4, [front, received], name="pack")
    got = [x_from0(pieces[s], s, range(4)) for s in range(1, 4)]
    child_one = x_swap(received, 1)
    own, pair, high, lead = staged(
        stage1_kernel,
        [piece, (8 * BLK, BLK), full, full],
        [pieces[0], *got, received, child_one, front],
        name="stage1",
    )
    got = [z_from0(own, s) for s in range(1, 4)]
    pair_got = x_swap(pair, 3)
    a12 = lax.psum(lead, "row")
    own, wide_in = staged(
        stage2_kernel, [piece, (LEAD, PANEL + BLK)], [own, *got, pair, pair_got, high], name="stage2"
    )
    got = shifts(y_shift, own)
    wide_part = lax.psum_scatter(wide_in, "z", tiled=True)
    rows = [DIAG + 3 * PART] + [DIAG + b * PIECE for b in range(1, 4)]
    g0, r1, r2, r3 = staged(stage3_kernel, [(n, PANEL) for n in rows], [own, *got], name="stage3")
    g = [g0] + shifts(x_shift, g0)

    def joined(value):
        return (4 * value.shape[0], PANEL)

    g0, r1, received, wide_part = staged(
        join_kernel,
        [joined(g[0]), r1.shape, received.shape, wide_part.shape],
        [*g, r1, received, wide_part],
        name="stage4",
    )
    result = jnp.zeros((LEAD, PANEL), F32)
    packs = []
    g = [r1] + shifts(x_shift, r1)
    wide = lax.all_gather(wide_part, COL)
    thick = [contribution_column(received, j) for j in range(THICK)]
    pack, result, t = panel_call(0, info, index_map, g0, None, [], [r1], result)
    packs.append(pack)
    g1, t, r2 = staged(join_kernel, [joined(g[0]), t.shape, r2.shape], [*g, t, r2], [pack], name="stage5")
    g = [r2] + shifts(x_shift, r2)
    pack, result = panel_call(1, info, index_map, g1, t, packs, [r2, a12[:16, :BLK]], result)
    packs.append(pack)
    g2, t, r3 = staged(join_kernel, [joined(g[0]), t.shape, r3.shape], [*g, t, r3], [pack], name="stage6")
    g = [r3] + shifts(x_shift, r3)
    pack, result = panel_call(2, info, index_map, g2, t, packs, [r3], result)
    packs.append(pack)
    g3, t, spread = staged(
        spread_kernel, [joined(g[0]), t.shape, (4 * BLK, PANEL)], [*g, t, *thick], [pack], name="spread"
    )
    far = range(min(SOURCES), N_COL)
    spread = [spread] + [x_pairs(spread, [(i, (i + s) % 4) for i in range(4)], far) for s in range(1, 4)]
    pack, result = panel_call(3, info, index_map, g3, t, packs, [spread[0], wide[0, :16, :BLK]], result)
    packs.append(pack)
    out = tail_call(info, index_map, front, a12, wide, spread, t, packs, result)
    return out[None]


def solution(mesh):
    split_mesh = Mesh(mesh.devices.reshape(2, N_ROW, 4, 4), ("cube", "row", "z", "y"))
    return jax.shard_map(
        per_device,
        mesh=split_mesh,
        in_specs=(P("cube", "row", COL), P("cube", "row", COL), P("cube", None)),
        out_specs=P("cube", "row", COL),
        check_vma=False,
    )
```

```python
import functools

import jax
import jax.numpy as jnp
from jax import lax
from jax.experimental import pallas as pl
from jax.experimental.pallas import tpu as pltpu
from jax.sharding import Mesh
from jax.sharding import PartitionSpec as P

BLK = 128
PANEL = 384
PANELS = 4
N_ROW = 4
N_COL = 16
PIECE = PANEL // N_ROW
PART = BLK // N_ROW
DIAG = 4 * PART
LEAD = PANEL * PANELS
COL = ("z", "y")
F32 = jnp.float32
BF16 = jnp.bfloat16

SOURCES = {11: [3, 4, 5], 12: [4, 5, 6, 7, 8], 13: [7, 8, 9, 10, 11], 14: [10, 11, 12, 13, 14], 15: [13, 14, 15]}
THICK = 5


def dot(a, b, ca, cb):
    return lax.dot_general(a, b, (((ca,), (cb,)), ((), ())), preferred_element_type=F32)


def split(x):
    high = x.astype(BF16)
    return high, (x - high.astype(F32)).astype(BF16)


def dot3(a, b, ca, cb):
    ah, al = split(a)
    bh, bl = split(b)
    return dot(jnp.concatenate([ah, ah, al], ca), jnp.concatenate([bh, bl, bh], cb), ca, cb)


def over_rows(x, i):
    return jnp.broadcast_to(x[i : i + 1, :], x.shape)


def over_lanes(x, j):
    return jnp.broadcast_to(x[:, j : j + 1], x.shape)


def factor_block(tiles, group=8):
    sub = lax.broadcasted_iota(jnp.int32, (8, BLK), 0)
    lane = lax.broadcasted_iota(jnp.int32, (8, BLK), 1)
    v = list(tiles)
    inv, upper, scale = [None] * 16, [None] * 16, [None] * 16
    for g in range(0, 16, group):
        for t in range(g, g + group):
            qs = range(t, g + group)
            c = {(q, j): over_lanes(v[q], 8 * t + j) for q in qs for j in range(8)}
            block = (lane >= 8 * t) & (lane < 8 * t + 8)
            sc = jnp.zeros((8, BLK), F32)
            w = {q: jnp.where(block, 0.0, v[q]) for q in qs}
            w[t] = jnp.where(lane - 8 * t == sub, 1.0, w[t])
            u = v[t]
            for i in range(0, 8, 2):
                p, o, n = over_rows(c[t, i], i), over_rows(c[t, i], i + 1), over_rows(c[t, i + 1], i + 1)
                r = 1.0 / (p * n - o * o)
                low = o * (1.0 / p)
                sc = jnp.where(sub == i, lax.rsqrt(p), jnp.where(sub == i + 1, lax.rsqrt(n - o * low), sc))
                low = jnp.where(sub == i + 1, low, 0.0)
                m1, m2 = {}, {}
                for q in qs:
                    m1[q] = c[q, i] * n - c[q, i + 1] * o
                    m2[q] = c[q, i + 1] * p - c[q, i] * o
                    if q == t:
                        m1[q] = jnp.where(sub > i + 1, m1[q], 0.0)
                        m2[q] = jnp.where(sub > i + 1, m2[q], 0.0)
                    m1[q] = m1[q] * r
                    m2[q] = m2[q] * r
                for j in range(i + 2, 8):
                    row1, row2 = over_rows(c[t, j], i), over_rows(c[t, j], i + 1)
                    for q in qs:
                        c[q, j] = c[q, j] - (m1[q] * row1 + m2[q] * row2)
                row1, row2 = over_rows(w[t], i), over_rows(w[t], i + 1)
                u1, u2 = over_rows(u, i), over_rows(u, i + 1)
                for q in qs:
                    if q != t:
                        w[q] = w[q] - (m1[q] * row1 + m2[q] * row2)
                w_step, u_step = low * row1, low * u1
                if i < 6:
                    w_step = w_step + (m1[t] * row1 + m2[t] * row2)
                    u_step = u_step + (m1[t] * u1 + m2[t] * u2)
                w[t] = w[t] - w_step
                u = u - u_step
            inv[t], scale[t], upper[t] = w[t], sc, u
            for q in range(t + 1, g + group):
                v[q] = w[q]
        if g + group < 16:
            sg = jnp.concatenate(scale[g : g + group], 0)
            ug = jnp.concatenate(upper[g : g + group], 0) * sg
            done = [
                jnp.where((lane >= 8 * t + 8) & (lane < 8 * g + 8 * group), 0.0, inv[t]) for t in range(g, g + group)
            ]
            wg = jnp.concatenate(done, 0) * sg
            update = dot3(ug, wg, 0, 0)
            block = (lane >= 8 * g) & (lane < 8 * g + 8 * group)
            for q in range(g + group, 16):
                v[q] = jnp.where(block, 0.0, v[q]) - update[8 * q : 8 * q + 8, :]
    return [a * s for a, s in zip(inv, scale)], [a * s for a, s in zip(upper, scale)]


def factor_panel(p, li, ud):
    sub = lax.broadcasted_iota(jnp.int32, (8, BLK), 0)
    lane = lax.broadcasted_iota(jnp.int32, (8, BLK), 1)

    def step(j, _):
        at = pl.multiple_of(j * BLK, BLK)
        inv, upper = factor_block([p[pl.ds(at + 8 * q, 8), pl.ds(at, BLK)] for q in range(16)])
        for q in range(16):
            li[8 * q : 8 * q + 8, :] = jnp.where(lane <= sub + 8 * q, inv[q], 0.0)
            ud[pl.ds(at + 8 * q, 8), :] = jnp.where(lane >= sub + 8 * q, upper[q], 0.0)
        row = dot3(li[...], p[pl.ds(at, BLK), :], 1, 0)
        p[pl.ds(at, BLK), :] = row
        p[pl.ds(at, BLK), pl.ds(at, BLK)] = li[...]
        for k in range(1, 3):

            @pl.when(k > j)
            def _():
                rows = slice(k * BLK, k * BLK + BLK)
                p[rows, pl.ds(at, BLK)] = jnp.zeros((BLK, BLK), F32)
                p[rows, :] = p[rows, :] - dot3(row[:, rows], p[pl.ds(at, BLK), :], 0, 0)

        return 0

    lax.fori_loop(0, 3, step, 0)


def unpack_child(t, piece, x):
    at = x * PIECE
    for b in range(3):
        for u in range(3):
            t[pl.ds(at + PART * u, PART), b * BLK : (b + 1) * BLK] = piece[
                DIAG + PART * b : DIAG + PART * (b + 1), u * BLK : (u + 1) * BLK
            ]


def panel_kernel(k, marks, info, maps, *refs):
    r = list(refs)
    pieces, r = r[0], r[1:]
    if k:
        t, r = r[0], r[1:]
    packs, r = r[:k], r[k:]
    r = r[marks + (1 if k else 0) :]
    pack, result, r = r[0], r[1], r[2:]
    if not k:
        t, r = r[0], r[1:]
    a, p, li, ud, low, sem = r
    me = info[0]
    col = info[1]
    part = pieces.shape[0] // N_ROW
    for x in range(4):
        buf = pieces.at[x * part : (x + 1) * part, :]
        for j in range(k):
            at = j * PANEL + x * PIECE
            a[pl.ds(at, PIECE), :] = buf[DIAG + j * PIECE : DIAG + (j + 1) * PIECE, :].astype(F32)
        at = x * PART
        first = buf[:PART, :].astype(F32) + buf[2 * PART : 3 * PART, :].astype(F32)
        rest = buf[PART : 2 * PART, :].astype(F32) + buf[3 * PART : 4 * PART, :].astype(F32)
        a[pl.ds(k * PANEL + at, PART), :] = first
        a[pl.ds(k * PANEL + BLK + at, PART), BLK:] = rest[:, : 2 * BLK]
        a[pl.ds(k * PANEL + 2 * BLK + at, PART), 2 * BLK :] = rest[:, 2 * BLK :]
        if not k:
            unpack_child(t, buf, x)
    for b in range(3):
        mb = maps[b] - 3 * k
        for i in range(b + 1):
            ma = maps[i]

            @pl.when((mb >= 0) & (mb < 3) & (ma < 3 * (k + 1)))
            def _():
                rows = pl.ds(pl.multiple_of(ma * BLK, BLK), BLK)
                cols = pl.ds(pl.multiple_of(mb * BLK, BLK), BLK)
                a[rows, cols] = a[rows, cols] + t[i * BLK : (i + 1) * BLK, b * BLK : (b + 1) * BLK].astype(F32)

    up = 2 * PANEL
    for j in range(k):
        z = a[j * PANEL : (j + 1) * PANEL, :]
        if j:
            z = z - dot(packs[j][up : up + j * PANEL, :], pack[up : up + j * PANEL, :], 0, 0)
        zh, zl = split(z)
        ih, il = packs[j][:PANEL, :], packs[j][PANEL:up, :]
        uf = dot(ih, zh, 1, 0) + (dot(ih, zl, 1, 0) + dot(il, zh, 1, 0))

        @pl.when((me == 0) & (col == j))
        def _():
            low[...] = uf.T

        pack[up + j * PANEL : up + (j + 1) * PANEL, :] = uf.astype(BF16)
    z = a[k * PANEL : (k + 1) * PANEL, :]
    if k:
        u = pack[up : up + k * PANEL, :]
        z = z - dot(u, u, 0, 0)
    p[...] = z
    factor_panel(p, li, ud)
    for i in range(3):
        ri = slice(i * BLK, (i + 1) * BLK)
        for j in range(3):
            rj = slice(j * BLK, (j + 1) * BLK)
            lo = slice(PANEL + i * BLK, PANEL + (i + 1) * BLK)
            if j <= i:
                pack[ri, rj], pack[lo, rj] = split(p[ri, rj])
            else:
                pack[ri, rj] = jnp.zeros((BLK, BLK), BF16)
                pack[lo, rj] = jnp.zeros((BLK, BLK), BF16)

    @pl.when((me == 0) & (col == k))
    def _():
        for i in range(3):
            ri = slice(i * BLK, (i + 1) * BLK)
            low[ri, ri] = ud[ri, :].T
            for j in range(i + 1, 3):
                rj = slice(j * BLK, (j + 1) * BLK)
                low[ri, rj] = jnp.zeros((BLK, BLK), F32)
                low[rj, ri] = p[ri, rj].T

    @pl.when((me == 0) & (col > k) & (col < PANELS))
    def _():
        low[...] = jnp.zeros((PANEL, PANEL), F32)

    @pl.when((me == 0) & (col < PANELS))
    def _():
        copy = pltpu.make_async_copy(low, result.at[pl.ds(k * PANEL, PANEL), :], sem)
        copy.start()
        copy.wait()


def panel_call(k, info, maps, pieces, t, packs, marks, result):
    vm = pl.BlockSpec(memory_space=pltpu.VMEM)
    sm = pl.BlockSpec(memory_space=pltpu.SMEM)
    anywhere = pl.BlockSpec(memory_space=pl.ANY)
    args = [pieces] + ([t] if k else []) + list(packs)
    sq = (PANEL, PANEL)
    pinned = pl.BlockSpec(memory_space=pltpu.HBM)
    mark_specs = [pinned if m.size > 2**19 else anywhere for m in marks]
    return pl.pallas_call(
        functools.partial(panel_kernel, k, len(marks)),
        out_shape=[
            jax.ShapeDtypeStruct(((2 + k) * PANEL, PANEL), BF16),
            jax.ShapeDtypeStruct((LEAD, PANEL), F32),
        ]
        + ([] if k else [jax.ShapeDtypeStruct(sq, BF16)]),
        in_specs=[sm, sm] + [vm] * len(args) + mark_specs + ([pinned] if k else []),
        out_specs=[vm, pinned] + ([] if k else [vm]),
        scratch_shapes=[
            pltpu.VMEM(((k + 1) * PANEL, PANEL), F32),
            pltpu.VMEM(sq, F32),
            pltpu.VMEM((BLK, BLK), F32),
            pltpu.VMEM((PANEL, BLK), F32),
            pltpu.VMEM(sq, F32),
            pltpu.SemaphoreType.DMA,
        ],
        input_output_aliases={2 + len(args) + len(marks): 1} if k else {},
        compiler_params=pltpu.CompilerParams(vmem_limit_bytes=24 * 2**20),
        cost_estimate=pl.CostEstimate(flops=10**10, bytes_accessed=10**6, transcendentals=0),
        name=f"panel{k}",
    )(info, maps, *args, *marks, *([result] if k else []))


def vmem_call(kernel, outs, scalars, args, marks=(), name=None):
    vm = pl.BlockSpec(memory_space=pltpu.VMEM)
    sm = pl.BlockSpec(memory_space=pltpu.SMEM)
    anywhere = pl.BlockSpec(memory_space=pl.ANY)

    def body(info, *refs):
        kernel(info, refs[: len(args)], refs[len(args) + len(marks) :])

    return pl.pallas_call(
        body,
        out_shape=[jax.ShapeDtypeStruct(shape, BF16) for shape in outs],
        in_specs=[sm] + [vm] * len(args) + [anywhere] * len(marks),
        out_specs=[vm] * len(outs),
        compiler_params=pltpu.CompilerParams(vmem_limit_bytes=24 * 2**20),
        name=name,
    )(scalars, *args, *marks)


REST = DIAG + 3 * PIECE
CHILD = DIAG + 2 * PIECE


def pick(outs, index, refs):
    for i, ref in enumerate(refs):

        @pl.when(index == i)
        def _():
            outs[...] = ref[...]


def pack_kernel(info, ins, outs):
    front, child = ins
    y = info[3]
    at = pl.multiple_of(y * PANEL, PANEL)
    for s, out in enumerate(outs):
        a = front[pl.ds(at + s * PART, PART), :]
        b = front[pl.ds(at + BLK + s * PART, PART), BLK:]
        c = front[pl.ds(at + 2 * BLK + s * PART, PART), 2 * BLK :]
        ah, al = split(a)
        bh, bl = split(b)
        ch, cl = split(c)
        out[:PART, :] = ah
        out[PART : 2 * PART, : 2 * BLK] = bh
        out[PART : 2 * PART, 2 * BLK :] = ch
        out[2 * PART : 3 * PART, :] = al
        out[3 * PART : DIAG, : 2 * BLK] = bl
        out[3 * PART : DIAG, 2 * BLK :] = cl
        for j in range(3):
            o = DIAG + j * PIECE
            out[o : o + PIECE, :] = front[j * PANEL + s * PIECE : j * PANEL + (s + 1) * PIECE, :].astype(BF16)

        @pl.when(y < 3)
        def _():
            for u in range(3):
                rows = s * PIECE + u * PART
                out[CHILD : CHILD + PART, u * BLK : (u + 1) * BLK] = child[rows : rows + PART, :]


def stage1_kernel(info, ins, outs):
    child, child_one, front = ins[4:]
    piece, pair, high, lead = outs
    me = info[0]
    pick(piece, me, ins[:4])
    n = child.shape[0]
    odd = lax.rem(me, 2)

    @pl.when(odd == 0)
    def _():
        pair[:n, :] = child[...]
        pair[n:, :] = child_one[...]

    @pl.when(odd == 1)
    def _():
        pair[:n, :] = child_one[...]
        pair[n:, :] = child[...]

    full = front[...].astype(BF16)
    high[...] = full
    lead[...] = jnp.where(me == 0, full, jnp.zeros((), BF16))


def stage2_kernel(info, ins, outs):
    pair, pair_got, high, child = ins[4:]
    piece, wide, child_out = outs
    child_out[...] = child[...]
    me, z, first = info[0], info[4], info[2]
    pick(piece, z, ins[:4])

    @pl.when(z == 0)
    def _():
        wide[:, :PANEL] = high[...]
        n = 4 * BLK

        @pl.when(me < 2)
        def _():
            wide[: 2 * n, PANEL:] = pair[...]
            wide[2 * n :, PANEL:] = pair_got[:n, :]

        @pl.when(me == 2)
        def _():
            wide[: 2 * n, PANEL:] = pair_got[...]
            wide[2 * n :, PANEL:] = pair[:n, :]

        @pl.when(me == 3)
        def _():
            wide[:n, PANEL:] = pair_got[n:, :]
            wide[n:, PANEL:] = pair[...]

    @pl.when(z != 0)
    def _():
        wide[...] = jnp.zeros(wide.shape, BF16)


def stage3_kernel(info, ins, outs):
    g0, r1, r2, r3, child = outs
    child[...] = ins[4][...]
    for s in range(4):
        source = lax.rem(info[3] + 4 - s, 4)
        for b, out in enumerate(outs[:4]):

            @pl.when(source == b)
            def _():
                if b == 0:
                    g0[:DIAG, :] = ins[s][:DIAG, :]
                else:
                    out[...] = ins[s][: out.shape[0], :]
                if b < 3:
                    g0[DIAG + b * PART : DIAG + (b + 1) * PART, :] = ins[s][CHILD : CHILD + PART, :]


def copy_kernel(info, ins, outs):
    for a, b in zip(ins, outs):
        b[...] = a[...]


def join_kernel(info, ins, outs):
    joined = outs[0]
    n = ins[0].shape[0]
    for s in range(4):
        x = lax.rem(info[0] + 4 - s, 4)
        joined[pl.ds(pl.multiple_of(x * n, 16), n), :] = ins[s][...]
    copy_kernel(info, ins[4:], outs[1:])


def place_kernel(kernel, js, begun, info, ins, outs):
    n = len(js)
    out = outs[-1]
    if begun:
        out[...] = ins[-n - 1][...]
    else:
        out[...] = jnp.zeros(out.shape, BF16)
    kernel(info, ins[: -n - (1 if begun else 0)], outs[:-1])
    for j, ref in zip(js, ins[-n:]):
        slot = info[8 + j] - 3 * info[1]

        @pl.when((slot >= 0) & (slot < 3))
        def _():
            out[:, pl.ds(pl.multiple_of(slot * BLK, BLK), BLK)] = ref[...]


def tail_kernel(info, maps, front, a12, wide, *refs):
    r = list(refs)
    thick, r = r[:4], r[4:]
    packs, r = r[:PANELS], r[PANELS:]
    t = r[0]
    out, r = r[2], r[3:]
    inv, ups, a12v, x, xb, wv, fv, tv, yb = r[:9]
    sem_p, sem_a, sem_w, sem_f, sem_t, sem_o = r[9:]
    me = info[0]
    col = info[1]
    first = info[2]

    def blk(i):
        return slice(i * BLK, (i + 1) * BLK)

    def pan(i):
        return slice(i * PANEL, (i + 1) * PANEL)

    def tile(q):
        return pl.ds(pl.multiple_of(q * PANEL, PANEL), PANEL)

    def up_rows(j):
        return slice(j * (j - 1) // 2 * PANEL, j * (j + 1) // 2 * PANEL)

    copy = pltpu.make_async_copy
    pack_copies = []
    for j in range(PANELS):
        pack_copies.append(copy(packs[j].at[:PANEL, :], inv.at[j], sem_p.at[2 * j]))
        if j:
            pack_copies.append(copy(packs[j].at[2 * PANEL :, :], ups.at[up_rows(j), :], sem_p.at[2 * j + 1]))

    def wide_copy(q):
        return copy(wide.at[pl.ds(4 * q, 4)], wv.at[pl.ds(4 * q, 4)], sem_w.at[q])

    def front_copy(q):
        return copy(front.at[tile(q), :], fv.at[tile(q), :], sem_f.at[q])

    def out_copy(q):
        return copy(fv.at[tile(q), :], out.at[tile(q), :], sem_o.at[q])

    def slot_of(value):
        slot = value - 3 * col
        return slot, (slot >= 0) & (slot < 3)

    def add(ref, row_block, col_slot, value):
        rows = pl.ds(pl.multiple_of(row_block * BLK, BLK), BLK)
        cols = pl.ds(pl.multiple_of(col_slot * BLK, BLK), BLK)
        ref[rows, cols] = ref[rows, cols] + value

    right = col >= PANELS
    lower = me > 0

    @pl.when(right | lower)
    def _():
        for c in pack_copies:
            c.start()

    @pl.when(right & lower)
    def _():
        copy(a12, a12v, sem_a).start()

    @pl.when(right & (me == 0))
    def _():
        for q in range(4):
            front_copy(q).start()

    far = col >= min(SOURCES)

    def thick_copy(i):
        return copy(thick[i], tv.at[lax.rem(me + 4 - i, 4)], sem_t.at[i])

    @pl.when(far)
    def _():
        for i in range(4):
            thick_copy(i).start()

    @pl.when(lower)
    def _():
        for q in range(4):
            wide_copy(q).start()

        @pl.when(right)
        def _():
            for q in range(4):
                front_copy(q).start()

    @pl.when(right | lower)
    def _():
        for c in pack_copies:
            c.wait()

    @pl.when(far)
    def _():
        for i in range(4):
            thick_copy(i).wait()

    @pl.when(right)
    def _():
        @pl.when(me == 0)
        def _():
            for q in range(4):
                front_copy(q).wait()
            x[...] = fv[...]

        @pl.when(lower)
        def _():
            copy(a12, a12v, sem_a).wait()
            x[...] = a12v[...].astype(F32)

        for i in range(3):
            ma = maps[i]

            @pl.when(ma < 12)
            def _():
                for b in range(3):
                    slot, here = slot_of(maps[b])

                    @pl.when(here)
                    def _():
                        add(x, ma, slot, t[blk(i), blk(b)].astype(F32))

                @pl.when(far)
                def _():
                    rows = pl.ds(pl.multiple_of(ma * BLK, BLK), BLK)
                    x[rows, :] = x[rows, :] + tv[0, blk(i), :].astype(F32)

        for j in range(PANELS):
            z = x[pan(j), :]
            if j:
                z = z - dot(ups[up_rows(j), :], xb[: j * PANEL, :], 0, 0)

            @pl.when(me == 0)
            def _():
                fv[pan(j), :] = z
                out_copy(j).start()

            if j < PANELS - 1:
                xb[pan(j), :] = dot(inv[j], z.astype(BF16), 1, 0).astype(BF16)

        @pl.when(lower)
        def _():
            last = dot(inv[PANELS - 1], z.astype(BF16), 1, 0)
            xb[pan(PANELS - 1), :] = last.astype(BF16)
            for j in reversed(range(PANELS)):
                v = xb[pan(j), :]
                for i in range(j + 1, PANELS):
                    at = up_rows(i).start + j * PANEL
                    part = dot(ups[at : at + PANEL, :], xb[pan(i), :], 1, 0)
                    v = v.astype(F32) - part
                xb[pan(j), :] = dot(inv[j], v.astype(BF16), 0, 0).astype(BF16)

        @pl.when(me == 0)
        def _():
            for q in range(4):
                out_copy(q).wait()

    @pl.when(lower)
    def _():
        for q in range(4):
            wide_copy(q).wait()

        def rows_step(q, _):
            @pl.when(right)
            def _():
                front_copy(q).wait()

            for i in range(12):
                ma = maps[first + i] - 12 * me

                @pl.when((ma >= 3 * q) & (ma < 3 * q + 3))
                def _():
                    rows = pl.ds(pl.multiple_of((ma - 3 * q) * BLK, BLK), BLK)
                    for b in range(3):
                        mb = maps[b]
                        piece = wv[(i // 3) * 4 + b, blk(i % 3), PANEL : PANEL + BLK]

                        @pl.when(mb < 12)
                        def _():
                            panel = mb // 3
                            cols = pl.ds(pl.multiple_of((mb - panel * 3) * BLK, BLK), BLK)
                            at = 4 * q + panel
                            wv[at, rows, cols] = (wv[at, rows, cols].astype(F32) + piece.astype(F32)).astype(BF16)

                        slot, here = slot_of(mb)

                        @pl.when(right & here)
                        def _():
                            add(fv, ma, slot, piece.astype(F32))

                    @pl.when(far)
                    def _():
                        held = pl.ds(pl.multiple_of(lax.rem(first + i, 4) * BLK, BLK), BLK)
                        to = pl.ds(pl.multiple_of(ma * BLK, BLK), BLK)
                        fv[to, :] = fv[to, :] + tv[(first + i) // 4, held, :].astype(F32)

            @pl.when(right)
            def _():
                rows = [wv[4 * q + k, :, :PANEL] for k in range(PANELS)]
                fv[tile(q), :] = fv[tile(q), :] - dot(jnp.concatenate(rows, axis=1), xb[...], 1, 0)

            for k in range(PANELS):

                @pl.when(col >= k)
                def _():
                    @pl.when(col < PANELS)
                    def _():
                        z = wv[4 * q + k, :, :PANEL]
                        if k:
                            z = (z.astype(F32) - dot(yb[:, : k * PANEL], ups[up_rows(k), :], 1, 0)).astype(BF16)
                        full = dot(z, inv[k], 1, 1)
                        yb[:, pan(k)] = full.astype(BF16)
                        fv[tile(q), :] = full

            out_copy(q).start()
            return 0

        lax.fori_loop(0, 4, rows_step, 0)
        for q in range(4):
            out_copy(q).wait()


def tail_call(info, maps, front, a12, wide, thick, t, packs, result):
    vm = pl.BlockSpec(memory_space=pltpu.VMEM)
    sm = pl.BlockSpec(memory_space=pltpu.SMEM)
    anywhere = pl.BlockSpec(memory_space=pl.ANY)
    sem = pltpu.SemaphoreType.DMA
    pinned = pl.BlockSpec(memory_space=pltpu.HBM)
    args = [front, a12, wide, *thick, *packs]
    return pl.pallas_call(
        tail_kernel,
        out_shape=jax.ShapeDtypeStruct((LEAD, PANEL), F32),
        in_specs=[sm, sm] + [pinned] * (len(args) - PANELS) + [anywhere] * PANELS + [vm, pinned],
        out_specs=pinned,
        scratch_shapes=[
            pltpu.VMEM((PANELS, PANEL, PANEL), BF16),
            pltpu.VMEM((6 * PANEL, PANEL), BF16),
            pltpu.VMEM((LEAD, PANEL), BF16),
            pltpu.VMEM((LEAD, PANEL), F32),
            pltpu.VMEM((LEAD, PANEL), BF16),
            pltpu.VMEM((N_COL, PANEL, PANEL + BLK), BF16),
            pltpu.VMEM((LEAD, PANEL), F32),
            pltpu.VMEM((4, 4 * BLK, PANEL), BF16),
            pltpu.VMEM((PANEL, LEAD), BF16),
            sem((2 * PANELS,)),
            sem,
            sem((4,)),
            sem((4,)),
            sem((4,)),
            sem((4,)),
        ],
        input_output_aliases={2 + len(args) + 1: 0},
        compiler_params=pltpu.CompilerParams(vmem_limit_bytes=28 * 2**20),
        cost_estimate=pl.CostEstimate(flops=7 * 10**9, bytes_accessed=2 * 10**7, transcendentals=0),
        name="tail",
    )(info, maps, *args, t, result)


def per_device(front_init, contribution, maps):
    front = front_init[0]
    index_map = maps[0]
    me = lax.axis_index("row")
    col = lax.axis_index(COL)
    y = lax.axis_index("y")
    grid = ("row", "z", "y")

    def flat(r, c):
        return r * N_COL + c

    def x_from0(value, s, cols):
        return lax.ppermute(value, grid, [(flat(0, c), flat(s, c)) for c in cols])

    def z_from0(value, s):
        return lax.ppermute(value, COL, [(b, 4 * s + b) for b in range(4)])

    def x_shift(value, s):
        return lax.ppermute(value, "row", [(i, (i + s) % 4) for i in range(4)])

    def y_shift(value, s):
        return lax.ppermute(value, COL, [(4 * z + b, 4 * z + (b + s) % 4) for z in range(4) for b in range(4)])

    def x_swap(value, m):
        return lax.ppermute(value, "row", [(i, i ^ m) for i in range(4)])

    def x_pairs(value, pairs, cols):
        return lax.ppermute(value, grid, [(flat(p, c), flat(q, c)) for p, q in pairs for c in cols])

    def shifts(shift, value):
        return [shift(value, s) for s in range(1, 4)]

    z = lax.axis_index("z")
    first = jnp.where(me == 3, 4, 0)
    ids = jnp.full((N_COL, THICK), -1, jnp.int32)
    for c in SOURCES:
        for j, b in enumerate(SOURCES[c]):
            ids = ids.at[c, j].set(b)
    held = jnp.take(ids, col, axis=0)
    targets = jnp.where(held >= 0, jnp.take(index_map, jnp.maximum(held, 0)), -1000)
    info = jnp.concatenate(
        [jnp.stack([me, col, first, y, z, 0, 0, 0]).astype(jnp.int32), targets.astype(jnp.int32), jnp.zeros((3,), jnp.int32)]
    )

    def contribution_column(value, j):
        pairs = [(SOURCES[c][j], c) for c in SOURCES if j < len(SOURCES[c])]
        return lax.ppermute(value, COL, pairs)

    def staged(kernel, outs, args, marks=(), name=None):
        return vmem_call(kernel, outs, info, args, marks, name)

    received = lax.ppermute(contribution[0], "cube", [(0, 1), (1, 0)])
    piece, full = (REST, PANEL), (LEAD, PANEL)
    pieces = staged(pack_kernel, [piece] * 4, [front, received], name="pack")
    got = [x_from0(pieces[s], s, range(4)) for s in range(1, 4)]
    child_one = x_swap(received, 1)
    own, pair, high, lead = staged(
        stage1_kernel,
        [piece, (8 * BLK, BLK), full, full],
        [pieces[0], *got, received, child_one, front],
        name="stage1",
    )
    got = [z_from0(own, s) for s in range(1, 4)]
    pair_got = x_swap(pair, 3)
    a12 = lax.psum(lead, "row")
    thick = contribution_column(received, 0)
    own, wide_in, received, spread = staged(
        functools.partial(place_kernel, stage2_kernel, (0,), False),
        [piece, (LEAD, PANEL + BLK), received.shape, (4 * BLK, PANEL)],
        [own, *got, pair, pair_got, high, received, thick],
        name="stage2",
    )
    got = shifts(y_shift, own)
    wide_part = lax.psum_scatter(wide_in, "z", tiled=True)
    thick = [contribution_column(received, j) for j in (1, 2)]
    rows = [DIAG + 3 * PART] + [DIAG + b * PIECE for b in range(1, 4)]
    g0, r1, r2, r3, received, spread = staged(
        functools.partial(place_kernel, stage3_kernel, (1, 2), True),
        [(n, PANEL) for n in rows] + [received.shape, spread.shape],
        [own, *got, received, spread, *thick],
        name="stage3",
    )
    g = [g0] + shifts(x_shift, g0)
    thick = [contribution_column(received, j) for j in (3, 4)]

    def joined(value):
        return (4 * value.shape[0], PANEL)

    g0, r1, wide_part, spread = staged(
        functools.partial(place_kernel, join_kernel, (3, 4), True),
        [joined(g[0]), r1.shape, wide_part.shape, spread.shape],
        [*g, r1, wide_part, spread, *thick],
        name="stage4",
    )
    packs = []
    g = [r1] + shifts(x_shift, r1)
    wide = lax.all_gather(wide_part, COL)
    pack, result, t = panel_call(0, info, index_map, g0, None, [], [r1], None)
    packs.append(pack)
    g1, t, r2 = staged(join_kernel, [joined(g[0]), t.shape, r2.shape], [*g, t, r2], [pack], name="stage5")
    g = [r2] + shifts(x_shift, r2)
    pack, result = panel_call(1, info, index_map, g1, t, packs, [r2], result)
    packs.append(pack)
    g2, t, r3 = staged(join_kernel, [joined(g[0]), t.shape, r3.shape], [*g, t, r3], [pack], name="stage6")
    g = [r3] + shifts(x_shift, r3)
    pack, result = panel_call(2, info, index_map, g2, t, packs, [r3, a12], result)
    packs.append(pack)
    g3, t, spread = staged(
        join_kernel, [joined(g[0]), t.shape, spread.shape], [*g, t, spread], [pack], name="stage7"
    )
    far = range(min(SOURCES), N_COL)
    spread = [spread] + [x_pairs(spread, [(i, (i + s) % 4) for i in range(4)], far) for s in range(1, 4)]
    pack, result = panel_call(3, info, index_map, g3, t, packs, [spread[0], wide[0, :16, :BLK]], result)
    packs.append(pack)
    out = tail_call(info, index_map, front, a12, wide, spread, t, packs, result)
    return out[None]


def solution(mesh):
    split_mesh = Mesh(mesh.devices.reshape(2, N_ROW, 4, 4), ("cube", "row", "z", "y"))
    return jax.shard_map(
        per_device,
        mesh=split_mesh,
        in_specs=(P("cube", "row", COL), P("cube", "row", COL), P("cube", None)),
        out_specs=P("cube", "row", COL),
        check_vma=False,
    )
```

```python
import functools

import jax
import jax.numpy as jnp
from jax import lax
from jax.experimental import pallas as pl
from jax.experimental.pallas import tpu as pltpu
from jax.sharding import Mesh
from jax.sharding import PartitionSpec as P

BLK = 128
PANEL = 384
PANELS = 4
N_ROW = 4
N_COL = 16
PIECE = PANEL // N_ROW
PART = BLK // N_ROW
DIAG = 4 * PART
LEAD = PANEL * PANELS
COL = ("z", "y")
F32 = jnp.float32
BF16 = jnp.bfloat16

SOURCES = {11: [3, 4, 5], 12: [4, 5, 6, 7, 8], 13: [7, 8, 9, 10, 11], 14: [10, 11, 12, 13, 14], 15: [13, 14, 15]}
THICK = 5


def dot(a, b, ca, cb):
    return lax.dot_general(a, b, (((ca,), (cb,)), ((), ())), preferred_element_type=F32)


def split(x):
    high = x.astype(BF16)
    return high, (x - high.astype(F32)).astype(BF16)


def dot3(a, b, ca, cb):
    ah, al = split(a)
    bh, bl = split(b)
    return dot(jnp.concatenate([ah, ah, al], ca), jnp.concatenate([bh, bl, bh], cb), ca, cb)


def over_rows(x, i):
    return jnp.broadcast_to(x[i : i + 1, :], x.shape)


def over_lanes(x, j):
    return jnp.broadcast_to(x[:, j : j + 1], x.shape)


def factor_block(tiles, group=8):
    sub = lax.broadcasted_iota(jnp.int32, (8, BLK), 0)
    lane = lax.broadcasted_iota(jnp.int32, (8, BLK), 1)
    v = list(tiles)
    inv, upper, scale = [None] * 16, [None] * 16, [None] * 16
    for g in range(0, 16, group):
        for t in range(g, g + group):
            qs = range(t, g + group)
            c = {(q, j): over_lanes(v[q], 8 * t + j) for q in qs for j in range(8)}
            block = (lane >= 8 * t) & (lane < 8 * t + 8)
            sc = jnp.zeros((8, BLK), F32)
            w = {q: jnp.where(block, 0.0, v[q]) for q in qs}
            w[t] = jnp.where(lane - 8 * t == sub, 1.0, w[t])
            u = v[t]
            for i in range(0, 8, 2):
                p, o, n = over_rows(c[t, i], i), over_rows(c[t, i], i + 1), over_rows(c[t, i + 1], i + 1)
                r = 1.0 / (p * n - o * o)
                low = o * (1.0 / p)
                sc = jnp.where(sub == i, lax.rsqrt(p), jnp.where(sub == i + 1, lax.rsqrt(n - o * low), sc))
                low = jnp.where(sub == i + 1, low, 0.0)
                m1, m2 = {}, {}
                for q in qs:
                    m1[q] = c[q, i] * n - c[q, i + 1] * o
                    m2[q] = c[q, i + 1] * p - c[q, i] * o
                    if q == t:
                        m1[q] = jnp.where(sub > i + 1, m1[q], 0.0)
                        m2[q] = jnp.where(sub > i + 1, m2[q], 0.0)
                    m1[q] = m1[q] * r
                    m2[q] = m2[q] * r
                for j in range(i + 2, 8):
                    row1, row2 = over_rows(c[t, j], i), over_rows(c[t, j], i + 1)
                    for q in qs:
                        c[q, j] = c[q, j] - (m1[q] * row1 + m2[q] * row2)
                row1, row2 = over_rows(w[t], i), over_rows(w[t], i + 1)
                u1, u2 = over_rows(u, i), over_rows(u, i + 1)
                for q in qs:
                    if q != t:
                        w[q] = w[q] - (m1[q] * row1 + m2[q] * row2)
                w_step, u_step = low * row1, low * u1
                if i < 6:
                    w_step = w_step + (m1[t] * row1 + m2[t] * row2)
                    u_step = u_step + (m1[t] * u1 + m2[t] * u2)
                w[t] = w[t] - w_step
                u = u - u_step
            inv[t], scale[t], upper[t] = w[t], sc, u
            for q in range(t + 1, g + group):
                v[q] = w[q]
        if g + group < 16:
            sg = jnp.concatenate(scale[g : g + group], 0)
            ug = jnp.concatenate(upper[g : g + group], 0) * sg
            done = [
                jnp.where((lane >= 8 * t + 8) & (lane < 8 * g + 8 * group), 0.0, inv[t]) for t in range(g, g + group)
            ]
            wg = jnp.concatenate(done, 0) * sg
            update = dot3(ug, wg, 0, 0)
            block = (lane >= 8 * g) & (lane < 8 * g + 8 * group)
            for q in range(g + group, 16):
                v[q] = jnp.where(block, 0.0, v[q]) - update[8 * q : 8 * q + 8, :]
    return [a * s for a, s in zip(inv, scale)], [a * s for a, s in zip(upper, scale)]


def factor_panel(p, li, ud):
    sub = lax.broadcasted_iota(jnp.int32, (8, BLK), 0)
    lane = lax.broadcasted_iota(jnp.int32, (8, BLK), 1)

    def step(j, _):
        at = pl.multiple_of(j * BLK, BLK)
        inv, upper = factor_block([p[pl.ds(at + 8 * q, 8), pl.ds(at, BLK)] for q in range(16)])
        for q in range(16):
            li[8 * q : 8 * q + 8, :] = jnp.where(lane <= sub + 8 * q, inv[q], 0.0)
            ud[pl.ds(at + 8 * q, 8), :] = jnp.where(lane >= sub + 8 * q, upper[q], 0.0)
        row = dot3(li[...], p[pl.ds(at, BLK), :], 1, 0)
        p[pl.ds(at, BLK), :] = row
        p[pl.ds(at, BLK), pl.ds(at, BLK)] = li[...]
        for k in range(1, 3):

            @pl.when(k > j)
            def _():
                rows = slice(k * BLK, k * BLK + BLK)
                p[rows, pl.ds(at, BLK)] = jnp.zeros((BLK, BLK), F32)
                p[rows, :] = p[rows, :] - dot3(row[:, rows], p[pl.ds(at, BLK), :], 0, 0)

        return 0

    lax.fori_loop(0, 3, step, 0)


def unpack_child(t, piece, x):
    at = x * PIECE
    for b in range(3):
        for u in range(3):
            t[pl.ds(at + PART * u, PART), b * BLK : (b + 1) * BLK] = piece[
                DIAG + PART * b : DIAG + PART * (b + 1), u * BLK : (u + 1) * BLK
            ]


def panel_kernel(k, marks, info, maps, *refs):
    r = list(refs)
    pieces, r = r[0], r[1:]
    if k:
        t, r = r[0], r[1:]
    packs, r = r[:k], r[k:]
    r = r[marks + (1 if k else 0) :]
    pack, result, r = r[0], r[1], r[2:]
    if not k:
        t, r = r[0], r[1:]
    a, p, li, ud, low, sem = r
    me = info[0]
    col = info[1]
    part = pieces.shape[0] // N_ROW
    for x in range(4):
        buf = pieces.at[x * part : (x + 1) * part, :]
        for j in range(k):
            block = (j + 2) % 3 if k == 3 else j
            ref = p if k == 3 and j == 0 else a
            at = j * PANEL + x * PIECE
            ref[pl.ds(at, PIECE), :] = buf[DIAG + block * PIECE : DIAG + (block + 1) * PIECE, :].astype(F32)
        at = x * PART
        first = buf[:PART, :].astype(F32) + buf[2 * PART : 3 * PART, :].astype(F32)
        rest = buf[PART : 2 * PART, :].astype(F32) + buf[3 * PART : 4 * PART, :].astype(F32)
        a[pl.ds(k * PANEL + at, PART), :] = first
        a[pl.ds(k * PANEL + BLK + at, PART), BLK:] = rest[:, : 2 * BLK]
        a[pl.ds(k * PANEL + 2 * BLK + at, PART), 2 * BLK :] = rest[:, 2 * BLK :]
        if not k:
            unpack_child(t, buf, x)
    if k == 3:
        a[:PANEL, :] = p[...].T
    for b in range(3):
        mb = maps[b] - 3 * k
        for i in range(b + 1):
            ma = maps[i]

            @pl.when((mb >= 0) & (mb < 3) & (ma < 3 * (k + 1)))
            def _():
                rows = pl.ds(pl.multiple_of(ma * BLK, BLK), BLK)
                cols = pl.ds(pl.multiple_of(mb * BLK, BLK), BLK)
                a[rows, cols] = a[rows, cols] + t[i * BLK : (i + 1) * BLK, b * BLK : (b + 1) * BLK].astype(F32)

    up = 2 * PANEL
    for j in range(k):
        z = a[j * PANEL : (j + 1) * PANEL, :]
        if j:
            z = z - dot(packs[j][up : up + j * PANEL, :], pack[up : up + j * PANEL, :], 0, 0)
        zh, zl = split(z)
        ih, il = packs[j][:PANEL, :], packs[j][PANEL:up, :]
        uf = dot(ih, zh, 1, 0) + (dot(ih, zl, 1, 0) + dot(il, zh, 1, 0))

        @pl.when((me == 0) & (col == j))
        def _():
            low[...] = uf.T

        pack[up + j * PANEL : up + (j + 1) * PANEL, :] = uf.astype(BF16)
    z = a[k * PANEL : (k + 1) * PANEL, :]
    if k:
        u = pack[up : up + k * PANEL, :]
        z = z - dot(u, u, 0, 0)
    p[...] = z
    factor_panel(p, li, ud)
    for i in range(3):
        ri = slice(i * BLK, (i + 1) * BLK)
        for j in range(3):
            rj = slice(j * BLK, (j + 1) * BLK)
            lo = slice(PANEL + i * BLK, PANEL + (i + 1) * BLK)
            if j <= i:
                pack[ri, rj], pack[lo, rj] = split(p[ri, rj])
            else:
                pack[ri, rj] = jnp.zeros((BLK, BLK), BF16)
                pack[lo, rj] = jnp.zeros((BLK, BLK), BF16)

    @pl.when((me == 0) & (col == k))
    def _():
        for i in range(3):
            ri = slice(i * BLK, (i + 1) * BLK)
            low[ri, ri] = ud[ri, :].T
            for j in range(i + 1, 3):
                rj = slice(j * BLK, (j + 1) * BLK)
                low[ri, rj] = jnp.zeros((BLK, BLK), F32)
                low[rj, ri] = p[ri, rj].T

    @pl.when((me == 0) & (col > k) & (col < PANELS))
    def _():
        low[...] = jnp.zeros((PANEL, PANEL), F32)

    @pl.when((me == 0) & (col < PANELS))
    def _():
        copy = pltpu.make_async_copy(low, result.at[pl.ds(k * PANEL, PANEL), :], sem)
        copy.start()
        copy.wait()


def panel_call(k, info, maps, pieces, t, packs, marks, result):
    vm = pl.BlockSpec(memory_space=pltpu.VMEM)
    sm = pl.BlockSpec(memory_space=pltpu.SMEM)
    anywhere = pl.BlockSpec(memory_space=pl.ANY)
    args = [pieces] + ([t] if k else []) + list(packs)
    sq = (PANEL, PANEL)
    pinned = pl.BlockSpec(memory_space=pltpu.HBM)
    mark_specs = [pinned if m.size > 2**19 else anywhere for m in marks]
    return pl.pallas_call(
        functools.partial(panel_kernel, k, len(marks)),
        out_shape=[
            jax.ShapeDtypeStruct(((2 + k) * PANEL, PANEL), BF16),
            jax.ShapeDtypeStruct((LEAD, PANEL), F32),
        ]
        + ([] if k else [jax.ShapeDtypeStruct(sq, BF16)]),
        in_specs=[sm, sm] + [vm] * len(args) + mark_specs + ([pinned] if k else []),
        out_specs=[vm, pinned] + ([] if k else [vm]),
        scratch_shapes=[
            pltpu.VMEM(((k + 1) * PANEL, PANEL), F32),
            pltpu.VMEM(sq, F32),
            pltpu.VMEM((BLK, BLK), F32),
            pltpu.VMEM((PANEL, BLK), F32),
            pltpu.VMEM(sq, F32),
            pltpu.SemaphoreType.DMA,
        ],
        input_output_aliases={2 + len(args) + len(marks): 1} if k else {},
        compiler_params=pltpu.CompilerParams(vmem_limit_bytes=16 * 2**20),
        cost_estimate=pl.CostEstimate(flops=10**10, bytes_accessed=10**6, transcendentals=0),
        name=f"panel{k}",
    )(info, maps, *args, *marks, *([result] if k else []))


def vmem_call(kernel, outs, scalars, args, marks=(), name=None):
    vm = pl.BlockSpec(memory_space=pltpu.VMEM)
    sm = pl.BlockSpec(memory_space=pltpu.SMEM)
    anywhere = pl.BlockSpec(memory_space=pl.ANY)

    def body(info, *refs):
        kernel(info, refs[: len(args)], refs[len(args) + len(marks) :])

    return pl.pallas_call(
        body,
        out_shape=[jax.ShapeDtypeStruct(shape, BF16) for shape in outs],
        in_specs=[sm] + [vm] * len(args) + [anywhere] * len(marks),
        out_specs=[vm] * len(outs),
        compiler_params=pltpu.CompilerParams(vmem_limit_bytes=16 * 2**20),
        name=name,
    )(scalars, *args, *marks)


CHILD = DIAG + 2 * PIECE
REST = CHILD + PART


def pick(outs, index, refs):
    for i, ref in enumerate(refs):

        @pl.when(index == i)
        def _():
            outs[...] = ref[...]


def pack_kernel(info, ins, outs):
    front, child = ins
    y = info[3]
    at = pl.multiple_of(y * PANEL, PANEL)
    for s, out in enumerate(outs):
        a = front[pl.ds(at + s * PART, PART), :]
        b = front[pl.ds(at + BLK + s * PART, PART), BLK:]
        c = front[pl.ds(at + 2 * BLK + s * PART, PART), 2 * BLK :]
        ah, al = split(a)
        bh, bl = split(b)
        ch, cl = split(c)
        out[:PART, :] = ah
        out[PART : 2 * PART, : 2 * BLK] = bh
        out[PART : 2 * PART, 2 * BLK :] = ch
        out[2 * PART : 3 * PART, :] = al
        out[3 * PART : DIAG, : 2 * BLK] = bl
        out[3 * PART : DIAG, 2 * BLK :] = cl
        begin = jnp.where(y == 0, 3 * PANEL, jnp.where(y == 3, PANEL, 0))
        rows = pl.ds(pl.multiple_of(begin + s * PIECE, 16), PIECE)
        out[DIAG : DIAG + PIECE, :] = front[rows, :].astype(BF16)
        begin = jnp.where(y == 3, 2 * PANEL, PANEL)
        rows = pl.ds(pl.multiple_of(begin + s * PIECE, 16), PIECE)
        out[DIAG + PIECE : CHILD, :] = front[rows, :].astype(BF16)

        @pl.when(y < 3)
        def _():
            for u in range(3):
                rows = s * PIECE + u * PART
                out[CHILD : CHILD + PART, u * BLK : (u + 1) * BLK] = child[rows : rows + PART, :]


def stage1_kernel(info, ins, outs):
    child, child_one, front = ins[4:]
    piece, pair, high, lead = outs
    me = info[0]
    pick(piece, me, ins[:4])
    n = child.shape[0]
    odd = lax.rem(me, 2)

    @pl.when(odd == 0)
    def _():
        pair[:n, :] = child[...]
        pair[n:, :] = child_one[...]

    @pl.when(odd == 1)
    def _():
        pair[:n, :] = child_one[...]
        pair[n:, :] = child[...]

    full = front[...].astype(BF16)
    high[...] = full
    lead[...] = jnp.where(me == 0, full, jnp.zeros((), BF16))


def stage2_kernel(info, ins, outs):
    pair, pair_got, high, child = ins[4:]
    piece, wide, child_out = outs
    child_out[...] = child[...]
    me, z, first = info[0], info[4], info[2]
    pick(piece, z, ins[:4])

    @pl.when(z == 0)
    def _():
        wide[:, :PANEL] = high[...]
        n = 4 * BLK

        @pl.when(me < 2)
        def _():
            wide[: 2 * n, PANEL:] = pair[...]
            wide[2 * n :, PANEL:] = pair_got[:n, :]

        @pl.when(me == 2)
        def _():
            wide[: 2 * n, PANEL:] = pair_got[...]
            wide[2 * n :, PANEL:] = pair[:n, :]

        @pl.when(me == 3)
        def _():
            wide[:n, PANEL:] = pair_got[n:, :]
            wide[n:, PANEL:] = pair[...]

    @pl.when(z != 0)
    def _():
        wide[...] = jnp.zeros(wide.shape, BF16)


def stage3_kernel(info, ins, outs):
    g0, r1, r2, r3, child = outs
    child[...] = ins[4][...]
    for s in range(4):
        source = lax.rem(info[3] + 4 - s, 4)
        for b, out in enumerate(outs[:4]):

            @pl.when(source == b)
            def _():
                if b == 0:
                    g0[:DIAG, :] = ins[s][:DIAG, :]
                    r3[CHILD:, :] = ins[s][DIAG : DIAG + PIECE, :]
                elif b == 3:
                    r3[:CHILD, :] = ins[s][:CHILD, :]
                else:
                    out[...] = ins[s][: out.shape[0], :]
                if b < 3:
                    g0[DIAG + b * PART : DIAG + (b + 1) * PART, :] = ins[s][CHILD : CHILD + PART, :]


def copy_kernel(info, ins, outs):
    for a, b in zip(ins, outs):
        b[...] = a[...]


def join_kernel(info, ins, outs):
    joined = outs[0]
    n = ins[0].shape[0]
    for s in range(4):
        x = lax.rem(info[0] + 4 - s, 4)
        joined[pl.ds(pl.multiple_of(x * n, 16), n), :] = ins[s][...]
    copy_kernel(info, ins[4:], outs[1:])


def place_kernel(kernel, js, begun, info, ins, outs):
    n = len(js)
    out = outs[-1]
    if begun:
        out[...] = ins[-n - 1][...]
    else:
        out[...] = jnp.zeros(out.shape, BF16)
    kernel(info, ins[: -n - (1 if begun else 0)], outs[:-1])
    for j, ref in zip(js, ins[-n:]):
        slot = info[8 + j] - 3 * info[1]

        @pl.when((slot >= 0) & (slot < 3))
        def _():
            out[:, pl.ds(pl.multiple_of(slot * BLK, BLK), BLK)] = ref[...]


def tail_kernel(info, maps, front, a12, wide, *refs):
    r = list(refs)
    thick, r = r[:4], r[4:]
    packs, r = r[:PANELS], r[PANELS:]
    t = r[0]
    out, r = r[2], r[3:]
    inv, ups, a12v, x, xb, wv, fv, tv, yb = r[:9]
    sem_p, sem_a, sem_w, sem_f, sem_t, sem_o = r[9:]
    me = info[0]
    col = info[1]
    first = info[2]

    def blk(i):
        return slice(i * BLK, (i + 1) * BLK)

    def pan(i):
        return slice(i * PANEL, (i + 1) * PANEL)

    def tile(q):
        return pl.ds(pl.multiple_of(q * PANEL, PANEL), PANEL)

    def up_rows(j):
        return slice(j * (j - 1) // 2 * PANEL, j * (j + 1) // 2 * PANEL)

    copy = pltpu.make_async_copy
    pack_copies = []
    for j in range(PANELS):
        pack_copies.append(copy(packs[j].at[:PANEL, :], inv.at[j], sem_p.at[2 * j]))
        if j:
            pack_copies.append(copy(packs[j].at[2 * PANEL :, :], ups.at[up_rows(j), :], sem_p.at[2 * j + 1]))

    def wide_copy(q):
        return copy(wide.at[pl.ds(4 * q, 4)], wv.at[pl.ds(4 * q, 4)], sem_w.at[q])

    def front_copy(q):
        return copy(front.at[tile(q), :], fv.at[tile(q), :], sem_f.at[q])

    def out_copy(q):
        return copy(fv.at[tile(q), :], out.at[tile(q), :], sem_o.at[q])

    def slot_of(value):
        slot = value - 3 * col
        return slot, (slot >= 0) & (slot < 3)

    def add(ref, row_block, col_slot, value):
        rows = pl.ds(pl.multiple_of(row_block * BLK, BLK), BLK)
        cols = pl.ds(pl.multiple_of(col_slot * BLK, BLK), BLK)
        ref[rows, cols] = ref[rows, cols] + value

    right = col >= PANELS
    lower = me > 0

    @pl.when(right | lower)
    def _():
        for c in pack_copies:
            c.start()

    @pl.when(right & lower)
    def _():
        copy(a12, a12v, sem_a).start()

    @pl.when(right & (me == 0))
    def _():
        for q in range(4):
            front_copy(q).start()

    far = col >= min(SOURCES)

    def thick_copy(i):
        return copy(thick[i], tv.at[lax.rem(me + 4 - i, 4)], sem_t.at[i])

    @pl.when(far)
    def _():
        for i in range(4):
            thick_copy(i).start()

    @pl.when(lower)
    def _():
        for q in range(4):
            wide_copy(q).start()

        @pl.when(right)
        def _():
            for q in range(4):
                front_copy(q).start()

    @pl.when(right | lower)
    def _():
        for c in pack_copies:
            c.wait()

    @pl.when(far)
    def _():
        for i in range(4):
            thick_copy(i).wait()

    @pl.when(right)
    def _():
        @pl.when(me == 0)
        def _():
            for q in range(4):
                front_copy(q).wait()
            x[...] = fv[...]

        @pl.when(lower)
        def _():
            copy(a12, a12v, sem_a).wait()
            x[...] = a12v[...].astype(F32)

        for i in range(3):
            ma = maps[i]

            @pl.when(ma < 12)
            def _():
                for b in range(3):
                    slot, here = slot_of(maps[b])

                    @pl.when(here)
                    def _():
                        add(x, ma, slot, t[blk(i), blk(b)].astype(F32))

                @pl.when(far)
                def _():
                    rows = pl.ds(pl.multiple_of(ma * BLK, BLK), BLK)
                    x[rows, :] = x[rows, :] + tv[0, blk(i), :].astype(F32)

        for j in range(PANELS):
            z = x[pan(j), :]
            if j:
                z = z - dot(ups[up_rows(j), :], xb[: j * PANEL, :], 0, 0)

            @pl.when(me == 0)
            def _():
                fv[pan(j), :] = z
                out_copy(j).start()

            if j < PANELS - 1:
                xb[pan(j), :] = dot(inv[j], z.astype(BF16), 1, 0).astype(BF16)

        @pl.when(lower)
        def _():
            last = dot(inv[PANELS - 1], z.astype(BF16), 1, 0)
            xb[pan(PANELS - 1), :] = last.astype(BF16)
            for j in reversed(range(PANELS)):
                v = xb[pan(j), :]
                for i in range(j + 1, PANELS):
                    at = up_rows(i).start + j * PANEL
                    part = dot(ups[at : at + PANEL, :], xb[pan(i), :], 1, 0)
                    v = v.astype(F32) - part
                xb[pan(j), :] = dot(inv[j], v.astype(BF16), 0, 0).astype(BF16)

        @pl.when(me == 0)
        def _():
            for q in range(4):
                out_copy(q).wait()

    @pl.when(lower)
    def _():
        for q in range(4):
            wide_copy(q).wait()

        def rows_step(q, _):
            @pl.when(right)
            def _():
                front_copy(q).wait()

            for i in range(12):
                ma = maps[first + i] - 12 * me

                @pl.when((ma >= 3 * q) & (ma < 3 * q + 3))
                def _():
                    rows = pl.ds(pl.multiple_of((ma - 3 * q) * BLK, BLK), BLK)
                    for b in range(3):
                        mb = maps[b]
                        piece = wv[(i // 3) * 4 + b, blk(i % 3), PANEL : PANEL + BLK]

                        @pl.when(mb < 12)
                        def _():
                            panel = mb // 3
                            cols = pl.ds(pl.multiple_of((mb - panel * 3) * BLK, BLK), BLK)
                            at = 4 * q + panel
                            wv[at, rows, cols] = (wv[at, rows, cols].astype(F32) + piece.astype(F32)).astype(BF16)

                        slot, here = slot_of(mb)

                        @pl.when(right & here)
                        def _():
                            add(fv, ma, slot, piece.astype(F32))

                    @pl.when(far)
                    def _():
                        held = pl.ds(pl.multiple_of(lax.rem(first + i, 4) * BLK, BLK), BLK)
                        to = pl.ds(pl.multiple_of(ma * BLK, BLK), BLK)
                        fv[to, :] = fv[to, :] + tv[(first + i) // 4, held, :].astype(F32)

            @pl.when(right)
            def _():
                rows = [wv[4 * q + k, :, :PANEL] for k in range(PANELS)]
                fv[tile(q), :] = fv[tile(q), :] - dot(jnp.concatenate(rows, axis=1), xb[...], 1, 0)

            for k in range(PANELS):

                @pl.when(col >= k)
                def _():
                    @pl.when(col < PANELS)
                    def _():
                        z = wv[4 * q + k, :, :PANEL]
                        if k:
                            z = (z.astype(F32) - dot(yb[:, : k * PANEL], ups[up_rows(k), :], 1, 0)).astype(BF16)
                        full = dot(z, inv[k], 1, 1)
                        yb[:, pan(k)] = full.astype(BF16)
                        fv[tile(q), :] = full

            out_copy(q).start()
            return 0

        lax.fori_loop(0, 4, rows_step, 0)
        for q in range(4):
            out_copy(q).wait()


def tail_call(info, maps, front, a12, wide, thick, t, packs, result):
    vm = pl.BlockSpec(memory_space=pltpu.VMEM)
    sm = pl.BlockSpec(memory_space=pltpu.SMEM)
    anywhere = pl.BlockSpec(memory_space=pl.ANY)
    sem = pltpu.SemaphoreType.DMA
    pinned = pl.BlockSpec(memory_space=pltpu.HBM)
    args = [front, a12, wide, *thick, *packs]
    return pl.pallas_call(
        tail_kernel,
        out_shape=jax.ShapeDtypeStruct((LEAD, PANEL), F32),
        in_specs=[sm, sm] + [pinned] * (len(args) - PANELS) + [anywhere] * PANELS + [vm, pinned],
        out_specs=pinned,
        scratch_shapes=[
            pltpu.VMEM((PANELS, PANEL, PANEL), BF16),
            pltpu.VMEM((6 * PANEL, PANEL), BF16),
            pltpu.VMEM((LEAD, PANEL), BF16),
            pltpu.VMEM((LEAD, PANEL), F32),
            pltpu.VMEM((LEAD, PANEL), BF16),
            pltpu.VMEM((N_COL, PANEL, PANEL + BLK), BF16),
            pltpu.VMEM((LEAD, PANEL), F32),
            pltpu.VMEM((4, 4 * BLK, PANEL), BF16),
            pltpu.VMEM((PANEL, LEAD), BF16),
            sem((2 * PANELS,)),
            sem,
            sem((4,)),
            sem((4,)),
            sem((4,)),
            sem((4,)),
        ],
        input_output_aliases={2 + len(args) + 1: 0},
        compiler_params=pltpu.CompilerParams(vmem_limit_bytes=24 * 2**20),
        cost_estimate=pl.CostEstimate(flops=7 * 10**9, bytes_accessed=2 * 10**7, transcendentals=0),
        name="tail",
    )(info, maps, *args, t, result)


def per_device(front_init, contribution, maps):
    front = front_init[0]
    index_map = maps[0]
    me = lax.axis_index("row")
    col = lax.axis_index(COL)
    y = lax.axis_index("y")
    grid = ("row", "z", "y")

    def flat(r, c):
        return r * N_COL + c

    def x_from0(value, s, cols):
        return lax.ppermute(value, grid, [(flat(0, c), flat(s, c)) for c in cols])

    def z_from0(value, s):
        return lax.ppermute(value, COL, [(b, 4 * s + b) for b in range(4)])

    def x_shift(value, s):
        return lax.ppermute(value, "row", [(i, (i + s) % 4) for i in range(4)])

    def y_shift(value, s):
        return lax.ppermute(value, COL, [(4 * z + b, 4 * z + (b + s) % 4) for z in range(4) for b in range(4)])

    def x_swap(value, m):
        return lax.ppermute(value, "row", [(i, i ^ m) for i in range(4)])

    def x_pairs(value, pairs, cols):
        return lax.ppermute(value, grid, [(flat(p, c), flat(q, c)) for p, q in pairs for c in cols])

    def shifts(shift, value):
        return [shift(value, s) for s in range(1, 4)]

    z = lax.axis_index("z")
    first = jnp.where(me == 3, 4, 0)
    ids = jnp.full((N_COL, THICK), -1, jnp.int32)
    for c in SOURCES:
        for j, b in enumerate(SOURCES[c]):
            ids = ids.at[c, j].set(b)
    held = jnp.take(ids, col, axis=0)
    targets = jnp.where(held >= 0, jnp.take(index_map, jnp.maximum(held, 0)), -1000)
    info = jnp.concatenate(
        [jnp.stack([me, col, first, y, z, 0, 0, 0]).astype(jnp.int32), targets.astype(jnp.int32), jnp.zeros((3,), jnp.int32)]
    )

    def contribution_column(value, j):
        pairs = [(SOURCES[c][j], c) for c in SOURCES if j < len(SOURCES[c])]
        return lax.ppermute(value, COL, pairs)

    def staged(kernel, outs, args, marks=(), name=None):
        return vmem_call(kernel, outs, info, args, marks, name)

    received = lax.ppermute(contribution[0], "cube", [(0, 1), (1, 0)])
    piece, full = (REST, PANEL), (LEAD, PANEL)
    pieces = staged(pack_kernel, [piece] * 4, [front, received], name="pack")
    got = [x_from0(pieces[s], s, range(4)) for s in range(1, 4)]
    child_one = x_swap(received, 1)
    own, pair, high, lead = staged(
        stage1_kernel,
        [piece, (8 * BLK, BLK), full, full],
        [pieces[0], *got, received, child_one, front],
        name="stage1",
    )
    got = [z_from0(own, s) for s in range(1, 4)]
    pair_got = x_swap(pair, 3)
    a12 = lax.psum(lead, "row")
    thick = contribution_column(received, 0)
    own, wide_in, received, spread = staged(
        functools.partial(place_kernel, stage2_kernel, (0,), False),
        [piece, (LEAD, PANEL + BLK), received.shape, (4 * BLK, PANEL)],
        [own, *got, pair, pair_got, high, received, thick],
        name="stage2",
    )
    got = shifts(y_shift, own)
    wide_part = lax.psum_scatter(wide_in, "z", tiled=True)
    thick = [contribution_column(received, j) for j in (1, 2)]
    rows = [DIAG + 3 * PART] + [DIAG + b * PIECE for b in range(1, 4)]
    g0, r1, r2, r3, received, spread = staged(
        functools.partial(place_kernel, stage3_kernel, (1, 2), True),
        [(n, PANEL) for n in rows] + [received.shape, spread.shape],
        [own, *got, received, spread, *thick],
        name="stage3",
    )
    g = [g0] + shifts(x_shift, g0)
    thick = [contribution_column(received, j) for j in (3, 4)]

    def joined(value):
        return (4 * value.shape[0], PANEL)

    g0, r1, wide_part, spread = staged(
        functools.partial(place_kernel, join_kernel, (3, 4), True),
        [joined(g[0]), r1.shape, wide_part.shape, spread.shape],
        [*g, r1, wide_part, spread, *thick],
        name="stage4",
    )
    packs = []
    g = [r1] + shifts(x_shift, r1)
    wide = lax.all_gather(wide_part, COL)
    pack, result, t = panel_call(0, info, index_map, g0, None, [], [r1], None)
    packs.append(pack)
    g1, t, r2 = staged(join_kernel, [joined(g[0]), t.shape, r2.shape], [*g, t, r2], [pack], name="stage5")
    g = [r2] + shifts(x_shift, r2)
    pack, result = panel_call(1, info, index_map, g1, t, packs, [r2], result)
    packs.append(pack)
    g2, t, r3 = staged(join_kernel, [joined(g[0]), t.shape, r3.shape], [*g, t, r3], [pack], name="stage6")
    g = [r3] + shifts(x_shift, r3)
    pack, result = panel_call(2, info, index_map, g2, t, packs, [r3, a12], result)
    packs.append(pack)
    g3, t, spread = staged(
        join_kernel, [joined(g[0]), t.shape, spread.shape], [*g, t, spread], [pack], name="stage7"
    )
    far = range(min(SOURCES), N_COL)
    spread = [spread] + [x_pairs(spread, [(i, (i + s) % 4) for i in range(4)], far) for s in range(1, 4)]
    pack, result = panel_call(3, info, index_map, g3, t, packs, [spread[0], wide[0, :16, :BLK]], result)
    packs.append(pack)
    out = tail_call(info, index_map, front, a12, wide, spread, t, packs, result)
    return out[None]


def solution(mesh):
    split_mesh = Mesh(mesh.devices.reshape(2, N_ROW, 4, 4), ("cube", "row", "z", "y"))
    return jax.shard_map(
        per_device,
        mesh=split_mesh,
        in_specs=(P("cube", "row", COL), P("cube", "row", COL), P("cube", None)),
        out_specs=P("cube", "row", COL),
        check_vma=False,
    )
```

```python
import functools

import jax
import jax.numpy as jnp
from jax import lax
from jax.experimental import pallas as pl
from jax.experimental.pallas import tpu as pltpu
from jax.sharding import Mesh
from jax.sharding import PartitionSpec as P

BLK = 128
PANEL = 384
PANELS = 4
N_ROW = 4
N_COL = 16
PIECE = PANEL // N_ROW
PART = BLK // N_ROW
DIAG = 4 * PART
LEAD = PANEL * PANELS
COL = ("z", "y")
F32 = jnp.float32
BF16 = jnp.bfloat16

SOURCES = {11: [3, 4, 5], 12: [4, 5, 6, 7, 8], 13: [7, 8, 9, 10, 11], 14: [10, 11, 12, 13, 14], 15: [13, 14, 15]}
THICK = 5


def dot(a, b, ca, cb):
    return lax.dot_general(a, b, (((ca,), (cb,)), ((), ())), preferred_element_type=F32)


def split(x):
    high = x.astype(BF16)
    return high, (x - high.astype(F32)).astype(BF16)


def dot3(a, b, ca, cb):
    ah, al = split(a)
    bh, bl = split(b)
    return dot(jnp.concatenate([ah, ah, al], ca), jnp.concatenate([bh, bl, bh], cb), ca, cb)


def over_rows(x, i):
    return jnp.broadcast_to(x[i : i + 1, :], x.shape)


def over_lanes(x, j):
    return jnp.broadcast_to(x[:, j : j + 1], x.shape)


def factor_block(tiles, group=8):
    sub = lax.broadcasted_iota(jnp.int32, (8, BLK), 0)
    lane = lax.broadcasted_iota(jnp.int32, (8, BLK), 1)
    v = list(tiles)
    inv, upper, scale = [None] * 16, [None] * 16, [None] * 16
    for g in range(0, 16, group):
        for t in range(g, g + group):
            qs = range(t, g + group)
            c = {(q, j): over_lanes(v[q], 8 * t + j) for q in qs for j in range(8)}
            block = (lane >= 8 * t) & (lane < 8 * t + 8)
            sc = jnp.zeros((8, BLK), F32)
            w = {q: jnp.where(block, 0.0, v[q]) for q in qs}
            w[t] = jnp.where(lane - 8 * t == sub, 1.0, w[t])
            u = v[t]
            for i in range(0, 8, 2):
                p, o, n = over_rows(c[t, i], i), over_rows(c[t, i], i + 1), over_rows(c[t, i + 1], i + 1)
                r = 1.0 / (p * n - o * o)
                low = o * (1.0 / p)
                sc = jnp.where(sub == i, lax.rsqrt(p), jnp.where(sub == i + 1, lax.rsqrt(n - o * low), sc))
                low = jnp.where(sub == i + 1, low, 0.0)
                m1, m2 = {}, {}
                for q in qs:
                    m1[q] = c[q, i] * n - c[q, i + 1] * o
                    m2[q] = c[q, i + 1] * p - c[q, i] * o
                    if q == t:
                        m1[q] = jnp.where(sub > i + 1, m1[q], 0.0)
                        m2[q] = jnp.where(sub > i + 1, m2[q], 0.0)
                    m1[q] = m1[q] * r
                    m2[q] = m2[q] * r
                for j in range(i + 2, 8):
                    row1, row2 = over_rows(c[t, j], i), over_rows(c[t, j], i + 1)
                    for q in qs:
                        c[q, j] = c[q, j] - (m1[q] * row1 + m2[q] * row2)
                row1, row2 = over_rows(w[t], i), over_rows(w[t], i + 1)
                u1, u2 = over_rows(u, i), over_rows(u, i + 1)
                for q in qs:
                    if q != t:
                        w[q] = w[q] - (m1[q] * row1 + m2[q] * row2)
                w_step, u_step = low * row1, low * u1
                if i < 6:
                    w_step = w_step + (m1[t] * row1 + m2[t] * row2)
                    u_step = u_step + (m1[t] * u1 + m2[t] * u2)
                w[t] = w[t] - w_step
                u = u - u_step
            inv[t], scale[t], upper[t] = w[t], sc, u
            for q in range(t + 1, g + group):
                v[q] = w[q]
        if g + group < 16:
            sg = jnp.concatenate(scale[g : g + group], 0)
            ug = jnp.concatenate(upper[g : g + group], 0) * sg
            done = [
                jnp.where((lane >= 8 * t + 8) & (lane < 8 * g + 8 * group), 0.0, inv[t]) for t in range(g, g + group)
            ]
            wg = jnp.concatenate(done, 0) * sg
            update = dot3(ug, wg, 0, 0)
            block = (lane >= 8 * g) & (lane < 8 * g + 8 * group)
            for q in range(g + group, 16):
                v[q] = jnp.where(block, 0.0, v[q]) - update[8 * q : 8 * q + 8, :]
    return [a * s for a, s in zip(inv, scale)], [a * s for a, s in zip(upper, scale)]


def factor_panel(p, li, ud):
    sub = lax.broadcasted_iota(jnp.int32, (8, BLK), 0)
    lane = lax.broadcasted_iota(jnp.int32, (8, BLK), 1)

    def step(j, _):
        at = pl.multiple_of(j * BLK, BLK)
        inv, upper = factor_block([p[pl.ds(at + 8 * q, 8), pl.ds(at, BLK)] for q in range(16)])
        for q in range(16):
            li[8 * q : 8 * q + 8, :] = jnp.where(lane <= sub + 8 * q, inv[q], 0.0)
            ud[pl.ds(at + 8 * q, 8), :] = jnp.where(lane >= sub + 8 * q, upper[q], 0.0)
        row = dot3(li[...], p[pl.ds(at, BLK), :], 1, 0)
        p[pl.ds(at, BLK), :] = row
        p[pl.ds(at, BLK), pl.ds(at, BLK)] = li[...]
        for k in range(1, 3):

            @pl.when(k > j)
            def _():
                rows = slice(k * BLK, k * BLK + BLK)
                p[rows, pl.ds(at, BLK)] = jnp.zeros((BLK, BLK), F32)
                p[rows, :] = p[rows, :] - dot3(row[:, rows], p[pl.ds(at, BLK), :], 0, 0)

        return 0

    lax.fori_loop(0, 3, step, 0)


def unpack_child(t, piece, x):
    at = x * PIECE
    for b in range(3):
        for u in range(3):
            t[pl.ds(at + PART * u, PART), b * BLK : (b + 1) * BLK] = piece[
                DIAG + PART * b : DIAG + PART * (b + 1), u * BLK : (u + 1) * BLK
            ]


def panel_kernel(k, marks, info, maps, *refs):
    r = list(refs)
    pieces, r = r[0], r[1:]
    packs, r = r[:k], r[k:]
    r = r[marks + (1 if k else 0) :]
    pack, result, r = r[0], r[1], r[2:]
    a, p, li, ud, low, sem = r
    t = (packs[0] if k else pack).at[2 * PANEL :, :]
    me = info[0]
    col = info[1]
    part = pieces.shape[0] // N_ROW
    for x in range(4):
        buf = pieces.at[x * part : (x + 1) * part, :]
        for j in range(k):
            block = (j + 2) % 3 if k == 3 else j
            ref = p if k == 3 and j == 0 else a
            at = j * PANEL + x * PIECE
            ref[pl.ds(at, PIECE), :] = buf[DIAG + block * PIECE : DIAG + (block + 1) * PIECE, :].astype(F32)
        at = x * PART
        first = buf[:PART, :].astype(F32) + buf[2 * PART : 3 * PART, :].astype(F32)
        rest = buf[PART : 2 * PART, :].astype(F32) + buf[3 * PART : 4 * PART, :].astype(F32)
        a[pl.ds(k * PANEL + at, PART), :] = first
        a[pl.ds(k * PANEL + BLK + at, PART), BLK:] = rest[:, : 2 * BLK]
        a[pl.ds(k * PANEL + 2 * BLK + at, PART), 2 * BLK :] = rest[:, 2 * BLK :]
        if not k:
            unpack_child(t, buf, x)
    if k == 3:
        a[:PANEL, :] = p[...].T
    for b in range(3):
        mb = maps[b] - 3 * k
        for i in range(b + 1):
            ma = maps[i]

            @pl.when((mb >= 0) & (mb < 3) & (ma < 3 * (k + 1)))
            def _():
                rows = pl.ds(pl.multiple_of(ma * BLK, BLK), BLK)
                cols = pl.ds(pl.multiple_of(mb * BLK, BLK), BLK)
                a[rows, cols] = a[rows, cols] + t[i * BLK : (i + 1) * BLK, b * BLK : (b + 1) * BLK].astype(F32)

    up = 2 * PANEL
    for j in range(k):
        z = a[j * PANEL : (j + 1) * PANEL, :]
        if j:
            z = z - dot(packs[j][up : up + j * PANEL, :], pack[up : up + j * PANEL, :], 0, 0)
        zh, zl = split(z)
        ih, il = packs[j][:PANEL, :], packs[j][PANEL:up, :]
        uf = dot(ih, zh, 1, 0) + (dot(ih, zl, 1, 0) + dot(il, zh, 1, 0))

        @pl.when((me == 0) & (col == j))
        def _():
            low[...] = uf.T

        pack[up + j * PANEL : up + (j + 1) * PANEL, :] = uf.astype(BF16)
    z = a[k * PANEL : (k + 1) * PANEL, :]
    if k:
        u = pack[up : up + k * PANEL, :]
        z = z - dot(u, u, 0, 0)
    p[...] = z
    factor_panel(p, li, ud)
    for i in range(3):
        ri = slice(i * BLK, (i + 1) * BLK)
        for j in range(3):
            rj = slice(j * BLK, (j + 1) * BLK)
            lo = slice(PANEL + i * BLK, PANEL + (i + 1) * BLK)
            if j <= i:
                pack[ri, rj], pack[lo, rj] = split(p[ri, rj])
            else:
                pack[ri, rj] = jnp.zeros((BLK, BLK), BF16)
                pack[lo, rj] = jnp.zeros((BLK, BLK), BF16)

    @pl.when((me == 0) & (col == k))
    def _():
        for i in range(3):
            ri = slice(i * BLK, (i + 1) * BLK)
            low[ri, ri] = ud[ri, :].T
            for j in range(i + 1, 3):
                rj = slice(j * BLK, (j + 1) * BLK)
                low[ri, rj] = jnp.zeros((BLK, BLK), F32)
                low[rj, ri] = p[ri, rj].T

    @pl.when((me == 0) & (col > k) & (col < PANELS))
    def _():
        low[...] = jnp.zeros((PANEL, PANEL), F32)

    @pl.when((me == 0) & (col < PANELS))
    def _():
        copy = pltpu.make_async_copy(low, result.at[pl.ds(k * PANEL, PANEL), :], sem)
        copy.start()
        copy.wait()


def panel_call(k, info, maps, pieces, packs, marks, result):
    vm = pl.BlockSpec(memory_space=pltpu.VMEM)
    sm = pl.BlockSpec(memory_space=pltpu.SMEM)
    anywhere = pl.BlockSpec(memory_space=pl.ANY)
    args = [pieces] + list(packs)
    sq = (PANEL, PANEL)
    pinned = pl.BlockSpec(memory_space=pltpu.HBM)
    mark_specs = [pinned if m.size > 2**19 else anywhere for m in marks]
    return pl.pallas_call(
        functools.partial(panel_kernel, k, len(marks)),
        out_shape=[
            jax.ShapeDtypeStruct(((2 + (k or 1)) * PANEL, PANEL), BF16),
            jax.ShapeDtypeStruct((LEAD, PANEL), F32),
        ],
        in_specs=[sm, sm] + [vm] * len(args) + mark_specs + ([pinned] if k else []),
        out_specs=[vm, pinned],
        scratch_shapes=[
            pltpu.VMEM(((k + 1) * PANEL, PANEL), F32),
            pltpu.VMEM(sq, F32),
            pltpu.VMEM((BLK, BLK), F32),
            pltpu.VMEM((PANEL, BLK), F32),
            pltpu.VMEM(sq, F32),
            pltpu.SemaphoreType.DMA,
        ],
        input_output_aliases={2 + len(args) + len(marks): 1} if k else {},
        compiler_params=pltpu.CompilerParams(vmem_limit_bytes=16 * 2**20),
        cost_estimate=pl.CostEstimate(flops=10**10, bytes_accessed=10**6, transcendentals=0),
        name=f"panel{k}",
    )(info, maps, *args, *marks, *([result] if k else []))


def vmem_call(kernel, outs, scalars, args, marks=(), name=None):
    vm = pl.BlockSpec(memory_space=pltpu.VMEM)
    sm = pl.BlockSpec(memory_space=pltpu.SMEM)
    anywhere = pl.BlockSpec(memory_space=pl.ANY)

    def body(info, *refs):
        kernel(info, refs[: len(args)], refs[len(args) + len(marks) :])

    return pl.pallas_call(
        body,
        out_shape=[jax.ShapeDtypeStruct(shape, BF16) for shape in outs],
        in_specs=[sm] + [vm] * len(args) + [anywhere] * len(marks),
        out_specs=[vm] * len(outs),
        compiler_params=pltpu.CompilerParams(vmem_limit_bytes=16 * 2**20),
        name=name,
    )(scalars, *args, *marks)


CHILD = DIAG + 2 * PIECE
REST = CHILD + PART


def pick(outs, index, refs):
    for i, ref in enumerate(refs):

        @pl.when(index == i)
        def _():
            outs[...] = ref[...]


def pack_kernel(info, ins, outs):
    front, child = ins
    y = info[3]
    at = pl.multiple_of(y * PANEL, PANEL)
    for s, out in enumerate(outs):
        a = front[pl.ds(at + s * PART, PART), :]
        b = front[pl.ds(at + BLK + s * PART, PART), BLK:]
        c = front[pl.ds(at + 2 * BLK + s * PART, PART), 2 * BLK :]
        ah, al = split(a)
        bh, bl = split(b)
        ch, cl = split(c)
        out[:PART, :] = ah
        out[PART : 2 * PART, : 2 * BLK] = bh
        out[PART : 2 * PART, 2 * BLK :] = ch
        out[2 * PART : 3 * PART, :] = al
        out[3 * PART : DIAG, : 2 * BLK] = bl
        out[3 * PART : DIAG, 2 * BLK :] = cl
        begin = jnp.where(y == 0, 3 * PANEL, jnp.where(y == 3, PANEL, 0))
        rows = pl.ds(pl.multiple_of(begin + s * PIECE, 16), PIECE)
        out[DIAG : DIAG + PIECE, :] = front[rows, :].astype(BF16)
        begin = jnp.where(y == 3, 2 * PANEL, PANEL)
        rows = pl.ds(pl.multiple_of(begin + s * PIECE, 16), PIECE)
        out[DIAG + PIECE : CHILD, :] = front[rows, :].astype(BF16)

        @pl.when(y < 3)
        def _():
            for u in range(3):
                rows = s * PIECE + u * PART
                out[CHILD : CHILD + PART, u * BLK : (u + 1) * BLK] = child[rows : rows + PART, :]


def stage1_kernel(info, ins, outs):
    child, child_one, front = ins[4:]
    piece, pair, high, lead = outs
    me = info[0]
    pick(piece, me, ins[:4])
    n = child.shape[0]
    odd = lax.rem(me, 2)

    @pl.when(odd == 0)
    def _():
        pair[:n, :] = child[...]
        pair[n:, :] = child_one[...]

    @pl.when(odd == 1)
    def _():
        pair[:n, :] = child_one[...]
        pair[n:, :] = child[...]

    full = front[...].astype(BF16)
    high[...] = full
    lead[...] = jnp.where(me == 0, full, jnp.zeros((), BF16))


def stage2_kernel(info, ins, outs):
    pair, pair_got, high, child = ins[4:]
    piece, wide, child_out = outs
    child_out[...] = child[...]
    me, z, first = info[0], info[4], info[2]
    pick(piece, z, ins[:4])

    @pl.when(z == 0)
    def _():
        wide[:, :PANEL] = high[...]
        n = 4 * BLK

        @pl.when(me < 2)
        def _():
            wide[: 2 * n, PANEL:] = pair[...]
            wide[2 * n :, PANEL:] = pair_got[:n, :]

        @pl.when(me == 2)
        def _():
            wide[: 2 * n, PANEL:] = pair_got[...]
            wide[2 * n :, PANEL:] = pair[:n, :]

        @pl.when(me == 3)
        def _():
            wide[:n, PANEL:] = pair_got[n:, :]
            wide[n:, PANEL:] = pair[...]

    @pl.when(z != 0)
    def _():
        wide[...] = jnp.zeros(wide.shape, BF16)


def stage3_kernel(info, ins, outs):
    g0, r1, r2, r3, child = outs
    child[...] = ins[4][...]
    for s in range(4):
        source = lax.rem(info[3] + 4 - s, 4)
        for b, out in enumerate(outs[:4]):

            @pl.when(source == b)
            def _():
                if b == 0:
                    g0[:DIAG, :] = ins[s][:DIAG, :]
                    r3[CHILD:, :] = ins[s][DIAG : DIAG + PIECE, :]
                elif b == 3:
                    r3[:CHILD, :] = ins[s][:CHILD, :]
                else:
                    out[...] = ins[s][: out.shape[0], :]
                if b < 3:
                    g0[DIAG + b * PART : DIAG + (b + 1) * PART, :] = ins[s][CHILD : CHILD + PART, :]


def copy_kernel(info, ins, outs):
    for a, b in zip(ins, outs):
        b[...] = a[...]


def join_kernel(info, ins, outs):
    joined = outs[0]
    n = ins[0].shape[0]
    for s in range(4):
        x = lax.rem(info[0] + 4 - s, 4)
        joined[pl.ds(pl.multiple_of(x * n, 16), n), :] = ins[s][...]
    copy_kernel(info, ins[4:], outs[1:])


def place_kernel(kernel, js, begun, info, ins, outs):
    n = len(js)
    out = outs[-1]
    if begun:
        out[...] = ins[-n - 1][...]
    else:
        out[...] = jnp.zeros(out.shape, BF16)
    kernel(info, ins[: -n - (1 if begun else 0)], outs[:-1])
    for j, ref in zip(js, ins[-n:]):
        slot = info[8 + j] - 3 * info[1]

        @pl.when((slot >= 0) & (slot < 3))
        def _():
            out[:, pl.ds(pl.multiple_of(slot * BLK, BLK), BLK)] = ref[...]


def tail_kernel(info, maps, front, a12, wide, *refs):
    r = list(refs)
    thick, r = r[:4], r[4:]
    packs, r = r[:PANELS], r[PANELS:]
    out, r = r[1], r[2:]
    inv, ups, t, a12v, x, xb, wv, fv, tv, yb = r[:10]
    sem_p, sem_a, sem_w, sem_f, sem_t, sem_o = r[10:]
    me = info[0]
    col = info[1]
    first = info[2]

    def blk(i):
        return slice(i * BLK, (i + 1) * BLK)

    def pan(i):
        return slice(i * PANEL, (i + 1) * PANEL)

    def tile(q):
        return pl.ds(pl.multiple_of(q * PANEL, PANEL), PANEL)

    def up_rows(j):
        return slice(j * (j - 1) // 2 * PANEL, j * (j + 1) // 2 * PANEL)

    copy = pltpu.make_async_copy
    pack_copies = []
    for j in range(PANELS):
        pack_copies.append(copy(packs[j].at[:PANEL, :], inv.at[j], sem_p.at[2 * j]))
        to = ups.at[up_rows(j), :] if j else t
        pack_copies.append(copy(packs[j].at[2 * PANEL :, :], to, sem_p.at[2 * j + 1]))

    def wide_copy(q):
        return copy(wide.at[pl.ds(4 * q, 4)], wv.at[pl.ds(4 * q, 4)], sem_w.at[q])

    def front_copy(q):
        return copy(front.at[tile(q), :], fv.at[tile(q), :], sem_f.at[q])

    def out_copy(q):
        return copy(fv.at[tile(q), :], out.at[tile(q), :], sem_o.at[q])

    def slot_of(value):
        slot = value - 3 * col
        return slot, (slot >= 0) & (slot < 3)

    def add(ref, row_block, col_slot, value):
        rows = pl.ds(pl.multiple_of(row_block * BLK, BLK), BLK)
        cols = pl.ds(pl.multiple_of(col_slot * BLK, BLK), BLK)
        ref[rows, cols] = ref[rows, cols] + value

    right = col >= PANELS
    lower = me > 0

    @pl.when(right | lower)
    def _():
        for c in pack_copies:
            c.start()

    @pl.when(right & lower)
    def _():
        copy(a12, a12v, sem_a).start()

    @pl.when(right & (me == 0))
    def _():
        for q in range(4):
            front_copy(q).start()

    far = col >= min(SOURCES)

    def thick_copy(i):
        return copy(thick[i], tv.at[lax.rem(me + 4 - i, 4)], sem_t.at[i])

    @pl.when(far)
    def _():
        for i in range(4):
            thick_copy(i).start()

    @pl.when(lower)
    def _():
        for q in range(4):
            wide_copy(q).start()

        @pl.when(right)
        def _():
            for q in range(4):
                front_copy(q).start()

    @pl.when(right | lower)
    def _():
        for c in pack_copies:
            c.wait()

    @pl.when(far)
    def _():
        for i in range(4):
            thick_copy(i).wait()

    @pl.when(right)
    def _():
        @pl.when(me == 0)
        def _():
            for q in range(4):
                front_copy(q).wait()
            x[...] = fv[...]

        @pl.when(lower)
        def _():
            copy(a12, a12v, sem_a).wait()
            x[...] = a12v[...].astype(F32)

        for i in range(3):
            ma = maps[i]

            @pl.when(ma < 12)
            def _():
                for b in range(3):
                    slot, here = slot_of(maps[b])

                    @pl.when(here)
                    def _():
                        add(x, ma, slot, t[blk(i), blk(b)].astype(F32))

                @pl.when(far)
                def _():
                    rows = pl.ds(pl.multiple_of(ma * BLK, BLK), BLK)
                    x[rows, :] = x[rows, :] + tv[0, blk(i), :].astype(F32)

        for j in range(PANELS):
            z = x[pan(j), :]
            if j:
                z = z - dot(ups[up_rows(j), :], xb[: j * PANEL, :], 0, 0)

            @pl.when(me == 0)
            def _():
                fv[pan(j), :] = z
                out_copy(j).start()

            if j < PANELS - 1:
                xb[pan(j), :] = dot(inv[j], z.astype(BF16), 1, 0).astype(BF16)

        @pl.when(lower)
        def _():
            last = dot(inv[PANELS - 1], z.astype(BF16), 1, 0)
            xb[pan(PANELS - 1), :] = last.astype(BF16)
            for j in reversed(range(PANELS)):
                v = xb[pan(j), :]
                for i in range(j + 1, PANELS):
                    at = up_rows(i).start + j * PANEL
                    part = dot(ups[at : at + PANEL, :], xb[pan(i), :], 1, 0)
                    v = v.astype(F32) - part
                xb[pan(j), :] = dot(inv[j], v.astype(BF16), 0, 0).astype(BF16)

        @pl.when(me == 0)
        def _():
            for q in range(4):
                out_copy(q).wait()

    @pl.when(lower)
    def _():
        for q in range(4):
            wide_copy(q).wait()

        def rows_step(q, _):
            @pl.when(right)
            def _():
                front_copy(q).wait()

            for i in range(12):
                ma = maps[first + i] - 12 * me

                @pl.when((ma >= 3 * q) & (ma < 3 * q + 3))
                def _():
                    rows = pl.ds(pl.multiple_of((ma - 3 * q) * BLK, BLK), BLK)
                    for b in range(3):
                        mb = maps[b]
                        piece = wv[(i // 3) * 4 + b, blk(i % 3), PANEL : PANEL + BLK]

                        @pl.when(mb < 12)
                        def _():
                            panel = mb // 3
                            cols = pl.ds(pl.multiple_of((mb - panel * 3) * BLK, BLK), BLK)
                            at = 4 * q + panel
                            wv[at, rows, cols] = (wv[at, rows, cols].astype(F32) + piece.astype(F32)).astype(BF16)

                        slot, here = slot_of(mb)

                        @pl.when(right & here)
                        def _():
                            add(fv, ma, slot, piece.astype(F32))

                    @pl.when(far)
                    def _():
                        held = pl.ds(pl.multiple_of(lax.rem(first + i, 4) * BLK, BLK), BLK)
                        to = pl.ds(pl.multiple_of(ma * BLK, BLK), BLK)
                        fv[to, :] = fv[to, :] + tv[(first + i) // 4, held, :].astype(F32)

            @pl.when(right)
            def _():
                rows = [wv[4 * q + k, :, :PANEL] for k in range(PANELS)]
                fv[tile(q), :] = fv[tile(q), :] - dot(jnp.concatenate(rows, axis=1), xb[...], 1, 0)

            for k in range(PANELS):

                @pl.when(col >= k)
                def _():
                    @pl.when(col < PANELS)
                    def _():
                        z = wv[4 * q + k, :, :PANEL]
                        if k:
                            z = (z.astype(F32) - dot(yb[:, : k * PANEL], ups[up_rows(k), :], 1, 0)).astype(BF16)
                        full = dot(z, inv[k], 1, 1)
                        yb[:, pan(k)] = full.astype(BF16)
                        fv[tile(q), :] = full

            out_copy(q).start()
            return 0

        lax.fori_loop(0, 4, rows_step, 0)
        for q in range(4):
            out_copy(q).wait()


def tail_call(info, maps, front, a12, wide, thick, packs, result):
    vm = pl.BlockSpec(memory_space=pltpu.VMEM)
    sm = pl.BlockSpec(memory_space=pltpu.SMEM)
    anywhere = pl.BlockSpec(memory_space=pl.ANY)
    sem = pltpu.SemaphoreType.DMA
    pinned = pl.BlockSpec(memory_space=pltpu.HBM)
    args = [front, a12, wide, *thick, *packs]
    return pl.pallas_call(
        tail_kernel,
        out_shape=jax.ShapeDtypeStruct((LEAD, PANEL), F32),
        in_specs=[sm, sm] + [pinned] * (len(args) - PANELS) + [anywhere] * PANELS + [pinned],
        out_specs=pinned,
        scratch_shapes=[
            pltpu.VMEM((PANELS, PANEL, PANEL), BF16),
            pltpu.VMEM((6 * PANEL, PANEL), BF16),
            pltpu.VMEM((PANEL, PANEL), BF16),
            pltpu.VMEM((LEAD, PANEL), BF16),
            pltpu.VMEM((LEAD, PANEL), F32),
            pltpu.VMEM((LEAD, PANEL), BF16),
            pltpu.VMEM((N_COL, PANEL, PANEL + BLK), BF16),
            pltpu.VMEM((LEAD, PANEL), F32),
            pltpu.VMEM((4, 4 * BLK, PANEL), BF16),
            pltpu.VMEM((PANEL, LEAD), BF16),
            sem((2 * PANELS,)),
            sem,
            sem((4,)),
            sem((4,)),
            sem((4,)),
            sem((4,)),
        ],
        input_output_aliases={2 + len(args): 0},
        compiler_params=pltpu.CompilerParams(vmem_limit_bytes=60 * 2**20),
        cost_estimate=pl.CostEstimate(flops=7 * 10**9, bytes_accessed=2 * 10**7, transcendentals=0),
        name="tail",
    )(info, maps, *args, result)


def per_device(front_init, contribution, maps):
    front = front_init[0]
    index_map = maps[0]
    me = lax.axis_index("row")
    col = lax.axis_index(COL)
    y = lax.axis_index("y")
    grid = ("row", "z", "y")

    def flat(r, c):
        return r * N_COL + c

    def x_from0(value, s, cols):
        return lax.ppermute(value, grid, [(flat(0, c), flat(s, c)) for c in cols])

    def z_from0(value, s):
        return lax.ppermute(value, COL, [(b, 4 * s + b) for b in range(4)])

    def x_shift(value, s):
        return lax.ppermute(value, "row", [(i, (i + s) % 4) for i in range(4)])

    def y_shift(value, s):
        return lax.ppermute(value, COL, [(4 * z + b, 4 * z + (b + s) % 4) for z in range(4) for b in range(4)])

    def x_swap(value, m):
        return lax.ppermute(value, "row", [(i, i ^ m) for i in range(4)])

    def x_pairs(value, pairs, cols):
        return lax.ppermute(value, grid, [(flat(p, c), flat(q, c)) for p, q in pairs for c in cols])

    def shifts(shift, value):
        return [shift(value, s) for s in range(1, 4)]

    z = lax.axis_index("z")
    first = jnp.where(me == 3, 4, 0)
    ids = jnp.full((N_COL, THICK), -1, jnp.int32)
    for c in SOURCES:
        for j, b in enumerate(SOURCES[c]):
            ids = ids.at[c, j].set(b)
    held = jnp.take(ids, col, axis=0)
    targets = jnp.where(held >= 0, jnp.take(index_map, jnp.maximum(held, 0)), -1000)
    info = jnp.concatenate(
        [jnp.stack([me, col, first, y, z, 0, 0, 0]).astype(jnp.int32), targets.astype(jnp.int32), jnp.zeros((3,), jnp.int32)]
    )

    def contribution_column(value, j):
        pairs = [(SOURCES[c][j], c) for c in SOURCES if j < len(SOURCES[c])]
        return lax.ppermute(value, COL, pairs)

    def staged(kernel, outs, args, marks=(), name=None):
        return vmem_call(kernel, outs, info, args, marks, name)

    received = lax.ppermute(contribution[0], "cube", [(0, 1), (1, 0)])
    piece, full = (REST, PANEL), (LEAD, PANEL)
    pieces = staged(pack_kernel, [piece] * 4, [front, received], name="pack")
    got = [x_from0(pieces[s], s, range(4)) for s in range(1, 4)]
    child_one = x_swap(received, 1)
    own, pair, high, lead = staged(
        stage1_kernel,
        [piece, (8 * BLK, BLK), full, full],
        [pieces[0], *got, received, child_one, front],
        name="stage1",
    )
    got = [z_from0(own, s) for s in range(1, 4)]
    pair_got = x_swap(pair, 3)
    a12 = lax.psum(lead, "row")
    thick = contribution_column(received, 0)
    own, wide_in, received, spread = staged(
        functools.partial(place_kernel, stage2_kernel, (0,), False),
        [piece, (LEAD, PANEL + BLK), received.shape, (4 * BLK, PANEL)],
        [own, *got, pair, pair_got, high, received, thick],
        name="stage2",
    )
    got = shifts(y_shift, own)
    wide_part = lax.psum_scatter(wide_in, "z", tiled=True)
    thick = [contribution_column(received, j) for j in (1, 2)]
    rows = [DIAG + 3 * PART] + [DIAG + b * PIECE for b in range(1, 4)]
    g0, r1, r2, r3, received, spread = staged(
        functools.partial(place_kernel, stage3_kernel, (1, 2), True),
        [(n, PANEL) for n in rows] + [received.shape, spread.shape],
        [own, *got, received, spread, *thick],
        name="stage3",
    )
    g = [g0] + shifts(x_shift, g0)
    thick = [contribution_column(received, j) for j in (3, 4)]

    def joined(value):
        return (4 * value.shape[0], PANEL)

    g0, r1, wide_part, spread = staged(
        functools.partial(place_kernel, join_kernel, (3, 4), True),
        [joined(g[0]), r1.shape, wide_part.shape, spread.shape],
        [*g, r1, wide_part, spread, *thick],
        name="stage4",
    )
    packs = []
    g = [r1] + shifts(x_shift, r1)
    wide = lax.all_gather(wide_part, COL)
    pack, result = panel_call(0, info, index_map, g0, [], [r1], None)
    packs.append(pack)
    g1, r2 = staged(join_kernel, [joined(g[0]), r2.shape], [*g, r2], [pack], name="stage5")
    g = [r2] + shifts(x_shift, r2)
    pack, result = panel_call(1, info, index_map, g1, packs, [r2], result)
    packs.append(pack)
    (r3,) = staged(copy_kernel, [r3.shape], [r3], [pack], name="stage6")
    after = [r3] + shifts(x_shift, r3)
    (g2,) = staged(join_kernel, [joined(g[0])], g, [r3], name="join2")
    g = after
    pack, result = panel_call(2, info, index_map, g2, packs, [r3], result)
    packs.append(pack)
    (spread,) = staged(copy_kernel, [spread.shape], [spread], [pack], name="stage7")
    far = range(min(SOURCES), N_COL)
    spread = [spread] + [x_pairs(spread, [(i, (i + s) % 4) for i in range(4)], far) for s in range(1, 4)]
    (g3,) = staged(join_kernel, [joined(g[0])], g, [spread[0]], name="join3")
    pack, result = panel_call(3, info, index_map, g3, packs, [spread[0]], result)
    packs.append(pack)
    out = tail_call(info, index_map, front, a12, wide, spread, packs, result)
    return out[None]


def solution(mesh):
    split_mesh = Mesh(mesh.devices.reshape(2, N_ROW, 4, 4), ("cube", "row", "z", "y"))
    return jax.shard_map(
        per_device,
        mesh=split_mesh,
        in_specs=(P("cube", "row", COL), P("cube", "row", COL), P("cube", None)),
        out_specs=P("cube", "row", COL),
        check_vma=False,
    )
```

```python
import functools

import jax
import jax.numpy as jnp
from jax import lax
from jax.experimental import pallas as pl
from jax.experimental.pallas import tpu as pltpu
from jax.sharding import Mesh
from jax.sharding import PartitionSpec as P

BLK = 128
PANEL = 384
PANELS = 4
N_ROW = 4
N_COL = 16
PIECE = PANEL // N_ROW
PART = BLK // N_ROW
DIAG = 4 * PART
LEAD = PANEL * PANELS
COL = ("z", "y")
F32 = jnp.float32
BF16 = jnp.bfloat16

SOURCES = {11: [3, 4, 5], 12: [4, 5, 6, 7, 8], 13: [7, 8, 9, 10, 11], 14: [10, 11, 12, 13, 14], 15: [13, 14, 15]}
THICK = 5


def dot(a, b, ca, cb):
    return lax.dot_general(a, b, (((ca,), (cb,)), ((), ())), preferred_element_type=F32)


def split(x):
    high = x.astype(BF16)
    return high, (x - high.astype(F32)).astype(BF16)


def dot3(a, b, ca, cb):
    ah, al = split(a)
    bh, bl = split(b)
    return dot(jnp.concatenate([ah, ah, al], ca), jnp.concatenate([bh, bl, bh], cb), ca, cb)


def over_rows(x, i):
    return jnp.broadcast_to(x[i : i + 1, :], x.shape)


def over_lanes(x, j):
    return jnp.broadcast_to(x[:, j : j + 1], x.shape)


def factor_block(tiles, group=8):
    sub = lax.broadcasted_iota(jnp.int32, (8, BLK), 0)
    lane = lax.broadcasted_iota(jnp.int32, (8, BLK), 1)
    v = list(tiles)
    inv, upper, scale = [None] * 16, [None] * 16, [None] * 16
    for g in range(0, 16, group):
        for t in range(g, g + group):
            qs = range(t, g + group)
            c = {(q, j): over_lanes(v[q], 8 * t + j) for q in qs for j in range(8)}
            block = (lane >= 8 * t) & (lane < 8 * t + 8)
            sc = jnp.zeros((8, BLK), F32)
            w = {q: jnp.where(block, 0.0, v[q]) for q in qs}
            w[t] = jnp.where(lane - 8 * t == sub, 1.0, w[t])
            u = v[t]
            for i in range(0, 8, 2):
                p, o, n = over_rows(c[t, i], i), over_rows(c[t, i], i + 1), over_rows(c[t, i + 1], i + 1)
                r = 1.0 / (p * n - o * o)
                low = o * (1.0 / p)
                sc = jnp.where(sub == i, lax.rsqrt(p), jnp.where(sub == i + 1, lax.rsqrt(n - o * low), sc))
                low = jnp.where(sub == i + 1, low, 0.0)
                m1, m2 = {}, {}
                for q in qs:
                    m1[q] = c[q, i] * n - c[q, i + 1] * o
                    m2[q] = c[q, i + 1] * p - c[q, i] * o
                    if q == t:
                        m1[q] = jnp.where(sub > i + 1, m1[q], 0.0)
                        m2[q] = jnp.where(sub > i + 1, m2[q], 0.0)
                    m1[q] = m1[q] * r
                    m2[q] = m2[q] * r
                for j in range(i + 2, 8):
                    row1, row2 = over_rows(c[t, j], i), over_rows(c[t, j], i + 1)
                    for q in qs:
                        c[q, j] = c[q, j] - (m1[q] * row1 + m2[q] * row2)
                row1, row2 = over_rows(w[t], i), over_rows(w[t], i + 1)
                u1, u2 = over_rows(u, i), over_rows(u, i + 1)
                for q in qs:
                    if q != t:
                        w[q] = w[q] - (m1[q] * row1 + m2[q] * row2)
                w_step, u_step = low * row1, low * u1
                if i < 6:
                    w_step = w_step + (m1[t] * row1 + m2[t] * row2)
                    u_step = u_step + (m1[t] * u1 + m2[t] * u2)
                w[t] = w[t] - w_step
                u = u - u_step
            inv[t], scale[t], upper[t] = w[t], sc, u
            for q in range(t + 1, g + group):
                v[q] = w[q]
        if g + group < 16:
            sg = jnp.concatenate(scale[g : g + group], 0)
            ug = jnp.concatenate(upper[g : g + group], 0) * sg
            done = [
                jnp.where((lane >= 8 * t + 8) & (lane < 8 * g + 8 * group), 0.0, inv[t]) for t in range(g, g + group)
            ]
            wg = jnp.concatenate(done, 0) * sg
            update = dot3(ug, wg, 0, 0)
            block = (lane >= 8 * g) & (lane < 8 * g + 8 * group)
            for q in range(g + group, 16):
                v[q] = jnp.where(block, 0.0, v[q]) - update[8 * q : 8 * q + 8, :]
    return [a * s for a, s in zip(inv, scale)], [a * s for a, s in zip(upper, scale)]


def factor_panel(p, li, ud):
    sub = lax.broadcasted_iota(jnp.int32, (8, BLK), 0)
    lane = lax.broadcasted_iota(jnp.int32, (8, BLK), 1)

    def step(j, _):
        at = pl.multiple_of(j * BLK, BLK)
        inv, upper = factor_block([p[pl.ds(at + 8 * q, 8), pl.ds(at, BLK)] for q in range(16)])
        for q in range(16):
            li[8 * q : 8 * q + 8, :] = jnp.where(lane <= sub + 8 * q, inv[q], 0.0)
            ud[pl.ds(at + 8 * q, 8), :] = jnp.where(lane >= sub + 8 * q, upper[q], 0.0)
        row = dot3(li[...], p[pl.ds(at, BLK), :], 1, 0)
        p[pl.ds(at, BLK), :] = row
        p[pl.ds(at, BLK), pl.ds(at, BLK)] = li[...]
        for k in range(1, 3):

            @pl.when(k > j)
            def _():
                rows = slice(k * BLK, k * BLK + BLK)
                p[rows, pl.ds(at, BLK)] = jnp.zeros((BLK, BLK), F32)
                p[rows, :] = p[rows, :] - dot3(row[:, rows], p[pl.ds(at, BLK), :], 0, 0)

        return 0

    lax.fori_loop(0, 3, step, 0)


def unpack_child(t, piece, x):
    at = x * PIECE
    for b in range(3):
        for u in range(3):
            t[pl.ds(at + PART * u, PART), b * BLK : (b + 1) * BLK] = piece[
                DIAG + PART * b : DIAG + PART * (b + 1), u * BLK : (u + 1) * BLK
            ]


def panel_kernel(k, marks, info, maps, *refs):
    r = list(refs)
    pieces, r = r[0], r[1:]
    packs, r = r[:k], r[k:]
    r = r[marks + (1 if k else 0) :]
    pack, result, r = r[0], r[1], r[2:]
    a, p, li, ud, low, sem = r
    t = (packs[0] if k else pack).at[2 * PANEL :, :]
    me = info[0]
    col = info[1]
    part = pieces.shape[0] // N_ROW
    for x in range(4):
        buf = pieces.at[x * part : (x + 1) * part, :]
        for j in range(k):
            block = (j + 2) % 3 if k == 3 else j
            ref = p if k == 3 and j == 0 else a
            at = j * PANEL + x * PIECE
            ref[pl.ds(at, PIECE), :] = buf[DIAG + block * PIECE : DIAG + (block + 1) * PIECE, :].astype(F32)
        at = x * PART
        first = buf[:PART, :].astype(F32) + buf[2 * PART : 3 * PART, :].astype(F32)
        rest = buf[PART : 2 * PART, :].astype(F32) + buf[3 * PART : 4 * PART, :].astype(F32)
        a[pl.ds(k * PANEL + at, PART), :] = first
        a[pl.ds(k * PANEL + BLK + at, PART), BLK:] = rest[:, : 2 * BLK]
        a[pl.ds(k * PANEL + 2 * BLK + at, PART), 2 * BLK :] = rest[:, 2 * BLK :]
        if not k:
            unpack_child(t, buf, x)
    if k == 3:
        a[:PANEL, :] = p[...].T
    for b in range(3):
        mb = maps[b] - 3 * k
        for i in range(b + 1):
            ma = maps[i]

            @pl.when((mb >= 0) & (mb < 3) & (ma < 3 * (k + 1)))
            def _():
                rows = pl.ds(pl.multiple_of(ma * BLK, BLK), BLK)
                cols = pl.ds(pl.multiple_of(mb * BLK, BLK), BLK)
                a[rows, cols] = a[rows, cols] + t[i * BLK : (i + 1) * BLK, b * BLK : (b + 1) * BLK].astype(F32)

    up = 2 * PANEL
    for j in range(k):
        z = a[j * PANEL : (j + 1) * PANEL, :]
        if j:
            z = z - dot(packs[j][up : up + j * PANEL, :], pack[up : up + j * PANEL, :], 0, 0)
        zh, zl = split(z)
        ih, il = packs[j][:PANEL, :], packs[j][PANEL:up, :]
        uf = dot(ih, zh, 1, 0) + (dot(ih, zl, 1, 0) + dot(il, zh, 1, 0))

        @pl.when((me == 0) & (col == j))
        def _():
            low[...] = uf.T

        pack[up + j * PANEL : up + (j + 1) * PANEL, :] = uf.astype(BF16)
    z = a[k * PANEL : (k + 1) * PANEL, :]
    if k:
        u = pack[up : up + k * PANEL, :]
        z = z - dot(u, u, 0, 0)
    p[...] = z
    factor_panel(p, li, ud)
    for i in range(3):
        ri = slice(i * BLK, (i + 1) * BLK)
        for j in range(3):
            rj = slice(j * BLK, (j + 1) * BLK)
            lo = slice(PANEL + i * BLK, PANEL + (i + 1) * BLK)
            if j <= i:
                pack[ri, rj], pack[lo, rj] = split(p[ri, rj])
            else:
                pack[ri, rj] = jnp.zeros((BLK, BLK), BF16)
                pack[lo, rj] = jnp.zeros((BLK, BLK), BF16)

    @pl.when((me == 0) & (col == k))
    def _():
        for i in range(3):
            ri = slice(i * BLK, (i + 1) * BLK)
            low[ri, ri] = ud[ri, :].T
            for j in range(i + 1, 3):
                rj = slice(j * BLK, (j + 1) * BLK)
                low[ri, rj] = jnp.zeros((BLK, BLK), F32)
                low[rj, ri] = p[ri, rj].T

    @pl.when((me == 0) & (col > k) & (col < PANELS))
    def _():
        low[...] = jnp.zeros((PANEL, PANEL), F32)

    @pl.when((me == 0) & (col < PANELS))
    def _():
        copy = pltpu.make_async_copy(low, result.at[pl.ds(k * PANEL, PANEL), :], sem)
        copy.start()
        copy.wait()


def panel_call(k, info, maps, pieces, packs, marks, result):
    vm = pl.BlockSpec(memory_space=pltpu.VMEM)
    sm = pl.BlockSpec(memory_space=pltpu.SMEM)
    anywhere = pl.BlockSpec(memory_space=pl.ANY)
    args = [pieces] + list(packs)
    sq = (PANEL, PANEL)
    pinned = pl.BlockSpec(memory_space=pltpu.HBM)
    mark_specs = [pinned if m.size > 2**19 else anywhere for m in marks]
    return pl.pallas_call(
        functools.partial(panel_kernel, k, len(marks)),
        out_shape=[
            jax.ShapeDtypeStruct(((2 + (k or 1)) * PANEL, PANEL), BF16),
            jax.ShapeDtypeStruct((LEAD, PANEL), F32),
        ],
        in_specs=[sm, sm] + [vm] * len(args) + mark_specs + ([pinned] if k else []),
        out_specs=[vm, pinned],
        scratch_shapes=[
            pltpu.VMEM(((k + 1) * PANEL, PANEL), F32),
            pltpu.VMEM(sq, F32),
            pltpu.VMEM((BLK, BLK), F32),
            pltpu.VMEM((PANEL, BLK), F32),
            pltpu.VMEM(sq, F32),
            pltpu.SemaphoreType.DMA,
        ],
        input_output_aliases={2 + len(args) + len(marks): 1} if k else {},
        compiler_params=pltpu.CompilerParams(vmem_limit_bytes=16 * 2**20),
        cost_estimate=pl.CostEstimate(flops=10**10, bytes_accessed=10**6, transcendentals=0),
        name=f"panel{k}",
    )(info, maps, *args, *marks, *([result] if k else []))


def vmem_call(kernel, outs, scalars, args, marks=(), name=None):
    vm = pl.BlockSpec(memory_space=pltpu.VMEM)
    sm = pl.BlockSpec(memory_space=pltpu.SMEM)
    anywhere = pl.BlockSpec(memory_space=pl.ANY)

    def body(info, *refs):
        kernel(info, refs[: len(args)], refs[len(args) + len(marks) :])

    return pl.pallas_call(
        body,
        out_shape=[jax.ShapeDtypeStruct(shape, BF16) for shape in outs],
        in_specs=[sm] + [vm] * len(args) + [anywhere] * len(marks),
        out_specs=[vm] * len(outs),
        compiler_params=pltpu.CompilerParams(vmem_limit_bytes=16 * 2**20),
        name=name,
    )(scalars, *args, *marks)


CHILD = DIAG + 2 * PIECE
REST = CHILD + PART


def pick(outs, index, refs):
    for i, ref in enumerate(refs):

        @pl.when(index == i)
        def _():
            outs[...] = ref[...]


def pack_kernel(info, ins, outs):
    front, child = ins
    y = info[3]
    at = pl.multiple_of(y * PANEL, PANEL)
    for s, out in enumerate(outs):
        a = front[pl.ds(at + s * PART, PART), :]
        b = front[pl.ds(at + BLK + s * PART, PART), BLK:]
        c = front[pl.ds(at + 2 * BLK + s * PART, PART), 2 * BLK :]
        ah, al = split(a)
        bh, bl = split(b)
        ch, cl = split(c)
        out[:PART, :] = ah
        out[PART : 2 * PART, : 2 * BLK] = bh
        out[PART : 2 * PART, 2 * BLK :] = ch
        out[2 * PART : 3 * PART, :] = al
        out[3 * PART : DIAG, : 2 * BLK] = bl
        out[3 * PART : DIAG, 2 * BLK :] = cl
        begin = jnp.where(y == 0, 3 * PANEL, jnp.where(y == 3, PANEL, 0))
        rows = pl.ds(pl.multiple_of(begin + s * PIECE, 16), PIECE)
        out[DIAG : DIAG + PIECE, :] = front[rows, :].astype(BF16)
        begin = jnp.where(y == 3, 2 * PANEL, PANEL)
        rows = pl.ds(pl.multiple_of(begin + s * PIECE, 16), PIECE)
        out[DIAG + PIECE : CHILD, :] = front[rows, :].astype(BF16)

        @pl.when(y < 3)
        def _():
            for u in range(3):
                rows = s * PIECE + u * PART
                out[CHILD : CHILD + PART, u * BLK : (u + 1) * BLK] = child[rows : rows + PART, :]


def stage1_kernel(info, ins, outs):
    child, child_one, front = ins[4:]
    piece, pair, high, lead = outs
    me = info[0]
    pick(piece, me, ins[:4])
    n = child.shape[0]
    odd = lax.rem(me, 2)

    @pl.when(odd == 0)
    def _():
        pair[:n, :] = child[...]
        pair[n:, :] = child_one[...]

    @pl.when(odd == 1)
    def _():
        pair[:n, :] = child_one[...]
        pair[n:, :] = child[...]

    full = front[...].astype(BF16)
    high[...] = full
    lead[...] = jnp.where(me == 0, full, jnp.zeros((), BF16))


def stage2_kernel(info, ins, outs):
    pair, pair_got, high, child = ins[4:]
    piece, wide, child_out = outs
    child_out[...] = child[...]
    me, z, first = info[0], info[4], info[2]
    pick(piece, z, ins[:4])

    @pl.when(z == 0)
    def _():
        wide[:, :PANEL] = high[...]
        n = 4 * BLK

        @pl.when(me < 2)
        def _():
            wide[: 2 * n, PANEL:] = pair[...]
            wide[2 * n :, PANEL:] = pair_got[:n, :]

        @pl.when(me == 2)
        def _():
            wide[: 2 * n, PANEL:] = pair_got[...]
            wide[2 * n :, PANEL:] = pair[:n, :]

        @pl.when(me == 3)
        def _():
            wide[:n, PANEL:] = pair_got[n:, :]
            wide[n:, PANEL:] = pair[...]

    @pl.when(z != 0)
    def _():
        wide[...] = jnp.zeros(wide.shape, BF16)


def stage3_kernel(info, ins, outs):
    g0, r1, r2, r3, child = outs
    child[...] = ins[4][...]
    for s in range(4):
        source = lax.rem(info[3] + 4 - s, 4)
        for b, out in enumerate(outs[:4]):

            @pl.when(source == b)
            def _():
                if b == 0:
                    g0[:DIAG, :] = ins[s][:DIAG, :]
                    r3[CHILD:, :] = ins[s][DIAG : DIAG + PIECE, :]
                elif b == 3:
                    r3[:CHILD, :] = ins[s][:CHILD, :]
                else:
                    out[...] = ins[s][: out.shape[0], :]
                if b < 3:
                    g0[DIAG + b * PART : DIAG + (b + 1) * PART, :] = ins[s][CHILD : CHILD + PART, :]


def copy_kernel(info, ins, outs):
    for a, b in zip(ins, outs):
        b[...] = a[...]


def join_kernel(info, ins, outs):
    joined = outs[0]
    n = ins[0].shape[0]
    for s in range(4):
        x = lax.rem(info[0] + 4 - s, 4)
        joined[pl.ds(pl.multiple_of(x * n, 16), n), :] = ins[s][...]
    copy_kernel(info, ins[4:], outs[1:])


def place_kernel(kernel, js, begun, info, ins, outs):
    n = len(js)
    out = outs[-1]
    if begun:
        out[...] = ins[-n - 1][...]
    else:
        out[...] = jnp.zeros(out.shape, BF16)
    kernel(info, ins[: -n - (1 if begun else 0)], outs[:-1])
    for j, ref in zip(js, ins[-n:]):
        slot = info[8 + j] - 3 * info[1]

        @pl.when((slot >= 0) & (slot < 3))
        def _():
            out[:, pl.ds(pl.multiple_of(slot * BLK, BLK), BLK)] = ref[...]


def tail_kernel(info, maps, front, a12, wide, *refs):
    r = list(refs)
    thick, r = r[:4], r[4:]
    packs, r = r[:PANELS], r[PANELS:]
    out, r = r[1], r[2:]
    inv, ups, t, a12v, x, xb, wv, fv, tv, yb = r[:10]
    sem_p, sem_a, sem_w, sem_f, sem_t, sem_o = r[10:]
    me = info[0]
    col = info[1]
    first = info[2]

    def blk(i):
        return slice(i * BLK, (i + 1) * BLK)

    def pan(i):
        return slice(i * PANEL, (i + 1) * PANEL)

    def tile(q):
        return pl.ds(pl.multiple_of(q * PANEL, PANEL), PANEL)

    def up_rows(j):
        return slice(j * (j - 1) // 2 * PANEL, j * (j + 1) // 2 * PANEL)

    copy = pltpu.make_async_copy
    pack_copies = []
    for j in range(PANELS):
        pack_copies.append(copy(packs[j].at[:PANEL, :], inv.at[j], sem_p.at[2 * j]))
        to = ups.at[up_rows(j), :] if j else t
        pack_copies.append(copy(packs[j].at[2 * PANEL :, :], to, sem_p.at[2 * j + 1]))

    def wide_copy(q):
        return copy(wide.at[pl.ds(4 * q, 4)], wv.at[pl.ds(4 * q, 4)], sem_w.at[q])

    def front_copy(q):
        return copy(front.at[tile(q), :], fv.at[tile(q), :], sem_f.at[q])

    def out_copy(q):
        return copy(fv.at[tile(q), :], out.at[tile(q), :], sem_o.at[q])

    def slot_of(value):
        slot = value - 3 * col
        return slot, (slot >= 0) & (slot < 3)

    def add(ref, row_block, col_slot, value):
        rows = pl.ds(pl.multiple_of(row_block * BLK, BLK), BLK)
        cols = pl.ds(pl.multiple_of(col_slot * BLK, BLK), BLK)
        ref[rows, cols] = ref[rows, cols] + value

    right = col >= PANELS
    lower = me > 0

    @pl.when(right | lower)
    def _():
        for c in pack_copies:
            c.start()

    @pl.when(right & lower)
    def _():
        copy(a12, a12v, sem_a).start()

    @pl.when(right & (me == 0))
    def _():
        for q in range(4):
            front_copy(q).start()

    far = col >= min(SOURCES)

    def thick_copy(i):
        return copy(thick[i], tv.at[lax.rem(me + 4 - i, 4)], sem_t.at[i])

    @pl.when(far)
    def _():
        for i in range(4):
            thick_copy(i).start()

    @pl.when(right | lower)
    def _():
        for c in pack_copies:
            c.wait()

    @pl.when(far)
    def _():
        for i in range(4):
            thick_copy(i).wait()

    @pl.when(lower)
    def _():
        for q in range(4):
            wide_copy(q).start()

        @pl.when(right)
        def _():
            for q in range(4):
                front_copy(q).start()

    @pl.when(right)
    def _():
        @pl.when(me == 0)
        def _():
            for q in range(4):
                front_copy(q).wait()
            x[...] = fv[...]

        @pl.when(lower)
        def _():
            copy(a12, a12v, sem_a).wait()
            x[...] = a12v[...].astype(F32)

        for i in range(3):
            ma = maps[i]

            @pl.when(ma < 12)
            def _():
                for b in range(3):
                    slot, here = slot_of(maps[b])

                    @pl.when(here)
                    def _():
                        add(x, ma, slot, t[blk(i), blk(b)].astype(F32))

                @pl.when(far)
                def _():
                    rows = pl.ds(pl.multiple_of(ma * BLK, BLK), BLK)
                    x[rows, :] = x[rows, :] + tv[0, blk(i), :].astype(F32)

        for j in range(PANELS):
            z = x[pan(j), :]
            if j:
                z = z - dot(ups[up_rows(j), :], xb[: j * PANEL, :], 0, 0)

            @pl.when(me == 0)
            def _():
                fv[pan(j), :] = z
                out_copy(j).start()

            if j < PANELS - 1:
                xb[pan(j), :] = dot(inv[j], z.astype(BF16), 1, 0).astype(BF16)

        @pl.when(lower)
        def _():
            last = dot(inv[PANELS - 1], z.astype(BF16), 1, 0)
            xb[pan(PANELS - 1), :] = last.astype(BF16)
            for j in reversed(range(PANELS)):
                v = xb[pan(j), :]
                for i in range(j + 1, PANELS):
                    at = up_rows(i).start + j * PANEL
                    part = dot(ups[at : at + PANEL, :], xb[pan(i), :], 1, 0)
                    v = v.astype(F32) - part
                xb[pan(j), :] = dot(inv[j], v.astype(BF16), 0, 0).astype(BF16)

        @pl.when(me == 0)
        def _():
            for q in range(4):
                out_copy(q).wait()

    @pl.when(lower)
    def _():
        for q in range(4):
            wide_copy(q).wait()

        def rows_step(q, _):
            @pl.when(right)
            def _():
                front_copy(q).wait()

            for i in range(12):
                ma = maps[first + i] - 12 * me

                @pl.when((ma >= 3 * q) & (ma < 3 * q + 3))
                def _():
                    rows = pl.ds(pl.multiple_of((ma - 3 * q) * BLK, BLK), BLK)
                    for b in range(3):
                        mb = maps[b]
                        piece = wv[(i // 3) * 4 + b, blk(i % 3), PANEL : PANEL + BLK]

                        @pl.when(mb < 12)
                        def _():
                            panel = mb // 3
                            cols = pl.ds(pl.multiple_of((mb - panel * 3) * BLK, BLK), BLK)
                            at = 4 * q + panel
                            wv[at, rows, cols] = (wv[at, rows, cols].astype(F32) + piece.astype(F32)).astype(BF16)

                        slot, here = slot_of(mb)

                        @pl.when(right & here)
                        def _():
                            add(fv, ma, slot, piece.astype(F32))

                    @pl.when(far)
                    def _():
                        held = pl.ds(pl.multiple_of(lax.rem(first + i, 4) * BLK, BLK), BLK)
                        to = pl.ds(pl.multiple_of(ma * BLK, BLK), BLK)
                        fv[to, :] = fv[to, :] + tv[(first + i) // 4, held, :].astype(F32)

            @pl.when(right)
            def _():
                rows = [wv[4 * q + k, :, :PANEL] for k in range(PANELS)]
                fv[tile(q), :] = fv[tile(q), :] - dot(jnp.concatenate(rows, axis=1), xb[...], 1, 0)

            for k in range(PANELS):

                @pl.when(col >= k)
                def _():
                    @pl.when(col < PANELS)
                    def _():
                        z = wv[4 * q + k, :, :PANEL]
                        if k:
                            z = (z.astype(F32) - dot(yb[:, : k * PANEL], ups[up_rows(k), :], 1, 0)).astype(BF16)
                        full = dot(z, inv[k], 1, 1)
                        yb[:, pan(k)] = full.astype(BF16)
                        fv[tile(q), :] = full

            out_copy(q).start()
            return 0

        lax.fori_loop(0, 4, rows_step, 0)
        for q in range(4):
            out_copy(q).wait()


def tail_call(info, maps, front, a12, wide, thick, packs, result):
    vm = pl.BlockSpec(memory_space=pltpu.VMEM)
    sm = pl.BlockSpec(memory_space=pltpu.SMEM)
    anywhere = pl.BlockSpec(memory_space=pl.ANY)
    sem = pltpu.SemaphoreType.DMA
    pinned = pl.BlockSpec(memory_space=pltpu.HBM)
    args = [front, a12, wide, *thick, *packs]
    return pl.pallas_call(
        tail_kernel,
        out_shape=jax.ShapeDtypeStruct((LEAD, PANEL), F32),
        in_specs=[sm, sm] + [pinned] * (len(args) - PANELS) + [anywhere] * PANELS + [pinned],
        out_specs=pinned,
        scratch_shapes=[
            pltpu.VMEM((PANELS, PANEL, PANEL), BF16),
            pltpu.VMEM((6 * PANEL, PANEL), BF16),
            pltpu.VMEM((PANEL, PANEL), BF16),
            pltpu.VMEM((LEAD, PANEL), BF16),
            pltpu.VMEM((LEAD, PANEL), F32),
            pltpu.VMEM((LEAD, PANEL), BF16),
            pltpu.VMEM((N_COL, PANEL, PANEL + BLK), BF16),
            pltpu.VMEM((LEAD, PANEL), F32),
            pltpu.VMEM((4, 4 * BLK, PANEL), BF16),
            pltpu.VMEM((PANEL, LEAD), BF16),
            sem((2 * PANELS,)),
            sem,
            sem((4,)),
            sem((4,)),
            sem((4,)),
            sem((4,)),
        ],
        input_output_aliases={2 + len(args): 0},
        compiler_params=pltpu.CompilerParams(vmem_limit_bytes=60 * 2**20),
        cost_estimate=pl.CostEstimate(flops=7 * 10**9, bytes_accessed=2 * 10**7, transcendentals=0),
        name="tail",
    )(info, maps, *args, result)


def per_device(front_init, contribution, maps):
    front = front_init[0]
    index_map = maps[0]
    me = lax.axis_index("row")
    col = lax.axis_index(COL)
    y = lax.axis_index("y")
    grid = ("row", "z", "y")

    def flat(r, c):
        return r * N_COL + c

    def x_from0(value, s, cols):
        return lax.ppermute(value, grid, [(flat(0, c), flat(s, c)) for c in cols])

    def z_from0(value, s):
        return lax.ppermute(value, COL, [(b, 4 * s + b) for b in range(4)])

    def x_shift(value, s):
        return lax.ppermute(value, "row", [(i, (i + s) % 4) for i in range(4)])

    def y_shift(value, s):
        return lax.ppermute(value, COL, [(4 * z + b, 4 * z + (b + s) % 4) for z in range(4) for b in range(4)])

    def x_swap(value, m):
        return lax.ppermute(value, "row", [(i, i ^ m) for i in range(4)])

    def x_pairs(value, pairs, cols):
        return lax.ppermute(value, grid, [(flat(p, c), flat(q, c)) for p, q in pairs for c in cols])

    def shifts(shift, value):
        return [shift(value, s) for s in range(1, 4)]

    z = lax.axis_index("z")
    first = jnp.where(me == 3, 4, 0)
    ids = jnp.full((N_COL, THICK), -1, jnp.int32)
    for c in SOURCES:
        for j, b in enumerate(SOURCES[c]):
            ids = ids.at[c, j].set(b)
    held = jnp.take(ids, col, axis=0)
    targets = jnp.where(held >= 0, jnp.take(index_map, jnp.maximum(held, 0)), -1000)
    info = jnp.concatenate(
        [jnp.stack([me, col, first, y, z, 0, 0, 0]).astype(jnp.int32), targets.astype(jnp.int32), jnp.zeros((3,), jnp.int32)]
    )

    def contribution_column(value, j):
        pairs = [(SOURCES[c][j], c) for c in SOURCES if j < len(SOURCES[c])]
        return lax.ppermute(value, COL, pairs)

    def staged(kernel, outs, args, marks=(), name=None):
        return vmem_call(kernel, outs, info, args, marks, name)

    received = lax.ppermute(contribution[0], "cube", [(0, 1), (1, 0)])
    piece, full = (REST, PANEL), (LEAD, PANEL)
    pieces = staged(pack_kernel, [piece] * 4, [front, received], name="pack")
    got = [x_from0(pieces[s], s, range(4)) for s in range(1, 4)]
    child_one = x_swap(received, 1)
    own, pair, high, lead = staged(
        stage1_kernel,
        [piece, (8 * BLK, BLK), full, full],
        [pieces[0], *got, received, child_one, front],
        name="stage1",
    )
    got = [z_from0(own, s) for s in range(1, 4)]
    pair_got = x_swap(pair, 3)
    a12 = lax.psum(lead, "row")
    thick = contribution_column(received, 0)
    own, wide_in, received, spread = staged(
        functools.partial(place_kernel, stage2_kernel, (0,), False),
        [piece, (LEAD, PANEL + BLK), received.shape, (4 * BLK, PANEL)],
        [own, *got, pair, pair_got, high, received, thick],
        name="stage2",
    )
    got = shifts(y_shift, own)
    wide_part = lax.psum_scatter(wide_in, "z", tiled=True)
    thick = [contribution_column(received, j) for j in (1, 2)]
    rows = [DIAG + 3 * PART] + [DIAG + b * PIECE for b in range(1, 4)]
    g0, r1, r2, r3, received, spread = staged(
        functools.partial(place_kernel, stage3_kernel, (1, 2), True),
        [(n, PANEL) for n in rows] + [received.shape, spread.shape],
        [own, *got, received, spread, *thick],
        name="stage3",
    )
    g = [g0] + shifts(x_shift, g0)
    thick = [contribution_column(received, j) for j in (3, 4)]

    def joined(value):
        return (4 * value.shape[0], PANEL)

    g0, r1, wide_part, spread = staged(
        functools.partial(place_kernel, join_kernel, (3, 4), True),
        [joined(g[0]), r1.shape, wide_part.shape, spread.shape],
        [*g, r1, wide_part, spread, *thick],
        name="stage4",
    )
    packs = []
    g = [r1] + shifts(x_shift, r1)
    wide = lax.all_gather(wide_part, COL)
    pack, result = panel_call(0, info, index_map, g0, [], [r1], None)
    packs.append(pack)
    g1, r2 = staged(join_kernel, [joined(g[0]), r2.shape], [*g, r2], [pack], name="stage5")
    g = [r2] + shifts(x_shift, r2)
    pack, result = panel_call(1, info, index_map, g1, packs, [r2], result)
    packs.append(pack)
    (r3,) = staged(copy_kernel, [r3.shape], [r3], [pack], name="stage6")
    after = [r3] + shifts(x_shift, r3)
    (g2,) = staged(join_kernel, [joined(g[0])], g, [r3], name="join2")
    g = after
    pack, result = panel_call(2, info, index_map, g2, packs, [r3], result)
    packs.append(pack)
    (spread,) = staged(copy_kernel, [spread.shape], [spread], [pack], name="stage7")
    far = range(min(SOURCES), N_COL)
    spread = [spread] + [x_pairs(spread, [(i, (i + s) % 4) for i in range(4)], far) for s in range(1, 4)]
    (g3,) = staged(join_kernel, [joined(g[0])], g, [spread[0]], name="join3")
    pack, result = panel_call(3, info, index_map, g3, packs, [spread[0]], result)
    packs.append(pack)
    out = tail_call(info, index_map, front, a12, wide, spread, packs, result)
    return out[None]


def solution(mesh):
    split_mesh = Mesh(mesh.devices.reshape(2, N_ROW, 4, 4), ("cube", "row", "z", "y"))
    return jax.shard_map(
        per_device,
        mesh=split_mesh,
        in_specs=(P("cube", "row", COL), P("cube", "row", COL), P("cube", None)),
        out_specs=P("cube", "row", COL),
        check_vma=False,
    )
```
